32 devices in a mesh: img: 8 (over y, x, core), slab: 4 (over z).
Axes of the slice: x: 2, y: 2, z: 4, core: 2. Of those that a mesh axis runs over, the one named last changes fastest.
Arguments:
- images: bfloat16 [512, 32768], P('img'), may hold values from -6 to 6
- references: bfloat16 [2, 128, 32768], P(None, 'slab'), may hold values from -6 to 6
- orientations: int32 [512, 2, 64], P('img'), may hold values from 0 to 127
- ctf_table: float32 [512, 64], P('img'), may hold values from -1 to 1
- inv_noise: float32 [512], P('img'), may hold values from 0.002 to 0.02
- class_weight: float32 [2], replicated, may hold values from 0.2 to 5
Outputs:
- updated_volume: float32 [2, 128, 32768], P(None, 'slab', 'img')
The draws below stay inside these ranges and needn't reach their ends.
All inputs are finite; a program needn't handle non-finite values.
Results may differ from the reference program's by a relative error of at most 0.0065.
Values sent between devices are 32-bit elements; how exact they have to be, the bound alone decides.
No kernel may reach another device: no remote copies, remote signals or barrier semaphores. Data moves between devices by JAX's collectives and lax.ppermute only.
A program may use at most 192 MiB of HBM per device.

```python
import math
import jax
import jax.numpy as jnp

BOX = 128
KW = 2
LIST = 64
SHELLS = 64
IMGS = 512


def with_ends(entries, own_key, low, high):
    longest = entries.shape.index(max(entries.shape))
    spots = []
    for shift in (0, 1):
        where = [jax.random.randint(jax.random.fold_in(own_key, axis), (), 0, length) for axis, length in enumerate(entries.shape)]
        where[longest] = (where[longest] + shift) % entries.shape[longest]
        spots.append(tuple(where))
    return entries.at[spots[0]].set(low).at[spots[1]].set(high)


def block_scale(rng, dims, split, low, largest):
    def one(axis_at, blocks):
        draws = jax.random.uniform(jax.random.fold_in(jax.random.fold_in(rng, 6), axis_at), (blocks,), jnp.float32, low / len(split), largest / len(split))
        return jnp.repeat(jnp.exp(draws), dims[axis_at] // blocks).reshape((-1,) + (1,) * (len(dims) - axis_at - 1))

    factor_of = one(*split[0])
    for cut in split[1:]:
        factor_of = factor_of * one(*cut)
    return factor_of


def centred(own_key, dims, width, most, cuts=(), held_as=jnp.bfloat16):
    level = block_scale(own_key, dims, cuts, -0.22, 0.18) if cuts else 1.0
    values = jax.random.normal(own_key, dims, jnp.float32) * width * level
    return jnp.minimum(jnp.maximum(values, -most), most).astype(held_as)


def setup_inputs(seed: int = 0) -> dict:
    key_list = jax.random.split(jax.random.key(seed), 7)
    images = centred(key_list[0], (IMGS, 2 * BOX * BOX), 1.0, 6.0, ((0, 8),))
    references = centred(key_list[1], (KW, BOX, 2 * BOX * BOX), 1.0, 6.0, ((1, 4),))
    orientations = with_ends(jax.random.randint(key_list[2], (IMGS, KW, LIST), 0, BOX), jax.random.fold_in(key_list[2], 1), 0, BOX - 1).astype(jnp.int32)
    ctf_table = jnp.clip(jax.random.uniform(key_list[3], (IMGS, SHELLS), jnp.float32, -1.0, 1.0) * block_scale(key_list[3], (IMGS, SHELLS), ((0, 8),), -0.4, 0.0), -1.0, 1.0)
    inv_noise = jnp.clip(jnp.exp(math.log(0.02) - 2.30258502 * jax.random.uniform(key_list[4], (IMGS,), jnp.float32) ** block_scale(key_list[4], (IMGS,), ((0, 8),), -0.2, 0.2)), 0.002, 0.02)
    class_weight = jnp.clip(jnp.exp(jax.random.uniform(key_list[5], (KW,), jnp.float32, math.log(0.2), math.log(5.0))), 0.2, 5.0)
    return dict(images=images, references=references, orientations=orientations, ctf_table=ctf_table, inv_noise=inv_noise, class_weight=class_weight)


def shell_index():
    position = jnp.arange(BOX * BOX, dtype=jnp.int32)
    column = position % BOX - BOX // 2
    row_place = position // BOX - BOX // 2
    radius_sq = column * column + row_place * row_place
    levels = jnp.arange(1, SHELLS, dtype=jnp.int32)
    inside = (2 * levels[None, :] * levels[None, :] <= radius_sq[:, None]).astype(jnp.int32)
    return jnp.sum(inside, axis=1).astype(jnp.int32)


def reference(images, references, orientations, ctf_table, inv_noise, class_weight):
    shell = shell_index()
    ctf_pixel = ctf_table[:, shell]
    weighted = (images.astype(jnp.float32) * jnp.repeat(ctf_pixel, 2, axis=1)).astype(jnp.bfloat16)
    ctf_square = (ctf_pixel * ctf_pixel).astype(jnp.bfloat16)
    planes = references.reshape(KW * BOX, 2 * BOX * BOX)
    spread = references.astype(jnp.float32).reshape(KW * BOX, BOX * BOX, 2)
    power = jnp.sum(spread * spread, axis=2).astype(jnp.bfloat16)
    intersection = jnp.dot(weighted, planes.T, preferred_element_type=jnp.float32)
    energy = jnp.dot(ctf_square, power.T, preferred_element_type=jnp.float32)
    total_images = images.shape[0]
    table = (2.0 * intersection - energy).reshape(total_images, KW, BOX)
    picked = jnp.take_along_axis(table, orientations, axis=2)
    scores = jnp.log(class_weight)[None, :, None] + inv_noise[:, None, None] * picked
    peak = jnp.max(scores, axis=(1, 2), keepdims=True)
    expo = jnp.exp(scores - peak)
    resp = expo / jnp.sum(expo, axis=(1, 2), keepdims=True)
    image_ids = jnp.arange(total_images, dtype=jnp.int32)[:, None, None]
    class_ids = jnp.arange(KW, dtype=jnp.int32)[None, :, None]
    per_plane = jnp.zeros((total_images, KW, BOX), jnp.float32).at[image_ids, class_ids, orientations].add(resp)
    flat_plane = per_plane.astype(jnp.bfloat16).reshape(total_images, KW * BOX)
    numerator = jnp.dot(flat_plane.T, weighted, preferred_element_type=jnp.float32)
    weight_sum = jnp.dot(flat_plane.T, ctf_square, preferred_element_type=jnp.float32)
    updated = numerator / (jnp.repeat(weight_sum, 2, axis=1) + 1.0)
    return updated.reshape(KW, BOX, 2 * BOX * BOX)
```

```python
import functools
import math

import jax
import jax.numpy as jnp
import numpy as np
from jax import lax
from jax.experimental import pallas as pl
from jax.experimental.pallas import tpu as pltpu
from jax.sharding import PartitionSpec as P

F32 = jnp.float32
BF16 = jnp.bfloat16
LANES = 128
VMEM_LIMIT = 48 * 1024 * 1024


def entry_shells(width, shells):
    pixels = width // 2
    box = math.isqrt(pixels)
    place = np.arange(pixels)
    column = place % box - box // 2
    row = place // box - box // 2
    radius = column * column + row * row
    levels = np.arange(1, shells)
    shell = np.sum(2 * levels[None, :] ** 2 <= radius[:, None], axis=1)
    return np.repeat(shell, 2).astype(np.int32)[None, :]


def params(**more):
    return pltpu.CompilerParams(vmem_limit_bytes=VMEM_LIMIT, **more)


def lanes_wide(table):
    rows, shells = table.shape
    if shells == LANES:
        return table
    return jnp.concatenate([table, jnp.zeros((rows, LANES - shells), table.dtype)], axis=1)


def spread(table, index):
    return jnp.take_along_axis(table, jnp.broadcast_to(index, table.shape), axis=1)


def contract_last(left, right):
    return lax.dot_general(left, right, (((1,), (1,)), ((), ())), preferred_element_type=F32)


def estep_kernel(
    chips, me_ref, index_ref, image_ref, plane_ref, ctf_ref, noise_ref, prior_ref,
    give_ref, keep_ref, score_ref, table, weighted, squared, energy_of, total,
):
    step = pl.program_id(0)

    @pl.when(step == 0)
    def _():
        table[...] = lanes_wide(ctf_ref[...])
        total[...] = jnp.zeros_like(total)

    held = table[...]
    for start in range(0, image_ref.shape[1], LANES):
        cut = slice(start, start + LANES)
        ctf = spread(held, index_ref[:, cut])
        weighted[:, cut] = (image_ref[:, cut].astype(F32) * ctf).astype(BF16)
        squared[:, cut] = (ctf * ctf).astype(BF16)
        plane = plane_ref[:, cut].astype(F32)
        energy_of[:, cut] = (plane * plane).astype(BF16)
    fit = contract_last(weighted[...], plane_ref[...])
    energy = contract_last(squared[...], energy_of[...])
    total[...] += 2.0 * fit - energy

    @pl.when(step < chips)
    def _():
        give_ref[0] = weighted[...].astype(F32)

    @pl.when(step >= chips)
    def _():
        keep_ref[0] = weighted[...]

    @pl.when(step == pl.num_programs(0) - 1)
    def _():
        rows = total.shape[0]
        noise = jnp.broadcast_to(noise_ref[...], (rows, rows))
        diagonal = lax.broadcasted_iota(jnp.int32, (rows, rows), 0) == lax.broadcasted_iota(
            jnp.int32, (rows, rows), 1
        )
        column = jnp.sum(jnp.where(diagonal, noise, 0.0), axis=1, keepdims=True)
        classes = prior_ref.shape[0]
        lane = lax.broadcasted_iota(jnp.int32, total.shape, 1)
        each = total.shape[1] // classes
        weight = jnp.full(total.shape, prior_ref[0], F32)
        for one in range(1, classes):
            weight = jnp.where(lane >= one * each, prior_ref[one], weight)
        score_ref[...] = jnp.log(weight) + column * total[...]


def estep(me, index, images, planes, ctf_table, inv_noise, class_weight, share):
    rows, width = images.shape
    parts = width // share
    chips = parts // 2
    count = planes.shape[0]
    shells = ctf_table.shape[1]

    def block(step, me_ref):
        mine = me_ref[0]
        chip = (mine // 2) ^ (step % chips)
        core = jnp.where(step < chips, 1 - mine % 2, mine % 2)
        return 0, chip * 2 + core

    def whole(step, me_ref):
        return 0, 0

    grid_spec = pltpu.PrefetchScalarGridSpec(
        num_scalar_prefetch=1,
        grid=(parts,),
        in_specs=[
            pl.BlockSpec((1, share), block),
            pl.BlockSpec((rows, share), block),
            pl.BlockSpec((count, share), block),
            pl.BlockSpec((rows, shells), whole),
            pl.BlockSpec((1, rows), whole),
            pl.BlockSpec(memory_space=pltpu.SMEM),
        ],
        out_specs=[
            pl.BlockSpec((1, rows, share), lambda s, m: (jnp.minimum(s, chips - 1), 0, 0)),
            pl.BlockSpec((1, rows, share), lambda s, m: (jnp.maximum(s - chips, 0), 0, 0)),
            pl.BlockSpec((rows, count), whole),
        ],
        scratch_shapes=[
            pltpu.VMEM((rows, LANES), F32),
            pltpu.VMEM((rows, share), BF16),
            pltpu.VMEM((rows, share), BF16),
            pltpu.VMEM((count, share), BF16),
            pltpu.VMEM((rows, count), F32),
        ],
    )
    return pl.pallas_call(
        functools.partial(estep_kernel, chips),
        grid_spec=grid_spec,
        out_shape=[
            jax.ShapeDtypeStruct((chips, rows, share), F32),
            jax.ShapeDtypeStruct((chips, rows, share), BF16),
            jax.ShapeDtypeStruct((rows, count), F32),
        ],
        compiler_params=params(),
        name="estep",
    )(me, index, images, planes, ctf_table, inv_noise.reshape(1, rows), class_weight)


def count_kernel(slabs, slab_ref, list_ref, out_ref):
    rows, listed = list_ref.shape
    classes = out_ref.shape[0]
    each = listed // classes
    width = out_ref.shape[2]
    local = width // slabs
    lane = lax.broadcasted_iota(jnp.int32, (rows, width), 1)
    home = lax.rem(slab_ref[0] - lane // local + slabs, slabs)
    plane = home * local + lax.rem(lane, local)
    for one in range(classes):
        sums = jnp.zeros((rows, width), F32)
        for entry in range(each):
            place = one * each + entry
            sums += jnp.where(list_ref[:, place : place + 1] == plane, 1.0, 0.0)
        out_ref[one] = sums


def count_planes(slab, orientations, width, slabs):
    rows, classes, each = orientations.shape
    return pl.pallas_call(
        functools.partial(count_kernel, slabs),
        in_specs=[
            pl.BlockSpec(memory_space=pltpu.SMEM),
            pl.BlockSpec(memory_space=pltpu.VMEM),
        ],
        out_specs=pl.BlockSpec(memory_space=pltpu.VMEM),
        out_shape=jax.ShapeDtypeStruct((classes, rows, width), F32),
        compiler_params=params(),
        cost_estimate=pl.CostEstimate(flops=10**7, bytes_accessed=10**6, transcendentals=0),
        name="count",
    )(slab, orientations.reshape(rows, classes * each))


def weigh_kernel(*refs):
    count_ref, out_ref = refs[0], refs[-1]
    scores = [ref[...] for ref in refs[1:-1]]
    classes = count_ref.shape[0]
    local = scores[0].shape[1] // classes
    fits, counts = [], []
    for one in range(classes):
        cut = slice(one * local, (one + 1) * local)
        counts.append(count_ref[one])
        fit = jnp.concatenate([score[:, cut] for score in scores], axis=1)
        fits.append(jnp.where(counts[-1] > 0.0, fit, -jnp.inf))
    peak = functools.reduce(jnp.maximum, [jnp.max(fit, axis=1, keepdims=True) for fit in fits])
    raw = [count * jnp.exp(fit - peak) for count, fit in zip(counts, fits)]
    total = functools.reduce(jnp.add, [jnp.sum(part, axis=1, keepdims=True) for part in raw])
    own = jnp.concatenate([part[:, :local] for part in raw], axis=1) / total
    out_ref[...] = own.T


def weigh(counts, scores):
    rows, planes = scores[0].shape
    return pl.pallas_call(
        weigh_kernel,
        out_shape=jax.ShapeDtypeStruct((planes, rows), F32),
        compiler_params=params(),
        name="weigh",
    )(counts, *scores)


def sums_kernel(items, cells, own_w_ref, sib_w_ref, own_ctf_ref, sib_ctf_ref, keep_ref, got_ref, out_ref, *shell_ref):
    weights = jnp.concatenate([own_w_ref[...], sib_w_ref[...]], axis=1).astype(BF16)
    rows = keep_ref.shape[1]
    images = jnp.concatenate([keep_ref[0], got_ref[0].astype(BF16)], axis=0)
    out_ref[0] = jnp.dot(weights, images, preferred_element_type=F32)
    if shell_ref:

        @pl.when(pl.program_id(1) == 0)
        def _():
            ctf = jnp.concatenate([own_ctf_ref[...], sib_ctf_ref[...]], axis=0)
            square = lanes_wide((ctf * ctf).astype(BF16))
            shell_ref[0][0] = jnp.dot(weights, square, preferred_element_type=F32)


def partial_sums(bits, half, own_w, sib_w, own_ctf, sib_ctf, keep, got, tile):
    first, step, number = bits
    chips, rows, share = keep.shape
    planes = own_w.shape[0]
    cells = share // (2 * tile)

    def source(item, cell):
        return first + step * item, 0, 2 * cell + half

    def whole(item, cell):
        return 0, 0

    small = [pl.BlockSpec(array.shape, whole) for array in (own_w, sib_w, own_ctf, sib_ctf)]
    out_specs = [pl.BlockSpec((1, planes, tile), lambda item, cell: (item, 0, cell))]
    out_shape = [jax.ShapeDtypeStruct((number, planes, cells * tile), F32)]
    if half == 0:
        out_specs.append(pl.BlockSpec((1, planes, LANES), lambda item, cell: (item, 0, 0)))
        out_shape.append(jax.ShapeDtypeStruct((number, planes, LANES), F32))
    return pl.pallas_call(
        functools.partial(sums_kernel, number, cells),
        grid=(number, cells),
        in_specs=small
        + [pl.BlockSpec((1, rows, tile), source), pl.BlockSpec((1, rows, tile), source)],
        out_specs=out_specs,
        out_shape=out_shape,
        compiler_params=params(),
        name="sums",
    )(own_w, sib_w, own_ctf, sib_ctf, keep, got)


def finish_kernel(number, index_ref, *refs):
    out_ref = refs[-1]
    shells = functools.reduce(jnp.add, [ref[0] for ref in refs[:number]])
    left = functools.reduce(jnp.add, [ref[0] for ref in refs[number : 2 * number]])
    right = functools.reduce(jnp.add, [ref[0] for ref in refs[2 * number : 3 * number]])
    tile = left.shape[1]
    for side, block in ((0, left), (1, right)):
        for start in range(0, tile, LANES):
            cut = slice(side * tile + start, side * tile + start + LANES)
            weight = spread(shells, index_ref[:, cut])
            out_ref[:, cut] = block[:, start : start + LANES] / (weight + 1.0)


def finish(index, me, shells, left, right, share, tile):
    planes = left[0].shape[1]
    number = len(left)
    cells = share // (2 * tile)
    side = pl.BlockSpec((1, planes, tile), lambda cell, m: (0, 0, cell))
    grid_spec = pltpu.PrefetchScalarGridSpec(
        num_scalar_prefetch=1,
        grid=(cells,),
        in_specs=[pl.BlockSpec((1, 2 * tile), lambda cell, m: (0, m[0] * cells + cell))]
        + [pl.BlockSpec((1, planes, LANES), lambda cell, m: (0, 0, 0))] * number
        + [side] * (2 * number),
        out_specs=pl.BlockSpec((planes, 2 * tile), lambda cell, m: (0, cell)),
    )

    def body(me_ref, *refs):
        finish_kernel(number, *refs)

    return pl.pallas_call(
        body,
        grid_spec=grid_spec,
        out_shape=jax.ShapeDtypeStruct((planes, share), F32),
        compiler_params=params(),
        name="finish",
    )(me, index, *shells, *left, *right)


def swap(array, bit, size):
    return lax.ppermute(array, "img", [(one, one ^ bit) for one in range(size)])


def shards(images, references, orientations, ctf_table, inv_noise, class_weight):
    rows, width = images.shape
    classes, local_planes, _ = references.shape
    size = lax.axis_size("img")
    slabs = lax.axis_size("slab")
    chips = size // 2
    share = width // size
    tile = share // 4
    me = lax.axis_index("img").astype(jnp.int32).reshape(1)
    slab = lax.axis_index("slab").astype(jnp.int32).reshape(1)
    index = jnp.asarray(entry_shells(width, ctf_table.shape[1]))
    planes = references.reshape(classes * local_planes, width)

    give, keep, score = estep(me, index, images, planes, ctf_table, inv_noise, class_weight, share)
    sib_ctf = swap(ctf_table, 1, size)
    scores = [score] + [
        lax.ppermute(score, "slab", [(one, (one + hop) % slabs) for one in range(slabs)])
        for hop in range(1, slabs)
    ]
    got = swap(give, 1, size)
    counts = count_planes(slab, orientations, slabs * local_planes, slabs)
    own_w = weigh(counts, scores)
    sib_w = swap(own_w, 1, size)

    sums = functools.partial(
        partial_sums,
        own_w=own_w, sib_w=sib_w, own_ctf=ctf_table, sib_ctf=sib_ctf, keep=keep, got=got, tile=tile,
    )
    top = chips // 2
    send_left, send_shells = sums((1, 2, top), 0)
    left_in = swap(send_left, 2, size)
    (send_right,) = sums((top, 1, top), 1)
    right_in = swap(send_right, 2 * top, size)
    shells_in = swap(send_shells, 2, size)
    keep_left, keep_shells = sums((0, 2, top), 0)
    (keep_right,) = sums((0, 1, top), 1)

    lefts, rights, shells = [keep_left, left_in], [keep_right, right_in], [keep_shells, shells_in]
    bit = 2
    while bit < chips:
        number = rights[-1].shape[0] // 2
        left_out = sum(part[1::2] for part in lefts)
        shells_out = sum(part[1::2] for part in shells)
        right_out = sum(part[number:] for part in rights)
        if number > 1:
            lefts = [part[0::2] for part in lefts]
            shells = [part[0::2] for part in shells]
            rights = [part[:number] for part in rights]
        lefts.append(swap(left_out, 2 * bit, size))
        rights.append(swap(right_out, chips // bit, size))
        shells.append(swap(shells_out, 2 * bit, size))
        bit *= 2
    out = finish(index, me, shells, lefts, rights, share, tile)
    return out.reshape(classes, local_planes, share)


def solution(mesh):
    return jax.shard_map(
        shards,
        mesh=mesh,
        in_specs=(
            P("img", None),
            P(None, "slab", None),
            P("img", None, None),
            P("img", None),
            P("img"),
            P(),
        ),
        out_specs=P(None, "slab", "img"),
        check_vma=False,
    )
```

```python
import functools
import math

import jax
import jax.numpy as jnp
import numpy as np
from jax import lax
from jax.experimental import pallas as pl
from jax.experimental.pallas import tpu as pltpu
from jax.sharding import PartitionSpec as P

F32 = jnp.float32
BF16 = jnp.bfloat16
LANES = 128
VMEM_LIMIT = 60 * 1024 * 1024


def entry_shells(width, shells):
    pixels = width // 2
    box = math.isqrt(pixels)
    place = np.arange(pixels)
    column = place % box - box // 2
    row = place // box - box // 2
    radius = column * column + row * row
    levels = np.arange(1, shells)
    shell = np.sum(2 * levels[None, :] ** 2 <= radius[:, None], axis=1)
    return np.repeat(shell, 2).astype(np.int32)[None, :]


def params(**more):
    return pltpu.CompilerParams(vmem_limit_bytes=VMEM_LIMIT, **more)


def lanes_wide(table):
    rows, shells = table.shape
    if shells == LANES:
        return table
    return jnp.concatenate([table, jnp.zeros((rows, LANES - shells), table.dtype)], axis=1)


def spread(table, index):
    return jnp.take_along_axis(table, jnp.broadcast_to(index, table.shape), axis=1)


def contract_last(left, right):
    return lax.dot_general(left, right, (((1,), (1,)), ((), ())), preferred_element_type=F32)


def estep_kernel(
    blocks, me_ref, index_hbm, image_hbm, plane_hbm, ctf_hbm, give_hbm, keep_hbm, score_ref,
    index, image, plane, ctf_held, weighted, give, squared, energy_of, small_sem, in_sem, out_sem,
):
    rows, width = image.shape
    chips, _, share = give.shape
    box = math.isqrt(width // 2)
    line = 2 * box
    deep = box // (2 * blocks)
    span = deep * line

    small = [
        pltpu.make_async_copy(index_hbm, index, small_sem.at[0]),
        pltpu.make_async_copy(ctf_hbm, ctf_held, small_sem.at[1]),
    ]
    incoming = []
    for block in range(blocks):
        copies = []
        for side, start in enumerate((block * span, width - (block + 1) * span)):
            cut = pl.ds(start, span)
            copies += [
                pltpu.make_async_copy(
                    image_hbm.at[:, cut], image.at[:, cut], in_sem.at[block, side, 0]
                ),
                pltpu.make_async_copy(
                    plane_hbm.at[:, cut], plane.at[:, cut], in_sem.at[block, side, 1]
                ),
            ]
        incoming.append(copies)
    for copy in small + [copy for copies in incoming for copy in copies]:
        copy.start()
    for copy in small:
        copy.wait()
    table = lanes_wide(ctf_held[...])

    def weigh_image(cut, ctf):
        weighted[:, cut] = (image[:, cut].astype(F32) * ctf).astype(BF16)

    def square(cut):
        part = plane[:, cut].astype(F32)
        return part * part

    def expand(row, slot, place):
        mirror = box - row if 0 < row < box // 2 else None
        for start in range(0, line, LANES):
            cut = slice(row * line + start, row * line + start + LANES)
            ctf = spread(table, index[:, cut])
            weigh_image(cut, ctf)
            power = square(cut)
            if mirror is not None:
                other = slice(mirror * line + start, mirror * line + start + LANES)
                weigh_image(other, ctf)
                power += square(other)
            held = slice(place + start, place + start + LANES)
            squared[slot, :, held] = (ctf * ctf).astype(BF16)
            energy_of[slot, :, held] = power.astype(BF16)

    def fit(start, stop):
        return contract_last(weighted[:, start:stop], plane[:, start:stop])

    def energy(slot, size):
        return contract_last(squared[slot, :, :size], energy_of[slot, :, :size])

    def block_table(block):
        low, high = fit(block * span, (block + 1) * span), width - block * span
        stop = high + line if block else high
        low += fit(high - span + line, stop)
        return 2.0 * low - energy(block % 2, span)

    chip, core = me_ref[0] // 2, lax.rem(me_ref[0], 2)
    outgoing = []

    def hand_over(done):
        for pair in range(chips):
            first, last = 2 * pair * share // line, -(-2 * (pair + 1) * share // line)
            if pair in handed or not all(row in done for row in range(first, last)):
                continue
            handed.add(pair)
            place = pair ^ chip
            given = pl.ds(pl.multiple_of((2 * pair + 1 - core) * share, share), share)
            kept = pl.ds(pl.multiple_of((2 * pair + core) * share, share), share)
            give[place] = weighted[:, given].astype(F32)
            outgoing.extend([
                pltpu.make_async_copy(give.at[place], give_hbm.at[place], out_sem.at[pair, 0]),
                pltpu.make_async_copy(weighted.at[:, kept], keep_hbm.at[place], out_sem.at[pair, 1]),
            ])
            outgoing[-2].start()
            outgoing[-1].start()

    handed, done = set(), set()
    total = jnp.zeros(score_ref.shape, F32)
    for block in range(blocks):
        for copy in incoming[block]:
            copy.wait()
        for row in range(block * deep, (block + 1) * deep):
            expand(row, block % 2, (row - block * deep) * line)
            done |= {row, box - row}
        if block == blocks - 1:
            expand(box // 2, 2, 0)
            done.add(box // 2)
        if block:
            total += block_table(block - 1)
        hand_over(done)
    total += block_table(blocks - 1)
    middle = width // 2
    total += 2.0 * fit(middle, middle + line) - energy(2, line)
    score_ref[...] = total
    for copy in outgoing:
        copy.wait()


def estep(me, index, images, planes, ctf_table, share):
    rows, width = images.shape
    chips = width // share // 2
    count = planes.shape[0]
    blocks = 4
    span = width // (2 * blocks)
    held = pl.BlockSpec(memory_space=pl.ANY)
    return pl.pallas_call(
        functools.partial(estep_kernel, blocks),
        in_specs=[pl.BlockSpec(memory_space=pltpu.SMEM)] + [held] * 4,
        out_specs=[held, held, pl.BlockSpec(memory_space=pltpu.VMEM)],
        out_shape=[
            jax.ShapeDtypeStruct((chips, rows, share), F32),
            jax.ShapeDtypeStruct((chips, rows, share), BF16),
            jax.ShapeDtypeStruct((rows, count), F32),
        ],
        scratch_shapes=[
            pltpu.VMEM(index.shape, jnp.int32),
            pltpu.VMEM((rows, width), BF16),
            pltpu.VMEM((count, width), BF16),
            pltpu.VMEM(ctf_table.shape, F32),
            pltpu.VMEM((rows, width), BF16),
            pltpu.VMEM((chips, rows, share), F32),
            pltpu.VMEM((3, rows, span), BF16),
            pltpu.VMEM((3, count, span), BF16),
            pltpu.SemaphoreType.DMA((2,)),
            pltpu.SemaphoreType.DMA((blocks, 2, 2)),
            pltpu.SemaphoreType.DMA((chips, 2)),
        ],
        compiler_params=params(),
        name="estep",
    )(me, index, images, planes, ctf_table)


def count_kernel(slabs, slab_ref, prior_ref, noise_ref, list_ref, base_ref, scale_ref):
    rows, listed = list_ref.shape
    classes, _, width = base_ref.shape
    each = listed // classes
    local = width // slabs
    lane = lax.broadcasted_iota(jnp.int32, (rows, width), 1)
    home = lax.rem(slab_ref[0] - lane // local + slabs, slabs)
    plane = home * local + lax.rem(lane, local)
    for one in range(classes):
        sums = jnp.zeros((rows, width), F32)
        for entry in range(each):
            place = one * each + entry
            sums += jnp.where(list_ref[:, place : place + 1] == plane, 1.0, 0.0)
        base_ref[one] = jnp.where(sums > 0.0, jnp.log(sums) + jnp.log(prior_ref[:, one : one + 1]), -jnp.inf)
    noise = jnp.broadcast_to(noise_ref[...], (rows, rows))
    diagonal = lax.broadcasted_iota(jnp.int32, (rows, rows), 0) == lax.broadcasted_iota(
        jnp.int32, (rows, rows), 1
    )
    column = jnp.sum(jnp.where(diagonal, noise, 0.0), axis=1, keepdims=True)
    scale_ref[...] = jnp.broadcast_to(column, (rows, width))


def count_planes(slab, class_weight, inv_noise, orientations, width, slabs):
    rows, classes, each = orientations.shape
    vmem = pl.BlockSpec(memory_space=pltpu.VMEM)
    return pl.pallas_call(
        functools.partial(count_kernel, slabs),
        in_specs=[pl.BlockSpec(memory_space=pltpu.SMEM), vmem, vmem, vmem],
        out_specs=[vmem, vmem],
        out_shape=[
            jax.ShapeDtypeStruct((classes, rows, width), F32),
            jax.ShapeDtypeStruct((rows, width), F32),
        ],
        compiler_params=params(),
        cost_estimate=pl.CostEstimate(flops=10**7, bytes_accessed=10**6, transcendentals=0),
        name="count",
    )(
        slab,
        class_weight.reshape(1, classes),
        inv_noise.reshape(1, rows),
        orientations.reshape(rows, classes * each),
    )


def weigh_kernel(base_ref, scale_ref, *refs):
    out_ref = refs[-1]
    tables = [ref[...] for ref in refs[:-1]]
    classes = base_ref.shape[0]
    local = tables[0].shape[1] // classes
    scores = []
    for one in range(classes):
        cut = slice(one * local, (one + 1) * local)
        fit = jnp.concatenate([table[:, cut] for table in tables], axis=1)
        scores.append(base_ref[one] + scale_ref[...] * fit)
    peak = functools.reduce(jnp.maximum, [jnp.max(score, axis=1, keepdims=True) for score in scores])
    raw = [jnp.exp(score - peak) for score in scores]
    total = functools.reduce(jnp.add, [jnp.sum(part, axis=1, keepdims=True) for part in raw])
    own = jnp.concatenate([part[:, :local] for part in raw], axis=1) / total
    out_ref[...] = own.T


def weigh(base, scale, tables):
    rows, planes = tables[0].shape
    return pl.pallas_call(
        weigh_kernel,
        out_shape=jax.ShapeDtypeStruct((planes, rows), F32),
        compiler_params=params(),
        name="weigh",
    )(base, scale, *tables)


def sums_kernel(items, with_shells, own_w_ref, sib_w_ref, own_ctf_ref, sib_ctf_ref, keep_hbm, got_hbm, *refs):
    outs = refs[: len(items)]
    shell_ref = refs[len(items)] if with_shells else None
    keep, got, sums, in_sem, out_sem = refs[-5:]
    tile = keep_hbm.shape[2] // 4
    number, _, wide = keep.shape
    cells = wide // tile
    places = [(out, slot, k, side) for out, (side, ks) in enumerate(items) for slot, k in enumerate(ks)]
    incoming, outgoing = [], []
    for place, (out, slot, k, side) in enumerate(places):
        copies = []
        for cell in range(cells):
            source = slice((2 * cell + side) * tile, (2 * cell + side + 1) * tile)
            target = slice(cell * tile, (cell + 1) * tile)
            copies += [
                pltpu.make_async_copy(
                    keep_hbm.at[k, :, source], keep.at[place, :, target], in_sem.at[place, cell, 0]
                ),
                pltpu.make_async_copy(
                    got_hbm.at[k, :, source], got.at[place, :, target], in_sem.at[place, cell, 1]
                ),
            ]
        incoming.append(copies)
        outgoing.append(pltpu.make_async_copy(sums.at[place], outs[out].at[slot], out_sem.at[place]))
    for copy in [copy for copies in incoming for copy in copies]:
        copy.start()
    weights = jnp.concatenate([own_w_ref[...], sib_w_ref[...]], axis=1).astype(BF16)
    if with_shells:
        ctf = jnp.concatenate([own_ctf_ref[...], sib_ctf_ref[...]], axis=0)
        square = lanes_wide((ctf * ctf).astype(BF16))
        shell_ref[...] = jnp.dot(weights, square, preferred_element_type=F32)
    for place in range(number):
        for copy in incoming[place]:
            copy.wait()
        images = jnp.concatenate([keep[place], got[place].astype(BF16)], axis=0)
        sums[place] = jnp.dot(weights, images, preferred_element_type=F32)
        outgoing[place].start()
    for copy in outgoing:
        copy.wait()


def partial_sums(items, with_shells, own_w, sib_w, own_ctf, sib_ctf, keep, got):
    chips, rows, share = keep.shape
    planes = own_w.shape[0]
    wide = share // 2
    number = sum(len(ks) for _, ks in items)
    held = pl.BlockSpec(memory_space=pl.ANY)
    vmem = pl.BlockSpec(memory_space=pltpu.VMEM)
    out_specs = [held] * len(items)
    out_shape = [jax.ShapeDtypeStruct((len(ks), planes, wide), F32) for _, ks in items]
    if with_shells:
        out_specs.append(vmem)
        out_shape.append(jax.ShapeDtypeStruct((planes, LANES), F32))
    return pl.pallas_call(
        functools.partial(sums_kernel, items, with_shells),
        in_specs=[vmem] * 4 + [held] * 2,
        out_specs=out_specs,
        out_shape=out_shape,
        scratch_shapes=[
            pltpu.VMEM((number, rows, wide), BF16),
            pltpu.VMEM((number, rows, wide), F32),
            pltpu.VMEM((number, planes, wide), F32),
            pltpu.SemaphoreType.DMA((number, 2, 2)),
            pltpu.SemaphoreType.DMA((number,)),
        ],
        compiler_params=params(),
        cost_estimate=pl.CostEstimate(
            flops=4 * planes * rows * wide * number,
            bytes_accessed=10 * planes * wide * number,
            transcendentals=0,
        ),
        name="sums",
    )(own_w, sib_w, own_ctf, sib_ctf, keep, got)


def finish_kernel(number, me_ref, index_ref, shell_ref, *refs):
    out_ref = refs[-1]
    left = functools.reduce(jnp.add, [ref[0] for ref in refs[:number]])
    right = functools.reduce(jnp.add, [ref[0] for ref in refs[number : 2 * number]])
    shells = shell_ref[...]
    tile = left.shape[1]
    for side, block in ((0, left), (1, right)):
        for start in range(0, tile, LANES):
            cut = slice(side * tile + start, side * tile + start + LANES)
            weight = spread(shells, index_ref[:, cut])
            out_ref[:, cut] = block[:, start : start + LANES] / (weight + 1.0)


def finish(me, index, shells, left, right, share):
    planes = left[0].shape[1]
    tile = share // 4
    number = len(left)
    cells = share // (2 * tile)
    side = pl.BlockSpec((1, planes, tile), lambda cell, m: (0, 0, cell))
    grid_spec = pltpu.PrefetchScalarGridSpec(
        num_scalar_prefetch=1,
        grid=(cells,),
        in_specs=[
            pl.BlockSpec((1, 2 * tile), lambda cell, m: (0, m[0] * cells + cell)),
            pl.BlockSpec((planes, LANES), lambda cell, m: (0, 0)),
        ]
        + [side] * (2 * number),
        out_specs=pl.BlockSpec((planes, 2 * tile), lambda cell, m: (0, cell)),
    )
    return pl.pallas_call(
        functools.partial(finish_kernel, number),
        grid_spec=grid_spec,
        out_shape=jax.ShapeDtypeStruct((planes, share), F32),
        compiler_params=params(),
        name="finish",
    )(me, index, shells, *left, *right)


def swap(array, bit, size):
    return lax.ppermute(array, "img", [(one, one ^ bit) for one in range(size)])


def shards(images, references, orientations, ctf_table, inv_noise, class_weight):
    rows, width = images.shape
    classes, local_planes, _ = references.shape
    size = lax.axis_size("img")
    slabs = lax.axis_size("slab")
    chips = size // 2
    share = width // size
    me = lax.axis_index("img").astype(jnp.int32).reshape(1)
    slab = lax.axis_index("slab").astype(jnp.int32).reshape(1)
    index = entry_shells(width, ctf_table.shape[1])
    top_index = jnp.asarray(index[:, : width // 2 + 2 * math.isqrt(width // 2)])
    index = jnp.asarray(index)
    planes = references.reshape(classes * local_planes, width)

    give, keep, table = estep(me, top_index, images, planes, ctf_table, share)
    sib_ctf = swap(ctf_table, 1, size)
    tables = [table] + [
        lax.ppermute(table, "slab", [(one, (one + hop) % slabs) for one in range(slabs)])
        for hop in range(1, slabs)
    ]
    got = swap(give, 1, size)
    base, scale = count_planes(
        slab, class_weight, inv_noise, orientations, slabs * local_planes, slabs
    )
    own_w = weigh(base, scale, tables)
    sib_w = swap(own_w, 1, size)

    sums = functools.partial(
        partial_sums,
        own_w=own_w, sib_w=sib_w, own_ctf=ctf_table, sib_ctf=sib_ctf, keep=keep, got=got,
    )
    top = chips // 2
    send_left, send_right = sums(
        ((0, tuple(range(1, chips, 2))), (1, tuple(range(top, chips)))), False
    )
    left_in = swap(send_left, 2, size)
    right_in = swap(send_right, 2 * top, size)
    keep_left, keep_right, shells = sums(
        ((0, tuple(range(0, chips, 2))), (1, tuple(range(top)))), True
    )
    lefts, rights = [keep_left, left_in], [keep_right, right_in]
    bit = 2
    while bit < chips:
        number = rights[-1].shape[0] // 2
        left_out = sum(part[1::2] for part in lefts)
        right_out = sum(part[number:] for part in rights)
        if number > 1:
            lefts = [part[0::2] for part in lefts]
            rights = [part[:number] for part in rights]
        lefts.append(swap(left_out, 2 * bit, size))
        rights.append(swap(right_out, chips // bit, size))
        bit *= 2
    bit = 2
    while bit < size:
        shells = shells + swap(shells, bit, size)
        bit *= 2
    out = finish(me, index, shells, lefts, rights, share)
    return out.reshape(classes, local_planes, share)


def solution(mesh):
    return jax.shard_map(
        shards,
        mesh=mesh,
        in_specs=(
            P("img", None),
            P(None, "slab", None),
            P("img", None, None),
            P("img", None),
            P("img"),
            P(),
        ),
        out_specs=P(None, "slab", "img"),
        check_vma=False,
    )
```

```python
import functools
import math

import jax
import jax.numpy as jnp
import numpy as np
from jax import lax
from jax.experimental import pallas as pl
from jax.experimental.pallas import tpu as pltpu
from jax.sharding import PartitionSpec as P

F32 = jnp.float32
BF16 = jnp.bfloat16
LANES = 128
MIB = 1024 * 1024


def entry_shells(width, shells):
    pixels = width // 2
    box = math.isqrt(pixels)
    place = np.arange(pixels)
    column = place % box - box // 2
    row = place // box - box // 2
    radius = column * column + row * row
    levels = np.arange(1, shells)
    shell = np.sum(2 * levels[None, :] ** 2 <= radius[:, None], axis=1)
    return np.repeat(shell, 2).astype(np.int32)[None, :]


def params(mib):
    return pltpu.CompilerParams(vmem_limit_bytes=mib * MIB)


def lanes_wide(table):
    rows, shells = table.shape
    if shells == LANES:
        return table
    return jnp.concatenate([table, jnp.zeros((rows, LANES - shells), table.dtype)], axis=1)


def spread(table, index):
    return jnp.take_along_axis(table, jnp.broadcast_to(index, table.shape), axis=1)


def contract_last(left, right):
    return lax.dot_general(left, right, (((1,), (1,)), ((), ())), preferred_element_type=F32)


def estep_kernel(
    blocks, me_ref, index_hbm, image_hbm, plane_hbm, ctf_hbm, give_hbm, keep_hbm, score_ref,
    index, image, plane, ctf_held, weighted, give, squared, energy_of, small_sem, in_sem, out_sem,
):
    rows, width = image.shape
    chips, _, share = give.shape
    box = math.isqrt(width // 2)
    line = 2 * box
    deep = box // (2 * blocks)
    span = deep * line

    small = [
        pltpu.make_async_copy(index_hbm, index, small_sem.at[0]),
        pltpu.make_async_copy(ctf_hbm, ctf_held, small_sem.at[1]),
    ]
    incoming = []
    for block in range(blocks):
        copies = []
        for side, start in enumerate((block * span, width - (block + 1) * span)):
            cut = pl.ds(start, span)
            copies += [
                pltpu.make_async_copy(
                    image_hbm.at[:, cut], image.at[:, cut], in_sem.at[block, side, 0]
                ),
                pltpu.make_async_copy(
                    plane_hbm.at[:, cut], plane.at[:, cut], in_sem.at[block, side, 1]
                ),
            ]
        incoming.append(copies)
    for copy in small + [copy for copies in incoming for copy in copies]:
        copy.start()
    for copy in small:
        copy.wait()
    table = lanes_wide(ctf_held[...])

    def weigh_image(cut, ctf):
        weighted[:, cut] = (image[:, cut].astype(F32) * ctf).astype(BF16)

    def square(cut):
        part = plane[:, cut].astype(F32)
        return part * part

    def expand(row, slot, place):
        mirror = box - row if 0 < row < box // 2 else None
        for start in range(0, line, LANES):
            cut = slice(row * line + start, row * line + start + LANES)
            ctf = spread(table, index[:, cut])
            weigh_image(cut, ctf)
            power = square(cut)
            if mirror is not None:
                other = slice(mirror * line + start, mirror * line + start + LANES)
                weigh_image(other, ctf)
                power += square(other)
            held = slice(place + start, place + start + LANES)
            squared[slot, :, held] = (ctf * ctf).astype(BF16)
            energy_of[slot, :, held] = power.astype(BF16)

    def fit(start, stop):
        return contract_last(weighted[:, start:stop], plane[:, start:stop])

    def energy(slot, size):
        return contract_last(squared[slot, :, :size], energy_of[slot, :, :size])

    def block_table(block):
        low, high = fit(block * span, (block + 1) * span), width - block * span
        stop = high + line if block else high
        low += fit(high - span + line, stop)
        return 2.0 * low - energy(block % 2, span)

    chip, core = me_ref[0] // 2, lax.rem(me_ref[0], 2)
    outgoing = []

    def hand_over(done):
        for pair in range(chips):
            first, last = 2 * pair * share // line, -(-2 * (pair + 1) * share // line)
            if pair in handed or not all(row in done for row in range(first, last)):
                continue
            handed.add(pair)
            place = pair ^ chip
            given = pl.ds(pl.multiple_of((2 * pair + 1 - core) * share, share), share)
            kept = pl.ds(pl.multiple_of((2 * pair + core) * share, share), share)
            give[place] = weighted[:, given].astype(F32)
            outgoing.extend([
                pltpu.make_async_copy(give.at[place], give_hbm.at[place], out_sem.at[pair, 0]),
                pltpu.make_async_copy(weighted.at[:, kept], keep_hbm.at[place], out_sem.at[pair, 1]),
            ])
            outgoing[-2].start()
            outgoing[-1].start()

    handed, done = set(), set()
    total = jnp.zeros(score_ref.shape, F32)
    for block in range(blocks):
        for copy in incoming[block]:
            copy.wait()
        for row in range(block * deep, (block + 1) * deep):
            expand(row, block % 2, (row - block * deep) * line)
            done |= {row, box - row}
        if block == blocks - 1:
            expand(box // 2, 2, 0)
            done.add(box // 2)
        if block:
            total += block_table(block - 1)
        hand_over(done)
    total += block_table(blocks - 1)
    middle = width // 2
    total += 2.0 * fit(middle, middle + line) - energy(2, line)
    score_ref[...] = total
    for copy in outgoing:
        copy.wait()


def estep(me, index, images, planes, ctf_table, share):
    rows, width = images.shape
    chips = width // share // 2
    count = planes.shape[0]
    blocks = 4
    span = width // (2 * blocks)
    held = pl.BlockSpec(memory_space=pl.ANY)
    far = pl.BlockSpec(memory_space=pltpu.HBM)
    return pl.pallas_call(
        functools.partial(estep_kernel, blocks),
        in_specs=[pl.BlockSpec(memory_space=pltpu.SMEM)] + [far] * 4,
        out_specs=[held, held, pl.BlockSpec(memory_space=pltpu.VMEM)],
        out_shape=[
            jax.ShapeDtypeStruct((chips, rows, share), F32),
            jax.ShapeDtypeStruct((chips, rows, share), BF16),
            jax.ShapeDtypeStruct((rows, count), F32),
        ],
        scratch_shapes=[
            pltpu.VMEM(index.shape, jnp.int32),
            pltpu.VMEM((rows, width), BF16),
            pltpu.VMEM((count, width), BF16),
            pltpu.VMEM(ctf_table.shape, F32),
            pltpu.VMEM((rows, width), BF16),
            pltpu.VMEM((chips, rows, share), F32),
            pltpu.VMEM((3, rows, span), BF16),
            pltpu.VMEM((3, count, span), BF16),
            pltpu.SemaphoreType.DMA((2,)),
            pltpu.SemaphoreType.DMA((blocks, 2, 2)),
            pltpu.SemaphoreType.DMA((chips, 2)),
        ],
        compiler_params=params(28),
        name="estep",
    )(me, *[pltpu.with_memory_space_constraint(part, pltpu.HBM) for part in (index, images, planes, ctf_table)])


def count_kernel(slabs, slab_ref, prior_ref, noise_ref, list_ref, base_ref, scale_ref):
    rows, listed = list_ref.shape
    classes, _, width = base_ref.shape
    each = listed // classes
    local = width // slabs
    lane = lax.broadcasted_iota(jnp.int32, (rows, width), 1)
    home = lax.rem(slab_ref[0] - lane // local + slabs, slabs)
    plane = home * local + lax.rem(lane, local)
    for one in range(classes):
        sums = jnp.zeros((rows, width), F32)
        for entry in range(each):
            place = one * each + entry
            sums += jnp.where(list_ref[:, place : place + 1] == plane, 1.0, 0.0)
        base_ref[one] = jnp.where(sums > 0.0, jnp.log(sums) + jnp.log(prior_ref[:, one : one + 1]), -jnp.inf)
    noise = jnp.broadcast_to(noise_ref[...], (rows, rows))
    diagonal = lax.broadcasted_iota(jnp.int32, (rows, rows), 0) == lax.broadcasted_iota(
        jnp.int32, (rows, rows), 1
    )
    column = jnp.sum(jnp.where(diagonal, noise, 0.0), axis=1, keepdims=True)
    scale_ref[...] = jnp.broadcast_to(column, (rows, width))


def count_planes(slab, class_weight, inv_noise, orientations, width, slabs):
    rows, classes, each = orientations.shape
    vmem = pl.BlockSpec(memory_space=pltpu.VMEM)
    return pl.pallas_call(
        functools.partial(count_kernel, slabs),
        in_specs=[pl.BlockSpec(memory_space=pltpu.SMEM), vmem, vmem, vmem],
        out_specs=[vmem, vmem],
        out_shape=[
            jax.ShapeDtypeStruct((classes, rows, width), F32),
            jax.ShapeDtypeStruct((rows, width), F32),
        ],
        compiler_params=params(4),
        cost_estimate=pl.CostEstimate(flops=10**7, bytes_accessed=10**6, transcendentals=0),
        name="count",
    )(
        slab,
        class_weight.reshape(1, classes),
        inv_noise.reshape(1, rows),
        orientations.reshape(rows, classes * each),
    )


def weigh_kernel(base_ref, scale_ref, *refs):
    out_ref = refs[-1]
    tables = [ref[...] for ref in refs[:-1]]
    classes = base_ref.shape[0]
    local = tables[0].shape[1] // classes
    scores = []
    for one in range(classes):
        cut = slice(one * local, (one + 1) * local)
        fit = jnp.concatenate([table[:, cut] for table in tables], axis=1)
        scores.append(base_ref[one] + scale_ref[...] * fit)
    peak = functools.reduce(jnp.maximum, [jnp.max(score, axis=1, keepdims=True) for score in scores])
    raw = [jnp.exp(score - peak) for score in scores]
    total = functools.reduce(jnp.add, [jnp.sum(part, axis=1, keepdims=True) for part in raw])
    own = jnp.concatenate([part[:, :local] for part in raw], axis=1) / total
    out_ref[...] = own.T


def weigh(base, scale, tables):
    rows, planes = tables[0].shape
    return pl.pallas_call(
        weigh_kernel,
        out_shape=jax.ShapeDtypeStruct((planes, rows), F32),
        compiler_params=params(4),
        name="weigh",
    )(base, scale, *tables)


def sums_kernel(items, own_w_ref, sib_w_ref, own_ctf_ref, sib_ctf_ref, keep_hbm, got_hbm, *refs):
    outs = refs[: len(items)]
    keep, got, sums, in_sem, out_sem = refs[-5:]
    tile = keep_hbm.shape[2] // 4
    number, _, wide = keep.shape
    cells = wide // tile
    places = [(out, slot, k, out) for out, ks in enumerate(items) for slot, k in enumerate(ks)]
    incoming, outgoing = [], []
    for place, (out, slot, k, side) in enumerate(places):
        copies = []
        for cell in range(cells):
            source = slice((2 * cell + side) * tile, (2 * cell + side + 1) * tile)
            target = slice(cell * tile, (cell + 1) * tile)
            copies += [
                pltpu.make_async_copy(
                    keep_hbm.at[k, :, source], keep.at[place, :, target], in_sem.at[place, cell, 0]
                ),
                pltpu.make_async_copy(
                    got_hbm.at[k, :, source], got.at[place, :, target], in_sem.at[place, cell, 1]
                ),
            ]
        incoming.append(copies)
        filled = sums.at[place] if side == 0 else sums.at[place, :, :wide]
        outgoing.append(pltpu.make_async_copy(filled, outs[out].at[slot], out_sem.at[place]))
    for copy in [copy for copies in incoming for copy in copies]:
        copy.start()
    weights = jnp.concatenate([own_w_ref[...], sib_w_ref[...]], axis=1).astype(BF16)
    ctf = jnp.concatenate([own_ctf_ref[...], sib_ctf_ref[...]], axis=0)
    shells = jnp.dot(weights, lanes_wide((ctf * ctf).astype(BF16)), preferred_element_type=F32)
    for place, (_, _, _, side) in enumerate(places):
        for copy in incoming[place]:
            copy.wait()
        images = jnp.concatenate([keep[place], got[place].astype(BF16)], axis=0)
        sums[place, :, :wide] = jnp.dot(weights, images, preferred_element_type=F32)
        if side == 0:
            sums[place, :, wide:] = shells
        outgoing[place].start()
    for copy in outgoing:
        copy.wait()


def partial_sums(items, own_w, sib_w, own_ctf, sib_ctf, keep, got):
    chips, rows, share = keep.shape
    planes = own_w.shape[0]
    wide = share // 2
    number = sum(len(ks) for ks in items)
    held = pl.BlockSpec(memory_space=pl.ANY)
    vmem = pl.BlockSpec(memory_space=pltpu.VMEM)
    return pl.pallas_call(
        functools.partial(sums_kernel, items),
        in_specs=[vmem] * 4 + [held] * 2,
        out_specs=[held] * 2,
        out_shape=[
            jax.ShapeDtypeStruct((len(ks), planes, wide + extra), F32)
            for ks, extra in zip(items, (LANES, 0))
        ],
        scratch_shapes=[
            pltpu.VMEM((number, rows, wide), BF16),
            pltpu.VMEM((number, rows, wide), F32),
            pltpu.VMEM((number, planes, wide + LANES), F32),
            pltpu.SemaphoreType.DMA((number, 2, 2)),
            pltpu.SemaphoreType.DMA((number,)),
        ],
        compiler_params=params(12),
        cost_estimate=pl.CostEstimate(
            flops=4 * planes * rows * wide * number,
            bytes_accessed=10 * planes * wide * number,
            transcendentals=0,
        ),
        name="sums",
    )(own_w, sib_w, own_ctf, sib_ctf, keep, got)


def finish_kernel(numbers, me_ref, index_ref, *refs):
    out_ref = refs[-1]
    left = functools.reduce(jnp.add, [ref[0] for ref in refs[: numbers[0]]])
    shells = functools.reduce(jnp.add, [ref[0] for ref in refs[numbers[0] : 2 * numbers[0]]])
    right = functools.reduce(jnp.add, [ref[0] for ref in refs[2 * numbers[0] : -1]])
    tile = left.shape[1]
    for side, block in ((0, left), (1, right)):
        for start in range(0, tile, LANES):
            cut = slice(side * tile + start, side * tile + start + LANES)
            weight = spread(shells, index_ref[:, cut])
            out_ref[:, cut] = block[:, start : start + LANES] / (weight + 1.0)


def finish(me, index, left, right, share):
    planes = left[0][0].shape[1]
    tile = share // 4
    cells = share // (2 * tile)

    def side(place):
        return pl.BlockSpec((1, planes, tile), lambda cell, m: (place, 0, cell))

    def tail(place):
        return pl.BlockSpec((1, planes, LANES), lambda cell, m: (place, 0, share // 2 // LANES))

    grid_spec = pltpu.PrefetchScalarGridSpec(
        num_scalar_prefetch=1,
        grid=(cells,),
        in_specs=[pl.BlockSpec((1, 2 * tile), lambda cell, m: (0, m[0] * cells + cell))]
        + [side(place) for _, place in left]
        + [tail(place) for _, place in left]
        + [side(place) for _, place in right],
        out_specs=pl.BlockSpec((planes, 2 * tile), lambda cell, m: (0, cell)),
    )
    return pl.pallas_call(
        functools.partial(finish_kernel, (len(left), len(right))),
        grid_spec=grid_spec,
        out_shape=jax.ShapeDtypeStruct((planes, share), F32),
        compiler_params=params(12),
        name="finish",
    )(me, index, *[part for part, _ in left + left + right])


def swap(array, bit, size):
    return lax.ppermute(array, "img", [(one, one ^ bit) for one in range(size)])


def shards(images, references, orientations, ctf_table, inv_noise, class_weight):
    rows, width = images.shape
    classes, local_planes, _ = references.shape
    size = lax.axis_size("img")
    slabs = lax.axis_size("slab")
    chips = size // 2
    share = width // size
    me = lax.axis_index("img").astype(jnp.int32).reshape(1)
    slab = lax.axis_index("slab").astype(jnp.int32).reshape(1)
    index = entry_shells(width, ctf_table.shape[1])
    top_index = jnp.asarray(index[:, : width // 2 + 2 * math.isqrt(width // 2)])
    index = jnp.asarray(index)
    planes = references.reshape(classes * local_planes, width)

    give, keep, table = estep(me, top_index, images, planes, ctf_table, share)
    sib_ctf = swap(ctf_table, 1, size)
    tables = [table] + [
        lax.ppermute(table, "slab", [(one, (one + hop) % slabs) for one in range(slabs)])
        for hop in range(1, slabs)
    ]
    got = swap(give, 1, size)
    base, scale = count_planes(
        slab, class_weight, inv_noise, orientations, slabs * local_planes, slabs
    )
    own_w = weigh(base, scale, tables)
    sib_w = swap(own_w, 1, size)

    sums = functools.partial(
        partial_sums,
        own_w=own_w, sib_w=sib_w, own_ctf=ctf_table, sib_ctf=sib_ctf, keep=keep, got=got,
    )
    low = [1 << place for place in range(chips.bit_length() - 1)]
    orders = (low, low[::-1])
    first = [[k for k in range(chips) if k & order[0]] for order in orders]
    onward = [[k for k in ks if k & order[1]] for ks, order in zip(first, orders)]
    direct = [[k for k in ks if not k & order[1]] for ks, order in zip(first, orders)]
    stay = [[k for k in range(chips) if not k & order[0]] for order in orders]
    parts = [{k: [] for k in ks} for ks in stay]

    def deliver(side, ks, array, bit):
        arrived = swap(array, 2 * bit, size)
        for place, k in enumerate(ks):
            parts[side][k ^ bit].append((arrived, place))

    def compute(groups):
        return sums(tuple(tuple(ks) for ks in groups))

    sent = compute(onward)
    for side in (0, 1):
        deliver(side, onward[side], sent[side], orders[side][0])
    sent = compute(direct)
    for side in (0, 1):
        deliver(side, direct[side], sent[side], orders[side][0])
    kept = compute(stay)
    for side in (0, 1):
        for place, k in enumerate(stay[side]):
            parts[side][k].append((kept[side], place))
    for turn in range(1, len(low)):
        for side in (0, 1):
            bit = orders[side][turn]
            ks = [k for k in parts[side] if k & bit]
            sent = jnp.stack([sum(part[place] for part, place in parts[side].pop(k)) for k in ks])
            deliver(side, ks, sent, bit)
    out = finish(me, index, parts[0][0], parts[1][0], share)
    return out.reshape(classes, local_planes, share)


def solution(mesh):
    return jax.shard_map(
        shards,
        mesh=mesh,
        in_specs=(
            P("img", None),
            P(None, "slab", None),
            P("img", None, None),
            P("img", None),
            P("img"),
            P(),
        ),
        out_specs=P(None, "slab", "img"),
        check_vma=False,
    )
```

```python
import functools
import math

import jax
import jax.numpy as jnp
import numpy as np
from jax import lax
from jax.experimental import pallas as pl
from jax.experimental.pallas import tpu as pltpu
from jax.sharding import PartitionSpec as P

F32 = jnp.float32
BF16 = jnp.bfloat16
LANES = 128
MIB = 1024 * 1024


def entry_shells(width, shells):
    pixels = width // 2
    box = math.isqrt(pixels)
    place = np.arange(pixels)
    column = place % box - box // 2
    row = place // box - box // 2
    radius = column * column + row * row
    levels = np.arange(1, shells)
    shell = np.sum(2 * levels[None, :] ** 2 <= radius[:, None], axis=1)
    return np.repeat(shell, 2).astype(np.int32)[None, :]


def params(mib):
    return pltpu.CompilerParams(vmem_limit_bytes=mib * MIB)


def lanes_wide(table):
    rows, shells = table.shape
    if shells == LANES:
        return table
    return jnp.concatenate([table, jnp.zeros((rows, LANES - shells), table.dtype)], axis=1)


def spread(table, index):
    return jnp.take_along_axis(table, jnp.broadcast_to(index, table.shape), axis=1)


def contract_last(left, right):
    return lax.dot_general(left, right, (((1,), (1,)), ((), ())), preferred_element_type=F32)


def estep_kernel(
    blocks, me_ref, index_hbm, image_hbm, plane_hbm, ctf_hbm, give, weighted, score_ref,
    index, image, plane, ctf_held, squared, energy_of, small_sem, in_sem,
):
    rows, width = image.shape
    chips, _, share = give.shape
    box = math.isqrt(width // 2)
    line = 2 * box
    deep = box // (2 * blocks)
    span = deep * line

    small = [
        pltpu.make_async_copy(index_hbm, index, small_sem.at[0]),
        pltpu.make_async_copy(ctf_hbm, ctf_held, small_sem.at[1]),
    ]
    incoming = []
    for block in range(blocks):
        copies = []
        for side, start in enumerate((block * span, width - (block + 1) * span)):
            cut = pl.ds(start, span)
            copies += [
                pltpu.make_async_copy(
                    image_hbm.at[:, cut], image.at[:, cut], in_sem.at[block, side, 0]
                ),
                pltpu.make_async_copy(
                    plane_hbm.at[:, cut], plane.at[:, cut], in_sem.at[block, side, 1]
                ),
            ]
        incoming.append(copies)
    for copy in small + [copy for copies in incoming for copy in copies]:
        copy.start()
    for copy in small:
        copy.wait()
    table = lanes_wide(ctf_held[...])

    def weigh_image(cut, ctf):
        weighted[:, cut] = (image[:, cut].astype(F32) * ctf).astype(BF16)

    def square(cut):
        part = plane[:, cut].astype(F32)
        return part * part

    def expand(row, slot, place):
        mirror = box - row if 0 < row < box // 2 else None
        for start in range(0, line, LANES):
            cut = slice(row * line + start, row * line + start + LANES)
            ctf = spread(table, index[:, cut])
            weigh_image(cut, ctf)
            power = square(cut)
            if mirror is not None:
                other = slice(mirror * line + start, mirror * line + start + LANES)
                weigh_image(other, ctf)
                power += square(other)
            held = slice(place + start, place + start + LANES)
            squared[slot, :, held] = (ctf * ctf).astype(BF16)
            energy_of[slot, :, held] = power.astype(BF16)

    def fit(start, stop):
        return contract_last(weighted[:, start:stop], plane[:, start:stop])

    def energy(slot, size):
        return contract_last(squared[slot, :, :size], energy_of[slot, :, :size])

    def block_table(block):
        low, high = fit(block * span, (block + 1) * span), width - block * span
        stop = high + line if block else high
        low += fit(high - span + line, stop)
        return 2.0 * low - energy(block % 2, span)

    chip, core = me_ref[0] // 2, lax.rem(me_ref[0], 2)

    def hand_over(done):
        for pair in range(chips):
            first, last = 2 * pair * share // line, -(-2 * (pair + 1) * share // line)
            if pair in handed or not all(row in done for row in range(first, last)):
                continue
            handed.add(pair)
            given = pl.ds(pl.multiple_of((2 * pair + 1 - core) * share, share), share)
            give[pair ^ chip] = weighted[:, given].astype(F32)

    handed, done = set(), set()
    total = jnp.zeros(score_ref.shape, F32)
    for block in range(blocks):
        for copy in incoming[block]:
            copy.wait()
        for row in range(block * deep, (block + 1) * deep):
            expand(row, block % 2, (row - block * deep) * line)
            done |= {row, box - row}
        if block == blocks - 1:
            expand(box // 2, 2, 0)
            done.add(box // 2)
        if block:
            total += block_table(block - 1)
        hand_over(done)
    total += block_table(blocks - 1)
    middle = width // 2
    total += 2.0 * fit(middle, middle + line) - energy(2, line)
    score_ref[...] = total


def estep(me, index, images, planes, ctf_table, share):
    rows, width = images.shape
    chips = width // share // 2
    count = planes.shape[0]
    blocks = 4
    span = width // (2 * blocks)
    vmem = pl.BlockSpec(memory_space=pltpu.VMEM)
    far = pl.BlockSpec(memory_space=pltpu.HBM)
    operands = (index, images, planes, ctf_table)
    return pl.pallas_call(
        functools.partial(estep_kernel, blocks),
        in_specs=[pl.BlockSpec(memory_space=pltpu.SMEM)] + [far] * 4,
        out_specs=[vmem] * 3,
        out_shape=[
            jax.ShapeDtypeStruct((chips, rows, share), F32),
            jax.ShapeDtypeStruct((rows, width), BF16),
            jax.ShapeDtypeStruct((rows, count), F32),
        ],
        scratch_shapes=[
            pltpu.VMEM(index.shape, jnp.int32),
            pltpu.VMEM((rows, width), BF16),
            pltpu.VMEM((count, width), BF16),
            pltpu.VMEM(ctf_table.shape, F32),
            pltpu.VMEM((3, rows, span), BF16),
            pltpu.VMEM((3, count, span), BF16),
            pltpu.SemaphoreType.DMA((2,)),
            pltpu.SemaphoreType.DMA((blocks, 2, 2)),
        ],
        compiler_params=params(28),
        name="estep",
    )(me, *[pltpu.with_memory_space_constraint(operand, pltpu.HBM) for operand in operands])


def count_kernel(slabs, slab_ref, prior_ref, noise_ref, list_ref, base_ref, scale_ref):
    rows, listed = list_ref.shape
    classes, _, width = base_ref.shape
    each = listed // classes
    local = width // slabs
    lane = lax.broadcasted_iota(jnp.int32, (rows, width), 1)
    home = slab_ref[0] ^ (lane // local)
    plane = home * local + lax.rem(lane, local)
    for one in range(classes):
        sums = jnp.zeros((rows, width), F32)
        for entry in range(each):
            place = one * each + entry
            sums += jnp.where(list_ref[:, place : place + 1] == plane, 1.0, 0.0)
        base_ref[one] = jnp.where(sums > 0.0, jnp.log(sums) + jnp.log(prior_ref[:, one : one + 1]), -jnp.inf)
    noise = jnp.broadcast_to(noise_ref[...], (rows, rows))
    diagonal = lax.broadcasted_iota(jnp.int32, (rows, rows), 0) == lax.broadcasted_iota(
        jnp.int32, (rows, rows), 1
    )
    column = jnp.sum(jnp.where(diagonal, noise, 0.0), axis=1, keepdims=True)
    scale_ref[...] = jnp.broadcast_to(column, (rows, width))


def count_planes(slab, class_weight, inv_noise, orientations, width, slabs):
    rows, classes, each = orientations.shape
    vmem = pl.BlockSpec(memory_space=pltpu.VMEM)
    return pl.pallas_call(
        functools.partial(count_kernel, slabs),
        in_specs=[pl.BlockSpec(memory_space=pltpu.SMEM), vmem, vmem, vmem],
        out_specs=[vmem, vmem],
        out_shape=[
            jax.ShapeDtypeStruct((classes, rows, width), F32),
            jax.ShapeDtypeStruct((rows, width), F32),
        ],
        compiler_params=params(4),
        cost_estimate=pl.CostEstimate(flops=10**7, bytes_accessed=10**6, transcendentals=0),
        name="count",
    )(
        slab,
        class_weight.reshape(1, classes),
        inv_noise.reshape(1, rows),
        orientations.reshape(rows, classes * each),
    )


def weigh_kernel(base_ref, scale_ref, *refs):
    out_ref = refs[-1]
    classes = base_ref.shape[0]
    planes = out_ref.shape[0]
    local = planes // classes
    scores = []
    for one in range(classes):
        parts = [
            ref[:, start + one * local : start + (one + 1) * local]
            for ref in refs[:-1]
            for start in range(0, ref.shape[1], planes)
        ]
        scores.append(base_ref[one] + scale_ref[...] * jnp.concatenate(parts, axis=1))
    peak = functools.reduce(jnp.maximum, [jnp.max(score, axis=1, keepdims=True) for score in scores])
    raw = [jnp.exp(score - peak) for score in scores]
    total = functools.reduce(jnp.add, [jnp.sum(part, axis=1, keepdims=True) for part in raw])
    own = jnp.concatenate([part[:, :local] for part in raw], axis=1) / total
    out_ref[...] = own.T


def weigh(base, scale, tables, planes):
    return pl.pallas_call(
        weigh_kernel,
        out_shape=jax.ShapeDtypeStruct((planes, base.shape[1]), F32),
        compiler_params=params(4),
        name="weigh",
    )(base, scale, *tables)


def sums_kernel(items, me_ref, own_w_ref, sib_w_ref, own_ctf_ref, sib_ctf_ref, weighted_ref, got_ref, *outs):
    share = got_ref.shape[2]
    tile = share // 4
    wide = share // 2
    chip, core = me_ref[0] // 2, lax.rem(me_ref[0], 2)
    weights = jnp.concatenate([own_w_ref[...], sib_w_ref[...]], axis=1).astype(BF16)
    ctf = jnp.concatenate([own_ctf_ref[...], sib_ctf_ref[...]], axis=0)
    shells = jnp.dot(weights, lanes_wide((ctf * ctf).astype(BF16)), preferred_element_type=F32)
    for side, ks in enumerate(items):
        for slot, k in enumerate(ks):
            start = pl.multiple_of(((k ^ chip) * 2 + core) * share, share)
            for cell in range(wide // tile):
                place = (2 * cell + side) * tile
                images = jnp.concatenate(
                    [
                        weighted_ref[:, pl.ds(pl.multiple_of(start + place, tile), tile)],
                        got_ref[k, :, place : place + tile].astype(BF16),
                    ],
                    axis=0,
                )
                outs[side][slot, :, cell * tile : (cell + 1) * tile] = jnp.dot(
                    weights, images, preferred_element_type=F32
                )
            if side == 0:
                outs[side][slot, :, wide:] = shells


def partial_sums(items, me, own_w, sib_w, own_ctf, sib_ctf, weighted, got):
    chips, rows, share = got.shape
    planes = own_w.shape[0]
    wide = share // 2
    number = sum(len(ks) for ks in items)
    vmem = pl.BlockSpec(memory_space=pltpu.VMEM)
    return pl.pallas_call(
        functools.partial(sums_kernel, items),
        in_specs=[pl.BlockSpec(memory_space=pltpu.SMEM)] + [vmem] * 6,
        out_specs=[vmem] * 2,
        out_shape=[
            jax.ShapeDtypeStruct((len(ks), planes, wide + extra), F32)
            for ks, extra in zip(items, (LANES, 0))
        ],
        compiler_params=params(16),
        cost_estimate=pl.CostEstimate(
            flops=4 * planes * rows * wide * number,
            bytes_accessed=10 * planes * wide * number,
            transcendentals=0,
        ),
        name="sums",
    )(me, own_w, sib_w, own_ctf, sib_ctf, weighted, got)


def finish_kernel(numbers, me_ref, index_hbm, *refs):
    total = sum(numbers)
    parts, (out_hbm, index, out, in_sem, out_sem) = refs[:total], refs[total:]
    planes, share = out.shape
    tile = share // 4
    wide = share // 2
    mine = pl.ds(pl.multiple_of(me_ref[0] * share, share), share)
    fetch = pltpu.make_async_copy(index_hbm.at[:, mine], index, in_sem)
    fetch.start()
    left, right = parts[: numbers[0]], parts[numbers[0] :]
    shells = functools.reduce(jnp.add, [ref[0, :, wide:] for ref in left])
    fetch.wait()
    stores = []
    for cell in range(2):
        for side, refs in ((0, left), (1, right)):
            for start in range(0, tile, LANES):
                place = (2 * cell + side) * tile + start
                cut = slice(cell * tile + start, cell * tile + start + LANES)
                block = functools.reduce(jnp.add, [ref[0, :, cut] for ref in refs])
                weight = spread(shells, index[:, place : place + LANES])
                out[:, place : place + LANES] = block / (weight + 1.0)
        cut = slice(cell * wide, (cell + 1) * wide)
        stores.append(pltpu.make_async_copy(out.at[:, cut], out_hbm.at[:, cut], out_sem.at[cell]))
        stores[-1].start()
    for store in stores:
        store.wait()


def finish(me, index, left, right, share):
    planes = left[0][0].shape[1]
    numbers = len(left), len(right)
    held = pl.BlockSpec(memory_space=pl.ANY)

    def first(part, place):
        return pl.BlockSpec((1,) + part.shape[1:], lambda step: (place, 0, 0))

    return pl.pallas_call(
        functools.partial(finish_kernel, numbers),
        grid=(1,),
        in_specs=[pl.BlockSpec(memory_space=pltpu.SMEM), held]
        + [first(part, place) if part.shape[0] > 1 else pl.BlockSpec(memory_space=pltpu.VMEM) for part, place in left + right],
        out_specs=held,
        out_shape=jax.ShapeDtypeStruct((planes, share), F32),
        scratch_shapes=[
            pltpu.VMEM((1, share), jnp.int32),
            pltpu.VMEM((planes, share), F32),
            pltpu.SemaphoreType.DMA(()),
            pltpu.SemaphoreType.DMA((2,)),
        ],
        compiler_params=params(12),
        name="finish",
    )(me, index, *[part for part, _ in left + right])


def swap(array, bit, size):
    return lax.ppermute(array, "img", [(one, one ^ bit) for one in range(size)])


def shards(images, references, orientations, ctf_table, inv_noise, class_weight):
    rows, width = images.shape
    classes, local_planes, _ = references.shape
    size = lax.axis_size("img")
    slabs = lax.axis_size("slab")
    chips = size // 2
    share = width // size
    me = lax.axis_index("img").astype(jnp.int32).reshape(1)
    slab = lax.axis_index("slab").astype(jnp.int32).reshape(1)
    index = entry_shells(width, ctf_table.shape[1])
    top_index = jnp.asarray(index[:, : width // 2 + 2 * math.isqrt(width // 2)])
    index = jnp.asarray(index)
    planes = references.reshape(classes * local_planes, width)

    give, weighted, table = estep(me, top_index, images, planes, ctf_table, share)
    sib_ctf = swap(ctf_table, 1, size)
    tables, bit = [table], 1
    while bit < slabs:
        held = tables[0] if len(tables) == 1 else jnp.concatenate(tables, axis=1)
        tables = [
            held, lax.ppermute(held, "slab", [(one, one ^ bit) for one in range(slabs)])
        ]
        bit *= 2
    got = swap(give, 1, size)
    base, scale = count_planes(
        slab, class_weight, inv_noise, orientations, slabs * local_planes, slabs
    )
    own_w = weigh(base, scale, tables, classes * local_planes)
    sib_w = swap(own_w, 1, size)

    sums = functools.partial(
        partial_sums,
        me=me, own_w=own_w, sib_w=sib_w, own_ctf=ctf_table, sib_ctf=sib_ctf, weighted=weighted, got=got,
    )
    low = [1 << place for place in range(chips.bit_length() - 1)]
    orders = (low, low[::-1])
    first = [[k for k in range(chips) if k & order[0]] for order in orders]
    onward = [[k for k in ks if k & order[1]] for ks, order in zip(first, orders)]
    direct = [[k for k in ks if not k & order[1]] for ks, order in zip(first, orders)]
    stay = [[k for k in range(chips) if not k & order[0]] for order in orders]
    parts = [{k: [] for k in ks} for ks in stay]

    def deliver(side, ks, array, bit):
        arrived = swap(array, 2 * bit, size)
        for place, k in enumerate(ks):
            parts[side][k ^ bit].append((arrived, place))

    def compute(groups):
        return sums(tuple(tuple(ks) for ks in groups))

    sent = compute(onward)
    for side in (0, 1):
        deliver(side, onward[side], sent[side], orders[side][0])
    sent = compute(direct)
    for side in (0, 1):
        deliver(side, direct[side], sent[side], orders[side][0])
    kept = compute(stay)
    for side in (0, 1):
        for place, k in enumerate(stay[side]):
            parts[side][k].append((kept[side], place))
    for turn in range(1, len(low)):
        for side in (0, 1):
            bit = orders[side][turn]
            ks = [k for k in parts[side] if k & bit]
            sent = jnp.stack([sum(part[place] for part, place in parts[side].pop(k)) for k in ks])
            deliver(side, ks, sent, bit)
    out = finish(me, index, parts[0][0], parts[1][0], share)
    return out.reshape(classes, local_planes, share)


def solution(mesh):
    return jax.shard_map(
        shards,
        mesh=mesh,
        in_specs=(
            P("img", None),
            P(None, "slab", None),
            P("img", None, None),
            P("img", None),
            P("img"),
            P(),
        ),
        out_specs=P(None, "slab", "img"),
        check_vma=False,
    )
```

```python
import functools
import math

import jax
import jax.numpy as jnp
import numpy as np
from jax import lax
from jax.experimental import pallas as pl
from jax.experimental.pallas import tpu as pltpu
from jax.sharding import PartitionSpec as P

F32 = jnp.float32
BF16 = jnp.bfloat16
LANES = 128
MIB = 1024 * 1024


def entry_shells(width, shells):
    pixels = width // 2
    box = math.isqrt(pixels)
    place = np.arange(pixels)
    column = place % box - box // 2
    row = place // box - box // 2
    radius = column * column + row * row
    levels = np.arange(1, shells)
    shell = np.sum(2 * levels[None, :] ** 2 <= radius[:, None], axis=1)
    return np.repeat(shell, 2).astype(np.int32)[None, :]


def params(mib):
    return pltpu.CompilerParams(vmem_limit_bytes=mib * MIB)


def lanes_wide(table):
    rows, shells = table.shape
    if shells == LANES:
        return table
    return jnp.concatenate([table, jnp.zeros((rows, LANES - shells), table.dtype)], axis=1)


def spread(table, index):
    return jnp.take_along_axis(table, jnp.broadcast_to(index, table.shape), axis=1)


def contract_last(left, right):
    return lax.dot_general(left, right, (((1,), (1,)), ((), ())), preferred_element_type=F32)


def estep_kernel(
    blocks, me_ref, index_hbm, image_hbm, plane_hbm, ctf_hbm, give_hbm, keep_hbm, score_ref,
    index, image, plane, ctf_held, weighted, give, squared, energy_of, small_sem, in_sem, out_sem,
):
    rows, width = image.shape
    chips, _, share = give.shape
    box = math.isqrt(width // 2)
    line = 2 * box
    deep = box // (2 * blocks)
    span = deep * line

    small = [
        pltpu.make_async_copy(index_hbm, index, small_sem.at[0]),
        pltpu.make_async_copy(ctf_hbm, ctf_held, small_sem.at[1]),
    ]
    incoming = []
    for block in range(blocks):
        copies = []
        for side, start in enumerate((block * span, width - (block + 1) * span)):
            cut = pl.ds(start, span)
            copies += [
                pltpu.make_async_copy(
                    image_hbm.at[:, cut], image.at[:, cut], in_sem.at[block, side, 0]
                ),
                pltpu.make_async_copy(
                    plane_hbm.at[:, cut], plane.at[:, cut], in_sem.at[block, side, 1]
                ),
            ]
        incoming.append(copies)
    for copy in small + [copy for copies in incoming for copy in copies]:
        copy.start()
    for copy in small:
        copy.wait()
    table = lanes_wide(ctf_held[...])

    def weigh_image(cut, ctf):
        weighted[:, cut] = (image[:, cut].astype(F32) * ctf).astype(BF16)

    def square(cut):
        part = plane[:, cut].astype(F32)
        return part * part

    def expand(row, slot, place):
        mirror = box - row if 0 < row < box // 2 else None
        for start in range(0, line, LANES):
            cut = slice(row * line + start, row * line + start + LANES)
            ctf = spread(table, index[:, cut])
            weigh_image(cut, ctf)
            power = square(cut)
            if mirror is not None:
                other = slice(mirror * line + start, mirror * line + start + LANES)
                weigh_image(other, ctf)
                power += square(other)
            held = slice(place + start, place + start + LANES)
            squared[slot, :, held] = (ctf * ctf).astype(BF16)
            energy_of[slot, :, held] = power.astype(BF16)

    def fit(start, stop):
        return contract_last(weighted[:, start:stop], plane[:, start:stop])

    def energy(slot, size):
        return contract_last(squared[slot, :, :size], energy_of[slot, :, :size])

    def block_table(block):
        low, high = fit(block * span, (block + 1) * span), width - block * span
        stop = high + line if block else high
        low += fit(high - span + line, stop)
        return 2.0 * low - energy(block % 2, span)

    chip, core = me_ref[0] // 2, lax.rem(me_ref[0], 2)
    outgoing = []

    def hand_over(done):
        for pair in range(chips):
            first, last = 2 * pair * share // line, -(-2 * (pair + 1) * share // line)
            if pair in handed or not all(row in done for row in range(first, last)):
                continue
            handed.add(pair)
            place = pair ^ chip
            given = pl.ds(pl.multiple_of((2 * pair + 1 - core) * share, share), share)
            kept = pl.ds(pl.multiple_of((2 * pair + core) * share, share), share)
            give[place] = weighted[:, given].astype(F32)
            outgoing.extend([
                pltpu.make_async_copy(give.at[place], give_hbm.at[place], out_sem.at[pair, 0]),
                pltpu.make_async_copy(weighted.at[:, kept], keep_hbm.at[place], out_sem.at[pair, 1]),
            ])
            outgoing[-2].start()
            outgoing[-1].start()

    handed, done = set(), set()
    total = jnp.zeros(score_ref.shape, F32)
    for block in range(blocks):
        for copy in incoming[block]:
            copy.wait()
        for row in range(block * deep, (block + 1) * deep):
            expand(row, block % 2, (row - block * deep) * line)
            done |= {row, box - row}
        if block == blocks - 1:
            expand(box // 2, 2, 0)
            done.add(box // 2)
        if block:
            total += block_table(block - 1)
        hand_over(done)
    total += block_table(blocks - 1)
    middle = width // 2
    total += 2.0 * fit(middle, middle + line) - energy(2, line)
    score_ref[...] = total
    for copy in outgoing:
        copy.wait()


def estep(me, index, images, planes, ctf_table, share):
    rows, width = images.shape
    chips = width // share // 2
    count = planes.shape[0]
    blocks = 4
    span = width // (2 * blocks)
    held = pl.BlockSpec(memory_space=pl.ANY)
    far = pl.BlockSpec(memory_space=pltpu.HBM)
    return pl.pallas_call(
        functools.partial(estep_kernel, blocks),
        in_specs=[pl.BlockSpec(memory_space=pltpu.SMEM)] + [far] * 4,
        out_specs=[held, held, pl.BlockSpec(memory_space=pltpu.VMEM)],
        out_shape=[
            jax.ShapeDtypeStruct((chips, rows, share), F32),
            jax.ShapeDtypeStruct((chips, rows, share), BF16),
            jax.ShapeDtypeStruct((rows, count), F32),
        ],
        scratch_shapes=[
            pltpu.VMEM(index.shape, jnp.int32),
            pltpu.VMEM((rows, width), BF16),
            pltpu.VMEM((count, width), BF16),
            pltpu.VMEM(ctf_table.shape, F32),
            pltpu.VMEM((rows, width), BF16),
            pltpu.VMEM((chips, rows, share), F32),
            pltpu.VMEM((3, rows, span), BF16),
            pltpu.VMEM((3, count, span), BF16),
            pltpu.SemaphoreType.DMA((2,)),
            pltpu.SemaphoreType.DMA((blocks, 2, 2)),
            pltpu.SemaphoreType.DMA((chips, 2)),
        ],
        compiler_params=params(28),
        name="estep",
    )(me, *[pltpu.with_memory_space_constraint(part, pltpu.HBM) for part in (index, images, planes, ctf_table)])


def count_kernel(slabs, slab_ref, prior_ref, noise_ref, list_ref, base_ref, scale_ref):
    rows, listed = list_ref.shape
    classes, _, width = base_ref.shape
    each = listed // classes
    local = width // slabs
    lane = lax.broadcasted_iota(jnp.int32, (rows, width), 1)
    home = slab_ref[0] ^ (lane // local)
    plane = home * local + lax.rem(lane, local)
    for one in range(classes):
        sums = jnp.zeros((rows, width), F32)
        for entry in range(each):
            place = one * each + entry
            sums += jnp.where(list_ref[:, place : place + 1] == plane, 1.0, 0.0)
        base_ref[one] = jnp.where(sums > 0.0, jnp.log(sums) + jnp.log(prior_ref[:, one : one + 1]), -jnp.inf)
    noise = jnp.broadcast_to(noise_ref[...], (rows, rows))
    diagonal = lax.broadcasted_iota(jnp.int32, (rows, rows), 0) == lax.broadcasted_iota(
        jnp.int32, (rows, rows), 1
    )
    column = jnp.sum(jnp.where(diagonal, noise, 0.0), axis=1, keepdims=True)
    scale_ref[...] = jnp.broadcast_to(column, (rows, width))


def count_planes(slab, class_weight, inv_noise, orientations, width, slabs):
    rows, classes, each = orientations.shape
    vmem = pl.BlockSpec(memory_space=pltpu.VMEM)
    return pl.pallas_call(
        functools.partial(count_kernel, slabs),
        in_specs=[pl.BlockSpec(memory_space=pltpu.SMEM), vmem, vmem, vmem],
        out_specs=[vmem, vmem],
        out_shape=[
            jax.ShapeDtypeStruct((classes, rows, width), F32),
            jax.ShapeDtypeStruct((rows, width), F32),
        ],
        compiler_params=params(4),
        cost_estimate=pl.CostEstimate(flops=10**7, bytes_accessed=10**6, transcendentals=0),
        name="count",
    )(
        slab,
        class_weight.reshape(1, classes),
        inv_noise.reshape(1, rows),
        orientations.reshape(rows, classes * each),
    )


def weigh_kernel(base_ref, scale_ref, *refs):
    out_ref = refs[-1]
    tables = [ref[...] for ref in refs[:-1]]
    classes = base_ref.shape[0]
    local = tables[0].shape[1] // classes
    scores = []
    for one in range(classes):
        cut = slice(one * local, (one + 1) * local)
        fit = jnp.concatenate([table[:, cut] for table in tables], axis=1)
        scores.append(base_ref[one] + scale_ref[...] * fit)
    peak = functools.reduce(jnp.maximum, [jnp.max(score, axis=1, keepdims=True) for score in scores])
    raw = [jnp.exp(score - peak) for score in scores]
    total = functools.reduce(jnp.add, [jnp.sum(part, axis=1, keepdims=True) for part in raw])
    own = jnp.concatenate([part[:, :local] for part in raw], axis=1) / total
    out_ref[...] = own.T


def weigh(base, scale, tables):
    rows, planes = tables[0].shape
    return pl.pallas_call(
        weigh_kernel,
        out_shape=jax.ShapeDtypeStruct((planes, rows), F32),
        compiler_params=params(4),
        name="weigh",
    )(base, scale, *tables)


def sums_kernel(items, own_w_ref, sib_w_ref, own_ctf_ref, sib_ctf_ref, keep_hbm, got_hbm, *refs):
    outs = refs[: len(items)]
    keep, got, sums, in_sem, out_sem = refs[-5:]
    tile = keep_hbm.shape[2] // 4
    number, _, wide = keep.shape
    cells = wide // tile
    places = [(out, slot, k, out) for out, ks in enumerate(items) for slot, k in enumerate(ks)]
    incoming, outgoing = [], []
    for place, (out, slot, k, side) in enumerate(places):
        copies = []
        for cell in range(cells):
            source = slice((2 * cell + side) * tile, (2 * cell + side + 1) * tile)
            target = slice(cell * tile, (cell + 1) * tile)
            copies += [
                pltpu.make_async_copy(
                    keep_hbm.at[k, :, source], keep.at[place, :, target], in_sem.at[place, cell, 0]
                ),
                pltpu.make_async_copy(
                    got_hbm.at[k, :, source], got.at[place, :, target], in_sem.at[place, cell, 1]
                ),
            ]
        incoming.append(copies)
        filled = sums.at[place] if side == 0 else sums.at[place, :, :wide]
        outgoing.append(pltpu.make_async_copy(filled, outs[out].at[slot], out_sem.at[place]))
    for copy in [copy for copies in incoming for copy in copies]:
        copy.start()
    weights = jnp.concatenate([own_w_ref[...], sib_w_ref[...]], axis=1).astype(BF16)
    ctf = jnp.concatenate([own_ctf_ref[...], sib_ctf_ref[...]], axis=0)
    shells = jnp.dot(weights, lanes_wide((ctf * ctf).astype(BF16)), preferred_element_type=F32)
    for place, (_, _, _, side) in enumerate(places):
        for copy in incoming[place]:
            copy.wait()
        images = jnp.concatenate([keep[place], got[place].astype(BF16)], axis=0)
        sums[place, :, :wide] = jnp.dot(weights, images, preferred_element_type=F32)
        if side == 0:
            sums[place, :, wide:] = shells
        outgoing[place].start()
    for copy in outgoing:
        copy.wait()


def partial_sums(items, own_w, sib_w, own_ctf, sib_ctf, keep, got):
    chips, rows, share = keep.shape
    planes = own_w.shape[0]
    wide = share // 2
    number = sum(len(ks) for ks in items)
    held = pl.BlockSpec(memory_space=pl.ANY)
    vmem = pl.BlockSpec(memory_space=pltpu.VMEM)
    return pl.pallas_call(
        functools.partial(sums_kernel, items),
        in_specs=[vmem] * 4 + [held] * 2,
        out_specs=[held] * 2,
        out_shape=[
            jax.ShapeDtypeStruct((len(ks), planes, wide + extra), F32)
            for ks, extra in zip(items, (LANES, 0))
        ],
        scratch_shapes=[
            pltpu.VMEM((number, rows, wide), BF16),
            pltpu.VMEM((number, rows, wide), F32),
            pltpu.VMEM((number, planes, wide + LANES), F32),
            pltpu.SemaphoreType.DMA((number, 2, 2)),
            pltpu.SemaphoreType.DMA((number,)),
        ],
        compiler_params=params(12),
        cost_estimate=pl.CostEstimate(
            flops=4 * planes * rows * wide * number,
            bytes_accessed=10 * planes * wide * number,
            transcendentals=0,
        ),
        name="sums",
    )(own_w, sib_w, own_ctf, sib_ctf, keep, got)


def finish_kernel(numbers, me_ref, index_hbm, *refs):
    total = sum(numbers)
    parts, (out_hbm, index, out, in_sem, out_sem) = refs[:total], refs[total:]
    planes, share = out.shape
    tile = share // 4
    wide = share // 2
    mine = pl.ds(pl.multiple_of(me_ref[0] * share, share), share)
    fetch = pltpu.make_async_copy(index_hbm.at[:, mine], index, in_sem)
    fetch.start()
    left, right = parts[: numbers[0]], parts[numbers[0] :]
    shells = functools.reduce(jnp.add, [ref[0, :, wide:] for ref in left])
    fetch.wait()
    stores = []
    for cell in range(2):
        for side, refs in ((0, left), (1, right)):
            for start in range(0, tile, LANES):
                place = (2 * cell + side) * tile + start
                cut = slice(cell * tile + start, cell * tile + start + LANES)
                block = functools.reduce(jnp.add, [ref[0, :, cut] for ref in refs])
                weight = spread(shells, index[:, place : place + LANES])
                out[:, place : place + LANES] = block / (weight + 1.0)
        cut = slice(cell * wide, (cell + 1) * wide)
        stores.append(pltpu.make_async_copy(out.at[:, cut], out_hbm.at[:, cut], out_sem.at[cell]))
        stores[-1].start()
    for store in stores:
        store.wait()


def finish(me, index, left, right, share):
    planes = left[0][0].shape[1]
    numbers = len(left), len(right)
    held = pl.BlockSpec(memory_space=pl.ANY)

    def first(part, place):
        return pl.BlockSpec((1,) + part.shape[1:], lambda step: (place, 0, 0))

    return pl.pallas_call(
        functools.partial(finish_kernel, numbers),
        grid=(1,),
        in_specs=[pl.BlockSpec(memory_space=pltpu.SMEM), held]
        + [first(part, place) if part.shape[0] > 1 else pl.BlockSpec(memory_space=pltpu.VMEM) for part, place in left + right],
        out_specs=held,
        out_shape=jax.ShapeDtypeStruct((planes, share), F32),
        scratch_shapes=[
            pltpu.VMEM((1, share), jnp.int32),
            pltpu.VMEM((planes, share), F32),
            pltpu.SemaphoreType.DMA(()),
            pltpu.SemaphoreType.DMA((2,)),
        ],
        compiler_params=params(12),
        name="finish",
    )(me, index, *[part for part, _ in left + right])


def swap(array, bit, size):
    return lax.ppermute(array, "img", [(one, one ^ bit) for one in range(size)])


def shards(images, references, orientations, ctf_table, inv_noise, class_weight):
    rows, width = images.shape
    classes, local_planes, _ = references.shape
    size = lax.axis_size("img")
    slabs = lax.axis_size("slab")
    chips = size // 2
    share = width // size
    me = lax.axis_index("img").astype(jnp.int32).reshape(1)
    slab = lax.axis_index("slab").astype(jnp.int32).reshape(1)
    index = entry_shells(width, ctf_table.shape[1])
    top_index = jnp.asarray(index[:, : width // 2 + 2 * math.isqrt(width // 2)])
    index = jnp.asarray(index)
    planes = references.reshape(classes * local_planes, width)

    give, keep, table = estep(me, top_index, images, planes, ctf_table, share)
    sib_ctf = swap(ctf_table, 1, size)
    tables = [table] + [
        lax.ppermute(table, "slab", [(one, one ^ other) for one in range(slabs)])
        for other in range(1, slabs)
    ]
    got = swap(give, 1, size)
    base, scale = count_planes(
        slab, class_weight, inv_noise, orientations, slabs * local_planes, slabs
    )
    own_w = weigh(base, scale, tables)
    sib_w = swap(own_w, 1, size)

    sums = functools.partial(
        partial_sums,
        own_w=own_w, sib_w=sib_w, own_ctf=ctf_table, sib_ctf=sib_ctf, keep=keep, got=got,
    )
    low = [1 << place for place in range(chips.bit_length() - 1)]
    orders = (low, low[::-1])
    first = [[k for k in range(chips) if k & order[0]] for order in orders]
    onward = [[k for k in ks if k & order[1]] for ks, order in zip(first, orders)]
    direct = [[k for k in ks if not k & order[1]] for ks, order in zip(first, orders)]
    stay = [[k for k in range(chips) if not k & order[0]] for order in orders]
    parts = [{k: [] for k in ks} for ks in stay]

    def deliver(side, ks, array, bit):
        arrived = swap(array, 2 * bit, size)
        for place, k in enumerate(ks):
            parts[side][k ^ bit].append((arrived, place))

    def compute(groups):
        return sums(tuple(tuple(ks) for ks in groups))

    sent = compute(onward)
    for side in (0, 1):
        deliver(side, onward[side], sent[side], orders[side][0])
    sent = compute(direct)
    for side in (0, 1):
        deliver(side, direct[side], sent[side], orders[side][0])
    kept = compute(stay)
    for side in (0, 1):
        for place, k in enumerate(stay[side]):
            parts[side][k].append((kept[side], place))
    for turn in range(1, len(low)):
        for side in (0, 1):
            bit = orders[side][turn]
            ks = [k for k in parts[side] if k & bit]
            sent = jnp.stack([sum(part[place] for part, place in parts[side].pop(k)) for k in ks])
            deliver(side, ks, sent, bit)
    out = finish(me, index, parts[0][0], parts[1][0], share)
    return out.reshape(classes, local_planes, share)


def solution(mesh):
    return jax.shard_map(
        shards,
        mesh=mesh,
        in_specs=(
            P("img", None),
            P(None, "slab", None),
            P("img", None, None),
            P("img", None),
            P("img"),
            P(),
        ),
        out_specs=P(None, "slab", "img"),
        check_vma=False,
    )
```

```python
import functools
import math

import jax
import jax.numpy as jnp
import numpy as np
from jax import lax
from jax.experimental import pallas as pl
from jax.experimental.pallas import tpu as pltpu
from jax.sharding import PartitionSpec as P

F32 = jnp.float32
BF16 = jnp.bfloat16
LANES = 128
MIB = 1024 * 1024


def entry_shells(width, shells):
    pixels = width // 2
    box = math.isqrt(pixels)
    place = np.arange(pixels)
    column = place % box - box // 2
    row = place // box - box // 2
    radius = column * column + row * row
    levels = np.arange(1, shells)
    shell = np.sum(2 * levels[None, :] ** 2 <= radius[:, None], axis=1)
    return np.repeat(shell, 2).astype(np.int32)[None, :]


def split_share(share):
    met = max(LANES, 3 * share // 16 // LANES * LANES)
    return share // 2 - met, met


def met_column(share, owner, slab):
    wide, met = split_share(share)
    return pl.multiple_of(owner * share + 2 * wide + lax.rem(slab, 2) * met, LANES)


def params(mib):
    return pltpu.CompilerParams(vmem_limit_bytes=mib * MIB)


def lanes_wide(table):
    rows, shells = table.shape
    if shells == LANES:
        return table
    return jnp.concatenate([table, jnp.zeros((rows, LANES - shells), table.dtype)], axis=1)


def spread(table, index):
    return jnp.take_along_axis(table, jnp.broadcast_to(index, table.shape), axis=1)


def contract_last(left, right):
    return lax.dot_general(left, right, (((1,), (1,)), ((), ())), preferred_element_type=F32)


def estep_kernel(
    blocks, share, near, me_ref, slab_ref, index_hbm, image_hbm, plane_hbm, ctf_hbm, *refs,
):
    give_hbm, keep_hbm, score_ref = refs[:3]
    near_refs = refs[3 : 3 + len(near)]
    index, image, plane, ctf_held, weighted, give, squared, energy_of = refs[-11:-3]
    small_sem, in_sem, out_sem = refs[-3:]
    rows, width = image.shape
    chips, summed = width // share // 2, 2 * split_share(share)[0]
    box = math.isqrt(width // 2)
    line = 2 * box
    deep = box // (2 * blocks)
    span = deep * line

    small = [
        pltpu.make_async_copy(index_hbm, index, small_sem.at[0]),
        pltpu.make_async_copy(ctf_hbm, ctf_held, small_sem.at[1]),
    ]
    incoming = []
    for block in range(blocks):
        copies = []
        for side, start in enumerate((block * span, width - (block + 1) * span)):
            cut = pl.ds(start, span)
            copies += [
                pltpu.make_async_copy(
                    image_hbm.at[:, cut], image.at[:, cut], in_sem.at[block, side, 0]
                ),
                pltpu.make_async_copy(
                    plane_hbm.at[:, cut], plane.at[:, cut], in_sem.at[block, side, 1]
                ),
            ]
        incoming.append(copies)
    for copy in small + [copy for copies in incoming for copy in copies]:
        copy.start()
    for copy in small:
        copy.wait()
    table = lanes_wide(ctf_held[...])

    def weigh_image(cut, ctf):
        weighted[:, cut] = (image[:, cut].astype(F32) * ctf).astype(BF16)

    def square(cut):
        part = plane[:, cut].astype(F32)
        return part * part

    def expand(row, slot, place):
        mirror = box - row if 0 < row < box // 2 else None
        for start in range(0, line, LANES):
            cut = slice(row * line + start, row * line + start + LANES)
            ctf = spread(table, index[:, cut])
            weigh_image(cut, ctf)
            power = square(cut)
            if mirror is not None:
                other = slice(mirror * line + start, mirror * line + start + LANES)
                weigh_image(other, ctf)
                power += square(other)
            held = slice(place + start, place + start + LANES)
            squared[slot, :, held] = (ctf * ctf).astype(BF16)
            energy_of[slot, :, held] = power.astype(BF16)

    def fit(start, stop):
        return contract_last(weighted[:, start:stop], plane[:, start:stop])

    def energy(slot, size):
        return contract_last(squared[slot, :, :size], energy_of[slot, :, :size])

    def block_table(block):
        low, high = fit(block * span, (block + 1) * span), width - block * span
        stop = high + line if block else high
        low += fit(high - span + line, stop)
        return 2.0 * low - energy(block % 2, span)

    chip, core = me_ref[0] // 2, lax.rem(me_ref[0], 2)
    outgoing = []

    def hand_over(done):
        for pair in range(chips):
            first, last = 2 * pair * share // line, -(-2 * (pair + 1) * share // line)
            if pair in handed or not all(row in done for row in range(first, last)):
                continue
            handed.add(pair)
            place = pair ^ chip
            given = pl.ds(pl.multiple_of((2 * pair + 1 - core) * share, share), summed)
            kept = pl.ds(pl.multiple_of((2 * pair + core) * share, share), summed)
            at = pl.ds(pl.multiple_of(place * summed, LANES), summed)
            give[:, at] = weighted[:, given].astype(F32)
            outgoing.extend([
                pltpu.make_async_copy(give.at[:, at], give_hbm.at[:, at], out_sem.at[pair, 0]),
                pltpu.make_async_copy(weighted.at[:, kept], keep_hbm.at[:, at], out_sem.at[pair, 1]),
            ])
            outgoing[-2].start()
            outgoing[-1].start()

    tail = slice(chips * summed, chips * summed + LANES)
    give[:, tail] = table
    outgoing.append(pltpu.make_async_copy(give.at[:, tail], give_hbm.at[:, tail], out_sem.at[chips, 0]))
    outgoing[-1].start()
    handed, done = set(), set()
    total = jnp.zeros(score_ref.shape, F32)
    for block in range(blocks):
        for copy in incoming[block]:
            copy.wait()
        for row in range(block * deep, (block + 1) * deep):
            expand(row, block % 2, (row - block * deep) * line)
            done |= {row, box - row}
        if block == blocks - 1:
            expand(box // 2, 2, 0)
            done.add(box // 2)
        if block:
            total += block_table(block - 1)
        hand_over(done)
    total += block_table(blocks - 1)
    middle = width // 2
    total += 2.0 * fit(middle, middle + line) - energy(2, line)
    score_ref[...] = total
    for k, near_ref in zip(near, near_refs):
        for other in range(2):
            owner = (k ^ chip) * 2 + lax.rem(core + other, 2)
            part = weighted[:, pl.ds(met_column(share, owner, slab_ref[0]), near_ref.shape[2])]
            near_ref[other] = part.astype(near_ref.dtype)
    for copy in outgoing:
        copy.wait()


def far(*operands):
    return [pltpu.with_memory_space_constraint(operand, pltpu.HBM) for operand in operands]


def estep(me, slab, index, images, planes, ctf_table, share, near):
    rows, width = images.shape
    chips = width // share // 2
    wide, met = split_share(share)
    summed = 2 * wide
    count = planes.shape[0]
    blocks = 4
    span = width // (2 * blocks)
    held = pl.BlockSpec(memory_space=pl.ANY)
    vmem = pl.BlockSpec(memory_space=pltpu.VMEM)
    hbm = pl.BlockSpec(memory_space=pltpu.HBM)
    return pl.pallas_call(
        functools.partial(estep_kernel, blocks, share, near),
        in_specs=[pl.BlockSpec(memory_space=pltpu.SMEM)] * 2 + [hbm] * 4,
        out_specs=[held, held] + [vmem] * (1 + len(near)),
        out_shape=[
            jax.ShapeDtypeStruct((rows, chips * summed + LANES), F32),
            pltpu.HBM((rows, chips * summed), BF16),
            jax.ShapeDtypeStruct((rows, count), F32),
        ]
        + [
            jax.ShapeDtypeStruct((2, rows, met), F32) if k else pltpu.HBM((2, rows, met), BF16)
            for k in near
        ],
        scratch_shapes=[
            pltpu.VMEM(index.shape, jnp.int32),
            pltpu.VMEM((rows, width), BF16),
            pltpu.VMEM((count, width), BF16),
            pltpu.VMEM(ctf_table.shape, F32),
            pltpu.VMEM((rows, width), BF16),
            pltpu.VMEM((rows, chips * summed + LANES), F32),
            pltpu.VMEM((3, rows, span), BF16),
            pltpu.VMEM((3, count, span), BF16),
            pltpu.SemaphoreType.DMA((2,)),
            pltpu.SemaphoreType.DMA((blocks, 2, 2)),
            pltpu.SemaphoreType.DMA((chips + 1, 2)),
        ],
        compiler_params=params(28),
        name="estep",
    )(me, slab, *far(index, images, planes, ctf_table))


def early_kernel(share, beyond, me_ref, slab_ref, index_hbm, image_hbm, ctf_hbm, *refs):
    outs = refs[: len(beyond)]
    index, image, ctf_held, index_sem, image_sem, ctf_sem = refs[len(beyond) :]
    _, rows, met = outs[0].shape
    chip, core = me_ref[0] // 2, lax.rem(me_ref[0], 2)
    fetch = pltpu.make_async_copy(ctf_hbm, ctf_held, ctf_sem)
    fetch.start()
    copies = []
    for place, k in enumerate(beyond):
        for other in range(2):
            owner = (k ^ chip) * 2 + lax.rem(core + other, 2)
            cut = pl.ds(met_column(share, owner, slab_ref[0]), met)
            copies.append([
                pltpu.make_async_copy(
                    index_hbm.at[:, cut], index.at[place, other], index_sem.at[place, other]
                ),
                pltpu.make_async_copy(
                    image_hbm.at[:, cut], image.at[place, other], image_sem.at[place, other]
                ),
            ])
            for copy in copies[-1]:
                copy.start()
    fetch.wait()
    table = lanes_wide(ctf_held[...])
    for place, out_ref in enumerate(outs):
        for other in range(2):
            for copy in copies[2 * place + other]:
                copy.wait()
            for start in range(0, met, LANES):
                cut = slice(start, start + LANES)
                ctf = spread(table, index[place, other, :, cut])
                part = (image[place, other, :, cut].astype(F32) * ctf).astype(BF16)
                out_ref[other, :, cut] = part.astype(F32)


def early_images(me, slab, index, images, ctf_table, share, beyond):
    rows = images.shape[0]
    met = split_share(share)[1]
    number = len(beyond)
    vmem = pl.BlockSpec(memory_space=pltpu.VMEM)
    smem = pl.BlockSpec(memory_space=pltpu.SMEM)
    hbm = pl.BlockSpec(memory_space=pltpu.HBM)
    return pl.pallas_call(
        functools.partial(early_kernel, share, beyond),
        in_specs=[smem, smem, hbm, hbm, hbm],
        out_specs=[vmem] * number,
        out_shape=[jax.ShapeDtypeStruct((2, rows, met), F32)] * number,
        scratch_shapes=[
            pltpu.VMEM((number, 2, 1, met), jnp.int32),
            pltpu.VMEM((number, 2, rows, met), BF16),
            pltpu.VMEM(ctf_table.shape, F32),
            pltpu.SemaphoreType.DMA((number, 2)),
            pltpu.SemaphoreType.DMA((number, 2)),
            pltpu.SemaphoreType.DMA(()),
        ],
        compiler_params=params(12),
        name="early",
    )(me, slab, *far(index, images, ctf_table))


def count_kernel(slabs, slab_ref, prior_ref, noise_ref, list_ref, base_ref, scale_ref):
    rows, listed = list_ref.shape
    classes, _, width = base_ref.shape
    each = listed // classes
    local = width // slabs
    lane = lax.broadcasted_iota(jnp.int32, (rows, width), 1)
    home = slab_ref[0] ^ (lane // local)
    plane = home * local + lax.rem(lane, local)
    for one in range(classes):
        sums = jnp.zeros((rows, width), F32)
        for entry in range(each):
            place = one * each + entry
            sums += jnp.where(list_ref[:, place : place + 1] == plane, 1.0, 0.0)
        base_ref[one] = jnp.where(sums > 0.0, jnp.log(sums) + jnp.log(prior_ref[:, one : one + 1]), -jnp.inf)
    noise = jnp.broadcast_to(noise_ref[...], (rows, rows))
    diagonal = lax.broadcasted_iota(jnp.int32, (rows, rows), 0) == lax.broadcasted_iota(
        jnp.int32, (rows, rows), 1
    )
    column = jnp.sum(jnp.where(diagonal, noise, 0.0), axis=1, keepdims=True)
    scale_ref[...] = jnp.broadcast_to(column, (rows, width))


def count_planes(slab, class_weight, inv_noise, orientations, width, slabs):
    rows, classes, each = orientations.shape
    vmem = pl.BlockSpec(memory_space=pltpu.VMEM)
    return pl.pallas_call(
        functools.partial(count_kernel, slabs),
        in_specs=[pl.BlockSpec(memory_space=pltpu.SMEM), vmem, vmem, vmem],
        out_specs=[vmem, vmem],
        out_shape=[
            jax.ShapeDtypeStruct((classes, rows, width), F32),
            jax.ShapeDtypeStruct((rows, width), F32),
        ],
        compiler_params=params(4),
        name="count",
    )(
        slab,
        class_weight.reshape(1, classes),
        inv_noise.reshape(1, rows),
        orientations.reshape(rows, classes * each),
    )


def weigh_kernel(base_ref, scale_ref, *refs):
    table_refs, (own_ref, both_ref) = refs[:-2], refs[-2:]
    classes = base_ref.shape[0]
    planes = own_ref.shape[0]
    local = planes // classes
    scores = []
    for one in range(classes):
        parts = [
            ref[:, start + one * local : start + (one + 1) * local]
            for ref in table_refs
            for start in range(0, ref.shape[1], planes)
        ]
        scores.append(base_ref[one] + scale_ref[...] * jnp.concatenate(parts, axis=1))
    peak = functools.reduce(jnp.maximum, [jnp.max(score, axis=1, keepdims=True) for score in scores])
    raw = [jnp.exp(score - peak) for score in scores]
    total = functools.reduce(jnp.add, [jnp.sum(part, axis=1, keepdims=True) for part in raw])
    slabs = [
        jnp.concatenate([part[:, place * local : (place + 1) * local] for part in raw], axis=1) / total
        for place in range(2)
    ]
    own_ref[...] = slabs[0].T
    both_ref[...] = jnp.concatenate(slabs, axis=1)


def weigh(base, scale, tables, planes):
    rows = base.shape[1]
    return pl.pallas_call(
        weigh_kernel,
        out_shape=[
            jax.ShapeDtypeStruct((planes, rows), F32),
            jax.ShapeDtypeStruct((rows, 2 * planes), F32),
        ],
        compiler_params=params(4),
        name="weigh",
    )(base, scale, *tables)


def sums_kernel(items, own_w_ref, sib_w_ref, both_w_ref, own_ctf_ref, keep_hbm, got_hbm, *refs):
    outs = refs[: len(items)]
    keep, got, sib_ctf, in_sem, ctf_sem = refs[len(items) :]
    number, _, wide = keep.shape
    tail = slice(keep_hbm.shape[1], keep_hbm.shape[1] + LANES)
    fetch = pltpu.make_async_copy(got_hbm.at[:, tail], sib_ctf, ctf_sem)
    fetch.start()
    places = [(slot, k, side) for side, ks in enumerate(items) for slot, k in enumerate(ks)]
    incoming = []
    for place, (slot, k, side) in enumerate(places):
        source = slice((2 * k + side) * wide, (2 * k + side + 1) * wide)
        incoming.append([
            pltpu.make_async_copy(keep_hbm.at[:, source], keep.at[place], in_sem.at[place, 0]),
            pltpu.make_async_copy(got_hbm.at[:, source], got.at[place], in_sem.at[place, 1]),
        ])
        for copy in incoming[-1]:
            copy.start()
    weights = jnp.concatenate([own_w_ref[...], sib_w_ref[...]], axis=1).astype(BF16)
    fetch.wait()
    ctf = jnp.concatenate([lanes_wide(own_ctf_ref[...]), sib_ctf[...]], axis=0)
    shell_sums = jnp.dot(weights, (ctf * ctf).astype(BF16), preferred_element_type=F32)
    for place, (slot, k, side) in enumerate(places):
        for copy in incoming[place]:
            copy.wait()
        images = jnp.concatenate([keep[place], got[place].astype(BF16)], axis=0)
        outs[side][slot, :, :wide] = jnp.dot(weights, images, preferred_element_type=F32)
        if side == 0:
            outs[side][slot, :, wide : wide + LANES] = shell_sums
        behind = wide + (LANES if side == 0 else 0)
        if outs[side].shape[2] > behind:
            outs[side][slot, :, behind:] = both_w_ref[...]


def partial_sums(items, with_weights, own_w, sib_w, both_w, own_ctf, keep, got, wide):
    rows = keep.shape[0]
    planes = own_w.shape[0]
    number = sum(len(ks) for ks in items)
    held = pl.BlockSpec(memory_space=pl.ANY)
    vmem = pl.BlockSpec(memory_space=pltpu.VMEM)
    rider = both_w.shape[1] if with_weights else 0
    return pl.pallas_call(
        functools.partial(sums_kernel, items),
        in_specs=[vmem] * 4 + [held] * 2,
        out_specs=[vmem] * 2,
        out_shape=[
            jax.ShapeDtypeStruct((len(ks), planes, wide + extra + rider), F32)
            for ks, extra in zip(items, (LANES, 0))
        ],
        scratch_shapes=[
            pltpu.VMEM((number, rows, wide), BF16),
            pltpu.VMEM((number, rows, wide), F32),
            pltpu.VMEM((rows, LANES), F32),
            pltpu.SemaphoreType.DMA((number, 2)),
            pltpu.SemaphoreType.DMA(()),
        ],
        compiler_params=params(12),
        name="sums",
    )(own_w, sib_w, both_w, own_ctf, keep, got)


def meet_kernel(chips, *refs):
    weight_refs, image_refs, outs = refs[:chips], refs[chips : 2 * chips], refs[2 * chips :]
    planes = outs[0].shape[0]
    weights = []
    for ref in weight_refs:
        wide = ref.shape[-1]
        part = ref[:, wide - planes :] if len(ref.shape) == 2 else ref[0, :, wide - planes :]
        weights.append(part.astype(BF16))
    weights = jnp.concatenate(weights, axis=0)
    for other, out_ref in enumerate(outs):
        images = jnp.concatenate([ref[other].astype(BF16) for ref in image_refs], axis=0)
        out_ref[...] = lax.dot_general(
            weights, images, (((0,), (0,)), ((), ())), preferred_element_type=F32
        )


def meet(weights, images):
    _, rows, met = images[0].shape
    planes = weights[0].shape[1]
    return pl.pallas_call(
        functools.partial(meet_kernel, len(weights)),
        out_shape=[jax.ShapeDtypeStruct((planes, met), F32)] * 2,
        compiler_params=params(16),
        name="meet",
    )(*weights, *images)


def finish_kernel(numbers, me_ref, slab_ref, index_hbm, met_ref, sib_met_ref, partner_ref, *refs):
    total = sum(numbers)
    parts, (out_hbm, index, out, in_sem, out_sem) = refs[:total], refs[total:]
    planes, share = out.shape
    wide, met = split_share(share)
    mine = pl.ds(pl.multiple_of(me_ref[0] * share, share), share)
    fetch = pltpu.make_async_copy(index_hbm.at[:, mine], index, in_sem)
    fetch.start()
    left, right = parts[: numbers[0]], parts[numbers[0] :]
    shells = functools.reduce(jnp.add, [ref[0, :, wide : wide + LANES] for ref in left])
    half = lax.rem(slab_ref[0], 2)
    fetch.wait()

    def divide(block_of, place, size):
        for start in range(0, size, LANES):
            at = pl.ds(pl.multiple_of(place + start, LANES), LANES)
            weight = spread(shells, index[:, at])
            out[:, at] = block_of(slice(start, start + LANES)) / (weight + 1.0)

    def summed(sides):
        return lambda cut: functools.reduce(jnp.add, [ref[0, :, cut] for ref in sides])

    divide(lambda cut: met_ref[:planes, cut] + sib_met_ref[:planes, cut], 2 * wide + half * met, met)
    divide(lambda cut: partner_ref[:, cut], 2 * wide + (1 - half) * met, met)
    stores = []
    for step, work in enumerate((None, (left, 0), (right, 1))):
        cut = slice(2 * wide, share)
        if work is not None:
            sides, place = work
            divide(summed(sides), place * wide, wide)
            cut = slice(place * wide, (place + 1) * wide)
        stores.append(pltpu.make_async_copy(out.at[:, cut], out_hbm.at[:, cut], out_sem.at[step]))
        stores[-1].start()
    for store in stores:
        store.wait()


def finish(me, slab, index, met, sib_met, partner, left, right, share):
    planes = partner.shape[0]
    numbers = len(left), len(right)
    held = pl.BlockSpec(memory_space=pl.ANY)
    vmem = pl.BlockSpec(memory_space=pltpu.VMEM)

    def first(part, place):
        if part.shape[0] == 1:
            return vmem
        return pl.BlockSpec((1,) + part.shape[1:], lambda step: (place, 0, 0))

    return pl.pallas_call(
        functools.partial(finish_kernel, numbers),
        grid=(1,),
        in_specs=[pl.BlockSpec(memory_space=pltpu.SMEM)] * 2
        + [held, vmem, vmem, vmem]
        + [first(part, place) for part, place in left + right],
        out_specs=held,
        out_shape=jax.ShapeDtypeStruct((planes, share), F32),
        scratch_shapes=[
            pltpu.VMEM((1, share), jnp.int32),
            pltpu.VMEM((planes, share), F32),
            pltpu.SemaphoreType.DMA(()),
            pltpu.SemaphoreType.DMA((3,)),
        ],
        compiler_params=params(12),
        name="finish",
    )(me, slab, index, met, sib_met, partner, *[part for part, _ in left + right])


def swap(array, bit, size):
    return lax.ppermute(array, "img", [(one, one ^ bit) for one in range(size)])


def shards(images, references, orientations, ctf_table, inv_noise, class_weight):
    rows, width = images.shape
    classes, local_planes, _ = references.shape
    size = lax.axis_size("img")
    slabs = lax.axis_size("slab")
    chips = size // 2
    share = width // size
    me = lax.axis_index("img").astype(jnp.int32).reshape(1)
    slab = lax.axis_index("slab").astype(jnp.int32).reshape(1)
    index = entry_shells(width, ctf_table.shape[1])
    top_index = jnp.asarray(index[:, : width // 2 + 2 * math.isqrt(width // 2)])
    index = jnp.asarray(index)
    planes = references.reshape(classes * local_planes, width)

    beyond = tuple(k for k in range(chips) if k & (k - 1))
    near = tuple(k for k in range(chips) if k not in beyond)
    met_images = {}
    if beyond:
        early = early_images(me, slab, index, images, ctf_table, share, beyond)
        images, *early = lax.optimization_barrier((images, *early))
        met_images = {k: swap(part, 2 * k, size) for k, part in zip(beyond, early)}
    give, keep, table, *parts_near = estep(
        me, slab, top_index, images, planes, ctf_table, share, near
    )
    if beyond:
        give, keep, met_images[beyond[-1]], *parts_near = lax.optimization_barrier(
            (give, keep, met_images[beyond[-1]], *parts_near)
        )
    for k, part in zip(near, parts_near):
        met_images[k] = swap(part, 2 * k, size) if k else part
    keep, *met_images = lax.optimization_barrier(
        (keep, *[met_images[k] for k in range(chips)])
    )
    keep, *met_images = far(keep, *met_images)
    base, scale = count_planes(
        slab, class_weight, inv_noise, orientations, slabs * local_planes, slabs
    )
    tables, bit = [table], 1
    while bit < slabs:
        held = tables[0]
        if len(tables) > 1:
            held = jnp.concatenate(tables, axis=1)
        pairs = [(one, one ^ bit) for one in range(slabs)]
        tables = [held, lax.ppermute(held, "slab", pairs)]
        bit *= 2
    got = swap(give, 1, size)
    own_w, both_w = weigh(base, scale, tables, classes * local_planes)
    sib_w = swap(own_w, 1, size)

    sums = functools.partial(
        partial_sums,
        own_w=own_w, sib_w=sib_w, both_w=both_w, own_ctf=ctf_table, keep=keep, got=got,
        wide=split_share(share)[0],
    )
    low = [1 << place for place in range(chips.bit_length() - 1)]
    orders = (low, low[::-1])
    first = [[k for k in range(chips) if k & order[0]] for order in orders]
    onward = [[k for k in ks if k & order[1]] for ks, order in zip(first, orders)]
    direct = [[k for k in ks if not k & order[1]] for ks, order in zip(first, orders)]
    stay = [[k for k in range(chips) if not k & order[0]] for order in orders]
    parts = [{k: [] for k in ks} for ks in stay]

    def deliver(side, ks, array, bit):
        arrived = swap(array, 2 * bit, size)
        for place, k in enumerate(ks):
            parts[side][k ^ bit].append((arrived, place))
        return arrived

    def compute(groups, with_weights=False):
        return sums(tuple(tuple(ks) for ks in groups), with_weights)

    sent = compute(onward, True)
    far_w = {0: both_w}
    for side in (0, 1):
        bit = orders[side][0]
        far_w[bit] = deliver(side, onward[side], sent[side], bit)
    both_w, _ = lax.optimization_barrier((both_w, sent[1]))
    for k in range(1, chips):
        if k not in far_w:
            far_w[k] = swap(both_w, 2 * k, size)
    sent = compute(direct)
    for side in (0, 1):
        deliver(side, direct[side], sent[side], orders[side][0])
    kept = compute(stay)
    for side in (0, 1):
        for place, k in enumerate(stay[side]):
            parts[side][k].append((kept[side], place))

    met, for_sib = meet([far_w[k] for k in range(chips)], met_images)
    sib_met = swap(for_sib, 1, size)
    own_planes = classes * local_planes
    partner = lax.ppermute(
        met[own_planes:] + sib_met[own_planes:], "slab", [(one, one ^ 1) for one in range(slabs)]
    )

    for turn in range(1, len(low)):
        for side in (0, 1):
            bit = orders[side][turn]
            ks = [k for k in parts[side] if k & bit]
            size_out = kept[side].shape[2]
            sent = jnp.stack(
                [sum(part[place, :, :size_out] for part, place in parts[side].pop(k)) for k in ks]
            )
            deliver(side, ks, sent, bit)
    out = finish(me, slab, index, met, sib_met, partner, parts[0][0], parts[1][0], share)
    return out.reshape(classes, local_planes, share)


def solution(mesh):
    return jax.shard_map(
        shards,
        mesh=mesh,
        in_specs=(
            P("img", None),
            P(None, "slab", None),
            P("img", None, None),
            P("img", None),
            P("img"),
            P(),
        ),
        out_specs=P(None, "slab", "img"),
        check_vma=False,
    )
```

```python
import functools
import math

import jax
import jax.numpy as jnp
import numpy as np
from jax import lax
from jax.experimental import pallas as pl
from jax.experimental.pallas import tpu as pltpu
from jax.sharding import PartitionSpec as P

F32 = jnp.float32
BF16 = jnp.bfloat16
LANES = 128
MIB = 1024 * 1024


def entry_shells(width, shells):
    pixels = width // 2
    box = math.isqrt(pixels)
    place = np.arange(pixels)
    column = place % box - box // 2
    row = place // box - box // 2
    radius = column * column + row * row
    levels = np.arange(1, shells)
    shell = np.sum(2 * levels[None, :] ** 2 <= radius[:, None], axis=1)
    return np.repeat(shell, 2).astype(np.int32)[None, :]


def split_share(share):
    met = max(LANES, 6 * share // 32 // LANES * LANES)
    return share // 2 - met, met


def met_column(share, owner, slab):
    wide, met = split_share(share)
    return pl.multiple_of(owner * share + 2 * wide + lax.rem(slab, 2) * met, LANES)


def params(mib):
    return pltpu.CompilerParams(vmem_limit_bytes=mib * MIB)


def lanes_wide(table):
    rows, shells = table.shape
    if shells == LANES:
        return table
    return jnp.concatenate([table, jnp.zeros((rows, LANES - shells), table.dtype)], axis=1)


def spread(table, index):
    return jnp.take_along_axis(table, jnp.broadcast_to(index, table.shape), axis=1)


def contract_last(left, right):
    return lax.dot_general(left, right, (((1,), (1,)), ((), ())), preferred_element_type=F32)


def estep_kernel(
    blocks, share, near, me_ref, slab_ref, index_hbm, image_hbm, plane_hbm, ctf_hbm, *refs,
):
    give_hbm, keep_hbm, score_ref = refs[:3]
    near_refs = refs[3 : 3 + len(near)]
    index, image, plane, ctf_held, weighted, give, squared, energy_of = refs[-11:-3]
    small_sem, in_sem, out_sem = refs[-3:]
    rows, width = image.shape
    wide, met = split_share(share)
    chips, summed = width // share // 2, 2 * wide
    box = math.isqrt(width // 2)
    line = 2 * box
    deep = box // (2 * blocks)
    span = deep * line

    small = [
        pltpu.make_async_copy(index_hbm, index, small_sem.at[0]),
        pltpu.make_async_copy(ctf_hbm, ctf_held, small_sem.at[1]),
    ]
    incoming = []
    for block in range(blocks):
        copies = []
        for side, start in enumerate((block * span, width - (block + 1) * span)):
            cut = pl.ds(start, span)
            copies += [
                pltpu.make_async_copy(
                    image_hbm.at[:, cut], image.at[:, cut], in_sem.at[block, side, 0]
                ),
                pltpu.make_async_copy(
                    plane_hbm.at[:, cut], plane.at[:, cut], in_sem.at[block, side, 1]
                ),
            ]
        incoming.append(copies)
    for copy in small + [copy for copies in incoming for copy in copies]:
        copy.start()
    for copy in small:
        copy.wait()
    table = lanes_wide(ctf_held[...])

    def weigh_image(cut, ctf):
        weighted[:, cut] = (image[:, cut].astype(F32) * ctf).astype(BF16)

    def square(cut):
        part = plane[:, cut].astype(F32)
        return part * part

    def expand(row, slot, place):
        mirror = box - row if 0 < row < box // 2 else None
        for start in range(0, line, LANES):
            cut = slice(row * line + start, row * line + start + LANES)
            ctf = spread(table, index[:, cut])
            weigh_image(cut, ctf)
            power = square(cut)
            if mirror is not None:
                other = slice(mirror * line + start, mirror * line + start + LANES)
                weigh_image(other, ctf)
                power += square(other)
            held = slice(place + start, place + start + LANES)
            squared[slot, :, held] = (ctf * ctf).astype(BF16)
            energy_of[slot, :, held] = power.astype(BF16)

    def fit(start, stop):
        return contract_last(weighted[:, start:stop], plane[:, start:stop])

    def energy(slot, size):
        return contract_last(squared[slot, :, :size], energy_of[slot, :, :size])

    def block_table(block):
        low, high = fit(block * span, (block + 1) * span), width - block * span
        stop = high + line if block else high
        low += fit(high - span + line, stop)
        return 2.0 * low - energy(block % 2, span)

    chip, core = me_ref[0] // 2, lax.rem(me_ref[0], 2)
    outgoing = []

    def hand_over(done):
        for pair in range(chips):
            first, last = 2 * pair * share // line, -(-2 * (pair + 1) * share // line)
            if pair in handed or not all(row in done for row in range(first, last)):
                continue
            handed.add(pair)
            place = pair ^ chip
            given = pl.ds(pl.multiple_of((2 * pair + 1 - core) * share, share), summed)
            kept = pl.ds(pl.multiple_of((2 * pair + core) * share, share), summed)
            at = pl.ds(pl.multiple_of(place * summed, LANES), summed)
            give[:, at] = weighted[:, given].astype(F32)
            outgoing.extend([
                pltpu.make_async_copy(give.at[:, at], give_hbm.at[:, at], out_sem.at[pair, 0]),
                pltpu.make_async_copy(weighted.at[:, kept], keep_hbm.at[:, at], out_sem.at[pair, 1]),
            ])
            outgoing[-2].start()
            outgoing[-1].start()

    handed, done = set(), set()
    total = jnp.zeros(score_ref.shape, F32)
    for block in range(blocks):
        for copy in incoming[block]:
            copy.wait()
        for row in range(block * deep, (block + 1) * deep):
            expand(row, block % 2, (row - block * deep) * line)
            done |= {row, box - row}
        if block == blocks - 1:
            expand(box // 2, 2, 0)
            done.add(box // 2)
        if block:
            total += block_table(block - 1)
        hand_over(done)
    total += block_table(blocks - 1)
    middle = width // 2
    total += 2.0 * fit(middle, middle + line) - energy(2, line)
    score_ref[...] = total
    for k, near_ref in zip(near, near_refs):
        for other in range(2):
            owner = (k ^ chip) * 2 + lax.rem(core + other, 2)
            part = weighted[:, pl.ds(met_column(share, owner, slab_ref[0]), met)]
            near_ref[:, other * met : (other + 1) * met] = part.astype(near_ref.dtype)
        if k:
            near_ref[:, 2 * met :] = table
    for copy in outgoing:
        copy.wait()


def far(*operands):
    return [pltpu.with_memory_space_constraint(operand, pltpu.HBM) for operand in operands]


def estep(me, slab, index, images, planes, ctf_table, share, near):
    rows, width = images.shape
    chips = width // share // 2
    wide, met = split_share(share)
    summed = 2 * wide
    count = planes.shape[0]
    blocks = 4
    span = width // (2 * blocks)
    held = pl.BlockSpec(memory_space=pl.ANY)
    vmem = pl.BlockSpec(memory_space=pltpu.VMEM)
    hbm = pl.BlockSpec(memory_space=pltpu.HBM)
    return pl.pallas_call(
        functools.partial(estep_kernel, blocks, share, near),
        in_specs=[pl.BlockSpec(memory_space=pltpu.SMEM)] * 2 + [hbm] * 4,
        out_specs=[held, held] + [vmem] * (1 + len(near)),
        out_shape=[
            jax.ShapeDtypeStruct((rows, chips * summed), F32),
            pltpu.HBM((rows, chips * summed), BF16),
            jax.ShapeDtypeStruct((rows, count), F32),
        ]
        + [
            jax.ShapeDtypeStruct((rows, 2 * met + LANES), F32)
            if k
            else pltpu.HBM((rows, 2 * met), BF16)
            for k in near
        ],
        scratch_shapes=[
            pltpu.VMEM(index.shape, jnp.int32),
            pltpu.VMEM((rows, width), BF16),
            pltpu.VMEM((count, width), BF16),
            pltpu.VMEM(ctf_table.shape, F32),
            pltpu.VMEM((rows, width), BF16),
            pltpu.VMEM((rows, chips * summed), F32),
            pltpu.VMEM((3, rows, span), BF16),
            pltpu.VMEM((3, count, span), BF16),
            pltpu.SemaphoreType.DMA((2,)),
            pltpu.SemaphoreType.DMA((blocks, 2, 2)),
            pltpu.SemaphoreType.DMA((chips, 2)),
        ],
        compiler_params=params(28),
        name="estep",
    )(me, slab, *far(index, images, planes, ctf_table))


def early_kernel(share, beyond, me_ref, slab_ref, index_hbm, image_hbm, ctf_hbm, *refs):
    outs = refs[: len(beyond)]
    index, image, ctf_held, index_sem, image_sem, ctf_sem = refs[len(beyond) :]
    met = split_share(share)[1]
    chip, core = me_ref[0] // 2, lax.rem(me_ref[0], 2)
    fetch = pltpu.make_async_copy(ctf_hbm, ctf_held, ctf_sem)
    fetch.start()
    copies = []
    for place, k in enumerate(beyond):
        for other in range(2):
            owner = (k ^ chip) * 2 + lax.rem(core + other, 2)
            cut = pl.ds(met_column(share, owner, slab_ref[0]), met)
            copies.append([
                pltpu.make_async_copy(
                    index_hbm.at[:, cut], index.at[place, other], index_sem.at[place, other]
                ),
                pltpu.make_async_copy(
                    image_hbm.at[:, cut], image.at[place, other], image_sem.at[place, other]
                ),
            ])
            for copy in copies[-1]:
                copy.start()
    fetch.wait()
    table = lanes_wide(ctf_held[...])
    for place, out_ref in enumerate(outs):
        for other in range(2):
            for copy in copies[2 * place + other]:
                copy.wait()
            for start in range(0, met, LANES):
                cut = slice(start, start + LANES)
                ctf = spread(table, index[place, other, :, cut])
                part = (image[place, other, :, cut].astype(F32) * ctf).astype(BF16)
                out_ref[:, other * met + start : other * met + start + LANES] = part.astype(F32)
        out_ref[:, 2 * met :] = table


def early_images(me, slab, index, images, ctf_table, share, beyond):
    rows = images.shape[0]
    met = split_share(share)[1]
    number = len(beyond)
    vmem = pl.BlockSpec(memory_space=pltpu.VMEM)
    smem = pl.BlockSpec(memory_space=pltpu.SMEM)
    hbm = pl.BlockSpec(memory_space=pltpu.HBM)
    return pl.pallas_call(
        functools.partial(early_kernel, share, beyond),
        in_specs=[smem, smem, hbm, hbm, hbm],
        out_specs=[vmem] * number,
        out_shape=[jax.ShapeDtypeStruct((rows, 2 * met + LANES), F32)] * number,
        scratch_shapes=[
            pltpu.VMEM((number, 2, 1, met), jnp.int32),
            pltpu.VMEM((number, 2, rows, met), BF16),
            pltpu.VMEM(ctf_table.shape, F32),
            pltpu.SemaphoreType.DMA((number, 2)),
            pltpu.SemaphoreType.DMA((number, 2)),
            pltpu.SemaphoreType.DMA(()),
        ],
        compiler_params=params(12),
        name="early",
    )(me, slab, *far(index, images, ctf_table))


def count_kernel(slabs, slab_ref, prior_ref, noise_ref, list_ref, base_ref, scale_ref):
    rows, listed = list_ref.shape
    classes, _, width = base_ref.shape
    each = listed // classes
    local = width // slabs
    lane = lax.broadcasted_iota(jnp.int32, (rows, width), 1)
    home = slab_ref[0] ^ (lane // local)
    plane = home * local + lax.rem(lane, local)
    for one in range(classes):
        sums = jnp.zeros((rows, width), F32)
        for entry in range(each):
            place = one * each + entry
            sums += jnp.where(list_ref[:, place : place + 1] == plane, 1.0, 0.0)
        base_ref[one] = jnp.where(sums > 0.0, jnp.log(sums) + jnp.log(prior_ref[:, one : one + 1]), -jnp.inf)
    noise = jnp.broadcast_to(noise_ref[...], (rows, rows))
    diagonal = lax.broadcasted_iota(jnp.int32, (rows, rows), 0) == lax.broadcasted_iota(
        jnp.int32, (rows, rows), 1
    )
    column = jnp.sum(jnp.where(diagonal, noise, 0.0), axis=1, keepdims=True)
    scale_ref[...] = jnp.broadcast_to(column, (rows, width))


def count_planes(slab, class_weight, inv_noise, orientations, width, slabs):
    rows, classes, each = orientations.shape
    vmem = pl.BlockSpec(memory_space=pltpu.VMEM)
    return pl.pallas_call(
        functools.partial(count_kernel, slabs),
        in_specs=[pl.BlockSpec(memory_space=pltpu.SMEM), vmem, vmem, vmem],
        out_specs=[vmem, vmem],
        out_shape=[
            jax.ShapeDtypeStruct((classes, rows, width), F32),
            jax.ShapeDtypeStruct((rows, width), F32),
        ],
        compiler_params=params(4),
        name="count",
    )(
        slab,
        class_weight.reshape(1, classes),
        inv_noise.reshape(1, rows),
        orientations.reshape(rows, classes * each),
    )


def weigh_kernel(base_ref, scale_ref, *refs):
    table_refs, (own_ref, both_ref) = refs[:-2], refs[-2:]
    classes = base_ref.shape[0]
    planes = own_ref.shape[0]
    local = planes // classes
    scores = []
    for one in range(classes):
        parts = [
            ref[:, start + one * local : start + (one + 1) * local]
            for ref in table_refs
            for start in range(0, ref.shape[1], planes)
        ]
        scores.append(base_ref[one] + scale_ref[...] * jnp.concatenate(parts, axis=1))
    peak = functools.reduce(jnp.maximum, [jnp.max(score, axis=1, keepdims=True) for score in scores])
    raw = [jnp.exp(score - peak) for score in scores]
    total = functools.reduce(jnp.add, [jnp.sum(part, axis=1, keepdims=True) for part in raw])
    slabs = [
        jnp.concatenate([part[:, place * local : (place + 1) * local] for part in raw], axis=1) / total
        for place in range(2)
    ]
    own_ref[...] = slabs[0].T
    both_ref[...] = jnp.concatenate(slabs, axis=1)


def weigh(base, scale, tables, planes):
    rows = base.shape[1]
    return pl.pallas_call(
        weigh_kernel,
        out_shape=[
            jax.ShapeDtypeStruct((planes, rows), F32),
            jax.ShapeDtypeStruct((rows, 2 * planes), F32),
        ],
        compiler_params=params(4),
        name="weigh",
    )(base, scale, *tables)


def gather_kernel(items, keep_hbm, got_hbm, out_ref, got, in_sem):
    number, rows2, wide = out_ref.shape
    rows = rows2 // 2
    incoming = []
    for place, (side, k) in enumerate(items):
        cut = slice((2 * k + side) * wide, (2 * k + side + 1) * wide)
        incoming.append([
            pltpu.make_async_copy(keep_hbm.at[:, cut], out_ref.at[place, :rows], in_sem.at[place, 0]),
            pltpu.make_async_copy(got_hbm.at[:, cut], got.at[place], in_sem.at[place, 1]),
        ])
        for copy in incoming[-1]:
            copy.start()
    for place in range(number):
        for copy in incoming[place]:
            copy.wait()
        out_ref[place, rows:] = got[place].astype(BF16)


def gather_images(items, keep, got, wide):
    rows = keep.shape[0]
    number = len(items)
    held = pl.BlockSpec(memory_space=pl.ANY)
    return pl.pallas_call(
        functools.partial(gather_kernel, items),
        in_specs=[held] * 2,
        out_specs=pl.BlockSpec(memory_space=pltpu.VMEM),
        out_shape=jax.ShapeDtypeStruct((number, 2 * rows, wide), BF16),
        scratch_shapes=[
            pltpu.VMEM((number, rows, wide), F32),
            pltpu.SemaphoreType.DMA((number, 2)),
        ],
        compiler_params=params(8),
        name="gather",
    )(keep, got)


def first_sums_kernel(items, own_w_ref, sib_w_ref, both_w_ref, image_ref, *outs):
    wide = image_ref.shape[2]
    weights = jnp.concatenate([own_w_ref[...], sib_w_ref[...]], axis=1).astype(BF16)
    slots = [0] * len(outs)
    for place, (side, _) in enumerate(items):
        out_ref, slot = outs[side], slots[side]
        slots[side] += 1
        out_ref[slot, :, :wide] = jnp.dot(weights, image_ref[place], preferred_element_type=F32)
        out_ref[slot, :, wide:] = both_w_ref[...]


def first_sums(items, own_w, sib_w, both_w, images):
    planes = own_w.shape[0]
    wide = images.shape[2]
    vmem = pl.BlockSpec(memory_space=pltpu.VMEM)
    return pl.pallas_call(
        functools.partial(first_sums_kernel, items),
        in_specs=[vmem] * 4,
        out_specs=[vmem] * 2,
        out_shape=[
            jax.ShapeDtypeStruct(
                (sum(side == one for side, _ in items), planes, wide + both_w.shape[1]), F32
            )
            for one in (0, 1)
        ],
        compiler_params=params(8),
        name="first_sums",
    )(own_w, sib_w, both_w, images)


def sums_kernel(items, own_w_ref, sib_w_ref, keep_hbm, got_hbm, *refs):
    outs = refs[: len(items)]
    keep, got, in_sem = refs[len(items) :]
    number, _, wide = keep.shape
    places = [(slot, k, side) for side, ks in enumerate(items) for slot, k in enumerate(ks)]
    incoming = []
    for place, (slot, k, side) in enumerate(places):
        source = slice((2 * k + side) * wide, (2 * k + side + 1) * wide)
        incoming.append([
            pltpu.make_async_copy(keep_hbm.at[:, source], keep.at[place], in_sem.at[place, 0]),
            pltpu.make_async_copy(got_hbm.at[:, source], got.at[place], in_sem.at[place, 1]),
        ])
        for copy in incoming[-1]:
            copy.start()
    weights = jnp.concatenate([own_w_ref[...], sib_w_ref[...]], axis=1).astype(BF16)
    for place, (slot, k, side) in enumerate(places):
        for copy in incoming[place]:
            copy.wait()
        images = jnp.concatenate([keep[place], got[place].astype(BF16)], axis=0)
        outs[side][slot] = jnp.dot(weights, images, preferred_element_type=F32)


def partial_sums(items, own_w, sib_w, keep, got, wide):
    rows = keep.shape[0]
    planes = own_w.shape[0]
    number = sum(len(ks) for ks in items)
    held = pl.BlockSpec(memory_space=pl.ANY)
    vmem = pl.BlockSpec(memory_space=pltpu.VMEM)
    return pl.pallas_call(
        functools.partial(sums_kernel, items),
        in_specs=[vmem] * 2 + [held] * 2,
        out_specs=[vmem] * 2,
        out_shape=[jax.ShapeDtypeStruct((len(ks), planes, wide), F32) for ks in items],
        scratch_shapes=[
            pltpu.VMEM((number, rows, wide), BF16),
            pltpu.VMEM((number, rows, wide), F32),
            pltpu.SemaphoreType.DMA((number, 2)),
        ],
        compiler_params=params(12),
        name="sums",
    )(own_w, sib_w, keep, got)


def meet_kernel(chips, ctf_ref, *refs):
    weight_refs, image_refs, outs = refs[:chips], refs[chips : 2 * chips], refs[2 * chips :]
    planes, width = outs[0].shape
    met = width - LANES
    weights, ctf = [], []
    for ref in weight_refs:
        wide = ref.shape[-1]
        part = ref[:, wide - planes :] if len(ref.shape) == 2 else ref[0, :, wide - planes :]
        weights.append(part.astype(BF16))
    weights = jnp.concatenate(weights, axis=0)

    def sums(parts):
        return lax.dot_general(
            weights,
            jnp.concatenate(parts, axis=0),
            (((0,), (0,)), ((), ())),
            preferred_element_type=F32,
        )

    ctf = [lanes_wide(ctf_ref[...])] + [ref[:, 2 * met :] for ref in image_refs[1:]]
    shells = sums([(part * part).astype(BF16) for part in ctf])
    for other, out_ref in enumerate(outs):
        cut = slice(other * met, (other + 1) * met)
        out_ref[:, :met] = sums([ref[:, cut].astype(BF16) for ref in image_refs])
        out_ref[:, met:] = shells


def meet(ctf_table, weights, images):
    met = images[0].shape[1] // 2
    planes = weights[0].shape[1]
    return pl.pallas_call(
        functools.partial(meet_kernel, len(weights)),
        out_shape=[jax.ShapeDtypeStruct((planes, met + LANES), F32)] * 2,
        compiler_params=params(16),
        name="meet",
    )(ctf_table, *weights, *images)


def finish_kernel(numbers, me_ref, slab_ref, index_hbm, met_ref, sib_met_ref, partner_ref, *refs):
    total = sum(numbers)
    parts, (out_hbm, index, out, in_sem, out_sem) = refs[:total], refs[total:]
    planes, share = out.shape
    wide, met = split_share(share)
    mine = pl.ds(pl.multiple_of(me_ref[0] * share, share), share)
    fetch = pltpu.make_async_copy(index_hbm.at[:, mine], index, in_sem)
    fetch.start()
    left, right = parts[: numbers[0]], parts[numbers[0] :]
    shells = met_ref[:planes, met:] + sib_met_ref[:planes, met:]
    half = lax.rem(slab_ref[0], 2)
    fetch.wait()

    def divide(block_of, place, size):
        for start in range(0, size, LANES):
            at = pl.ds(pl.multiple_of(place + start, LANES), LANES)
            weight = spread(shells, index[:, at])
            out[:, at] = block_of(slice(start, start + LANES)) / (weight + 1.0)

    def summed(sides):
        return lambda cut: functools.reduce(jnp.add, [ref[0, :, cut] for ref in sides])

    divide(lambda cut: met_ref[:planes, cut] + sib_met_ref[:planes, cut], 2 * wide + half * met, met)
    divide(lambda cut: partner_ref[:, cut], 2 * wide + (1 - half) * met, met)
    stores = []
    for step, work in enumerate((None, (left, 0), (right, 1))):
        cut = slice(2 * wide, share)
        if work is not None:
            sides, place = work
            divide(summed(sides), place * wide, wide)
            cut = slice(place * wide, (place + 1) * wide)
        stores.append(pltpu.make_async_copy(out.at[:, cut], out_hbm.at[:, cut], out_sem.at[step]))
        stores[-1].start()
    for store in stores:
        store.wait()


def finish(me, slab, index, met, sib_met, partner, left, right, share):
    planes = partner.shape[0]
    numbers = len(left), len(right)
    held = pl.BlockSpec(memory_space=pl.ANY)
    vmem = pl.BlockSpec(memory_space=pltpu.VMEM)

    def first(part, place):
        if part.shape[0] == 1:
            return vmem
        return pl.BlockSpec((1,) + part.shape[1:], lambda step: (place, 0, 0))

    return pl.pallas_call(
        functools.partial(finish_kernel, numbers),
        grid=(1,),
        in_specs=[pl.BlockSpec(memory_space=pltpu.SMEM)] * 2
        + [held, vmem, vmem, vmem]
        + [first(part, place) for part, place in left + right],
        out_specs=held,
        out_shape=jax.ShapeDtypeStruct((planes, share), F32),
        scratch_shapes=[
            pltpu.VMEM((1, share), jnp.int32),
            pltpu.VMEM((planes, share), F32),
            pltpu.SemaphoreType.DMA(()),
            pltpu.SemaphoreType.DMA((3,)),
        ],
        compiler_params=params(12),
        name="finish",
    )(me, slab, index, met, sib_met, partner, *[part for part, _ in left + right])


def swap(array, bit, size):
    return lax.ppermute(array, "img", [(one, one ^ bit) for one in range(size)])


def shards(images, references, orientations, ctf_table, inv_noise, class_weight):
    rows, width = images.shape
    classes, local_planes, _ = references.shape
    size = lax.axis_size("img")
    slabs = lax.axis_size("slab")
    chips = size // 2
    share = width // size
    wide, met_wide = split_share(share)
    me = lax.axis_index("img").astype(jnp.int32).reshape(1)
    slab = lax.axis_index("slab").astype(jnp.int32).reshape(1)
    index = entry_shells(width, ctf_table.shape[1])
    top_index = jnp.asarray(index[:, : width // 2 + 2 * math.isqrt(width // 2)])
    index = jnp.asarray(index)
    planes = references.reshape(classes * local_planes, width)

    beyond = tuple(k for k in range(chips) if k & (k - 1))
    near = tuple(k for k in range(chips) if k not in beyond)
    met_images = {}
    if beyond:
        early = early_images(me, slab, index, images, ctf_table, share, beyond)
        images, *early = lax.optimization_barrier((images, *early))
        met_images = {k: swap(part, 2 * k, size) for k, part in zip(beyond, early)}
    give, keep, table, *parts_near = estep(
        me, slab, top_index, images, planes, ctf_table, share, near
    )
    if beyond:
        give, keep, met_images[beyond[-1]], *parts_near = lax.optimization_barrier(
            (give, keep, met_images[beyond[-1]], *parts_near)
        )
    for k, part in zip(near, parts_near):
        met_images[k] = swap(part, 2 * k, size) if k else part
    keep, *met_images = far(keep, *[met_images[k] for k in range(chips)])
    base, scale = count_planes(
        slab, class_weight, inv_noise, orientations, slabs * local_planes, slabs
    )
    tables, bit = [table], 1
    while bit < slabs:
        held = tables[0]
        if len(tables) > 1:
            held = jnp.concatenate(tables, axis=1)
        pairs = [(one, one ^ bit) for one in range(slabs)]
        tables = [held, lax.ppermute(held, "slab", pairs)]
        bit *= 2
    got = swap(give, 1, size)
    own_w, both_w = weigh(base, scale, tables, classes * local_planes)
    sib_w = swap(own_w, 1, size)

    sums = functools.partial(
        partial_sums, own_w=own_w, sib_w=sib_w, keep=keep, got=got, wide=wide,
    )
    low = [1 << place for place in range(chips.bit_length() - 1)]
    orders = (low, low[::-1])
    first = [[k for k in range(chips) if k & order[0]] for order in orders]
    onward = [[k for k in ks if k & order[1]] for ks, order in zip(first, orders)]
    direct = [[k for k in ks if not k & order[1]] for ks, order in zip(first, orders)]
    stay = [[k for k in range(chips) if not k & order[0]] for order in orders]
    parts = [{k: [] for k in ks} for ks in stay]

    def deliver(side, ks, array, bit):
        arrived = swap(array, 2 * bit, size)
        for place, k in enumerate(ks):
            parts[side][k ^ bit].append((arrived, place))
        return arrived

    def compute(groups):
        return sums(tuple(tuple(ks) for ks in groups))

    items = tuple((side, k) for side, ks in enumerate(onward) for k in ks)
    sent = first_sums(items, own_w, sib_w, both_w, gather_images(items, keep, got, wide))
    far_w = {0: both_w}
    for side in (0, 1):
        bit = orders[side][0]
        far_w[bit] = deliver(side, onward[side], sent[side], bit)
    both_w, _ = lax.optimization_barrier((both_w, sent[1]))
    for k in range(1, chips):
        if k not in far_w:
            far_w[k] = swap(both_w, 2 * k, size)
    sums.keywords["keep"], *met_images = lax.optimization_barrier((keep, *met_images))
    sent = compute(direct)
    for side in (0, 1):
        deliver(side, direct[side], sent[side], orders[side][0])
    kept = compute(stay)
    for side in (0, 1):
        for place, k in enumerate(stay[side]):
            parts[side][k].append((kept[side], place))

    met_images[0], _ = lax.optimization_barrier((met_images[0], sent[0]))
    met, for_sib = meet(ctf_table, [far_w[k] for k in range(chips)], met_images)
    sib_met = swap(for_sib, 1, size)
    own_planes = classes * local_planes
    partner = lax.ppermute(
        met[own_planes:, :met_wide] + sib_met[own_planes:, :met_wide], "slab", [(one, one ^ 1) for one in range(slabs)]
    )

    for turn in range(1, len(low)):
        for side in (0, 1):
            bit = orders[side][turn]
            ks = [k for k in parts[side] if k & bit]
            sent = jnp.stack(
                [sum(part[place, :, :wide] for part, place in parts[side].pop(k)) for k in ks]
            )
            deliver(side, ks, sent, bit)
    out = finish(me, slab, index, met, sib_met, partner, parts[0][0], parts[1][0], share)
    return out.reshape(classes, local_planes, share)


def solution(mesh):
    return jax.shard_map(
        shards,
        mesh=mesh,
        in_specs=(
            P("img", None),
            P(None, "slab", None),
            P("img", None, None),
            P("img", None),
            P("img"),
            P(),
        ),
        out_specs=P(None, "slab", "img"),
        check_vma=False,
    )
```

```python
import functools
import math

import jax
import jax.numpy as jnp
import numpy as np
from jax import lax
from jax.experimental import pallas as pl
from jax.experimental.pallas import tpu as pltpu
from jax.sharding import PartitionSpec as P

F32 = jnp.float32
BF16 = jnp.bfloat16
LANES = 128
MIB = 1024 * 1024


def entry_shells(width, shells):
    pixels = width // 2
    box = math.isqrt(pixels)
    place = np.arange(pixels)
    column = place % box - box // 2
    row = place // box - box // 2
    radius = column * column + row * row
    levels = np.arange(1, shells)
    shell = np.sum(2 * levels[None, :] ** 2 <= radius[:, None], axis=1)
    return np.repeat(shell, 2).astype(np.int32)[None, :]


def split_share(share):
    met = max(LANES, 6 * share // 32 // LANES * LANES)
    return share // 2 - met, met


def met_column(share, owner, slab):
    wide, met = split_share(share)
    return pl.multiple_of(owner * share + 2 * wide + lax.rem(slab, 2) * met, LANES)


def params(mib):
    return pltpu.CompilerParams(vmem_limit_bytes=mib * MIB)


def lanes_wide(table):
    rows, shells = table.shape
    if shells == LANES:
        return table
    return jnp.concatenate([table, jnp.zeros((rows, LANES - shells), table.dtype)], axis=1)


def spread(table, index):
    return jnp.take_along_axis(table, jnp.broadcast_to(index, table.shape), axis=1)


def contract_last(left, right):
    return lax.dot_general(left, right, (((1,), (1,)), ((), ())), preferred_element_type=F32)


def estep_kernel(
    blocks, share, near, index_hbm, image_hbm, plane_hbm, ctf_hbm, *refs,
):
    give_hbm, keep_hbm, score_ref = refs[:3]
    near_refs = refs[3 : 3 + len(near)]
    index, image, plane, ctf_held, weighted, give, squared, energy_of = refs[-11:-3]
    small_sem, in_sem, out_sem = refs[-3:]
    rows, width = image.shape
    wide, met = split_share(share)
    chips, summed = width // share // 2, 2 * wide
    box = math.isqrt(width // 2)
    line = 2 * box
    deep = box // (2 * blocks)
    span = deep * line

    small = [
        pltpu.make_async_copy(index_hbm, index, small_sem.at[0]),
        pltpu.make_async_copy(ctf_hbm, ctf_held, small_sem.at[1]),
    ]
    incoming = []
    for block in range(blocks):
        copies = []
        for side, start in enumerate((block * span, width - (block + 1) * span)):
            cut = pl.ds(start, span)
            copies += [
                pltpu.make_async_copy(
                    image_hbm.at[:, cut], image.at[:, cut], in_sem.at[block, side, 0]
                ),
                pltpu.make_async_copy(
                    plane_hbm.at[:, cut], plane.at[:, cut], in_sem.at[block, side, 1]
                ),
            ]
        incoming.append(copies)
    for copy in small + [copy for copies in incoming for copy in copies]:
        copy.start()
    for copy in small:
        copy.wait()
    table = lanes_wide(ctf_held[...])

    def weigh_image(cut, ctf):
        weighted[:, cut] = (image[:, cut].astype(F32) * ctf).astype(BF16)

    def square(cut):
        part = plane[:, cut].astype(F32)
        return part * part

    def expand(row, slot, place):
        mirror = box - row if 0 < row < box // 2 else None
        for start in range(0, line, LANES):
            cut = slice(row * line + start, row * line + start + LANES)
            ctf = spread(table, index[:, cut])
            weigh_image(cut, ctf)
            power = square(cut)
            if mirror is not None:
                other = slice(mirror * line + start, mirror * line + start + LANES)
                weigh_image(other, ctf)
                power += square(other)
            held = slice(place + start, place + start + LANES)
            squared[slot, :, held] = (ctf * ctf).astype(BF16)
            energy_of[slot, :, held] = power.astype(BF16)

    def fit(start, stop):
        return contract_last(weighted[:, start:stop], plane[:, start:stop])

    def energy(slot, size):
        return contract_last(squared[slot, :, :size], energy_of[slot, :, :size])

    def block_table(block):
        low, high = fit(block * span, (block + 1) * span), width - block * span
        stop = high + line if block else high
        low += fit(high - span + line, stop)
        return 2.0 * low - energy(block % 2, span)

    chip, core = lax.axis_index("img") // 2, lax.rem(lax.axis_index("img"), 2)
    outgoing = []

    def hand_over(done):
        for pair in range(chips):
            first, last = 2 * pair * share // line, -(-2 * (pair + 1) * share // line)
            if pair in handed or not all(row in done for row in range(first, last)):
                continue
            handed.add(pair)
            place = pair ^ chip
            given = pl.ds(pl.multiple_of((2 * pair + 1 - core) * share, share), summed)
            kept = pl.ds(pl.multiple_of((2 * pair + core) * share, share), summed)
            at = pl.ds(pl.multiple_of(place * summed, LANES), summed)
            give[:, at] = weighted[:, given].astype(F32)
            outgoing.extend([
                pltpu.make_async_copy(give.at[:, at], give_hbm.at[:, at], out_sem.at[pair, 0]),
                pltpu.make_async_copy(weighted.at[:, kept], keep_hbm.at[:, at], out_sem.at[pair, 1]),
            ])
            outgoing[-2].start()
            outgoing[-1].start()

    handed, done = set(), set()
    total = jnp.zeros(score_ref.shape, F32)
    for block in range(blocks):
        for copy in incoming[block]:
            copy.wait()
        for row in range(block * deep, (block + 1) * deep):
            expand(row, block % 2, (row - block * deep) * line)
            done |= {row, box - row}
        if block == blocks - 1:
            expand(box // 2, 2, 0)
            done.add(box // 2)
        if block:
            total += block_table(block - 1)
        hand_over(done)
    total += block_table(blocks - 1)
    middle = width // 2
    total += 2.0 * fit(middle, middle + line) - energy(2, line)
    score_ref[...] = total
    for k, near_ref in zip(near, near_refs):
        for other in range(2):
            owner = (k ^ chip) * 2 + lax.rem(core + other, 2)
            part = weighted[:, pl.ds(met_column(share, owner, lax.axis_index("slab")), met)]
            near_ref[:, other * met : (other + 1) * met] = part.astype(near_ref.dtype)
        if k:
            near_ref[:, 2 * met :] = table
    for copy in outgoing:
        copy.wait()


def far(*operands):
    return [pltpu.with_memory_space_constraint(operand, pltpu.HBM) for operand in operands]


def estep(index, images, planes, ctf_table, share, near):
    rows, width = images.shape
    chips = width // share // 2
    wide, met = split_share(share)
    summed = 2 * wide
    count = planes.shape[0]
    blocks = 4
    span = width // (2 * blocks)
    held = pl.BlockSpec(memory_space=pl.ANY)
    vmem = pl.BlockSpec(memory_space=pltpu.VMEM)
    hbm = pl.BlockSpec(memory_space=pltpu.HBM)
    return pl.pallas_call(
        functools.partial(estep_kernel, blocks, share, near),
        in_specs=[hbm] * 4,
        out_specs=[held, held] + [vmem] * (1 + len(near)),
        out_shape=[
            jax.ShapeDtypeStruct((rows, chips * summed), F32),
            pltpu.HBM((rows, chips * summed), BF16),
            jax.ShapeDtypeStruct((rows, count), F32),
        ]
        + [
            jax.ShapeDtypeStruct((rows, 2 * met + LANES), F32)
            if k
            else pltpu.HBM((rows, 2 * met), BF16)
            for k in near
        ],
        scratch_shapes=[
            pltpu.VMEM(index.shape, jnp.int32),
            pltpu.VMEM((rows, width), BF16),
            pltpu.VMEM((count, width), BF16),
            pltpu.VMEM(ctf_table.shape, F32),
            pltpu.VMEM((rows, width), BF16),
            pltpu.VMEM((rows, chips * summed), F32),
            pltpu.VMEM((3, rows, span), BF16),
            pltpu.VMEM((3, count, span), BF16),
            pltpu.SemaphoreType.DMA((2,)),
            pltpu.SemaphoreType.DMA((blocks, 2, 2)),
            pltpu.SemaphoreType.DMA((chips, 2)),
        ],
        compiler_params=params(28),
        name="estep",
    )(*far(index, images, planes, ctf_table))


def early_kernel(share, beyond, index_hbm, image_hbm, ctf_hbm, *refs):
    outs = refs[: len(beyond)]
    index, image, ctf_held, index_sem, image_sem, ctf_sem = refs[len(beyond) :]
    met = split_share(share)[1]
    chip, core = lax.axis_index("img") // 2, lax.rem(lax.axis_index("img"), 2)
    fetch = pltpu.make_async_copy(ctf_hbm, ctf_held, ctf_sem)
    fetch.start()
    copies = []
    for place, k in enumerate(beyond):
        for other in range(2):
            owner = (k ^ chip) * 2 + lax.rem(core + other, 2)
            cut = pl.ds(met_column(share, owner, lax.axis_index("slab")), met)
            copies.append([
                pltpu.make_async_copy(
                    index_hbm.at[:, cut], index.at[place, other], index_sem.at[place, other]
                ),
                pltpu.make_async_copy(
                    image_hbm.at[:, cut], image.at[place, other], image_sem.at[place, other]
                ),
            ])
            for copy in copies[-1]:
                copy.start()
    fetch.wait()
    table = lanes_wide(ctf_held[...])
    for place, out_ref in enumerate(outs):
        for other in range(2):
            for copy in copies[2 * place + other]:
                copy.wait()
            for start in range(0, met, LANES):
                cut = slice(start, start + LANES)
                ctf = spread(table, index[place, other, :, cut])
                part = (image[place, other, :, cut].astype(F32) * ctf).astype(BF16)
                out_ref[:, other * met + start : other * met + start + LANES] = part.astype(F32)
        out_ref[:, 2 * met :] = table


def early_images(index, images, ctf_table, share, beyond):
    rows = images.shape[0]
    met = split_share(share)[1]
    number = len(beyond)
    vmem = pl.BlockSpec(memory_space=pltpu.VMEM)
    hbm = pl.BlockSpec(memory_space=pltpu.HBM)
    return pl.pallas_call(
        functools.partial(early_kernel, share, beyond),
        in_specs=[hbm, hbm, hbm],
        out_specs=[vmem] * number,
        out_shape=[jax.ShapeDtypeStruct((rows, 2 * met + LANES), F32)] * number,
        scratch_shapes=[
            pltpu.VMEM((number, 2, 1, met), jnp.int32),
            pltpu.VMEM((number, 2, rows, met), BF16),
            pltpu.VMEM(ctf_table.shape, F32),
            pltpu.SemaphoreType.DMA((number, 2)),
            pltpu.SemaphoreType.DMA((number, 2)),
            pltpu.SemaphoreType.DMA(()),
        ],
        compiler_params=params(12),
        name="early",
    )(*far(index, images, ctf_table))


def count_kernel(slabs, prior_ref, noise_ref, list_ref, base_ref, scale_ref):
    rows, listed = list_ref.shape
    classes, _, width = base_ref.shape
    each = listed // classes
    local = width // slabs
    lane = lax.broadcasted_iota(jnp.int32, (rows, width), 1)
    home = lax.axis_index("slab") ^ (lane // local)
    plane = home * local + lax.rem(lane, local)
    for one in range(classes):
        sums = jnp.zeros((rows, width), F32)
        for entry in range(each):
            place = one * each + entry
            sums += jnp.where(list_ref[:, place : place + 1] == plane, 1.0, 0.0)
        base_ref[one] = jnp.where(sums > 0.0, jnp.log(sums) + jnp.log(prior_ref[:, one : one + 1]), -jnp.inf)
    noise = jnp.broadcast_to(noise_ref[...], (rows, rows))
    diagonal = lax.broadcasted_iota(jnp.int32, (rows, rows), 0) == lax.broadcasted_iota(
        jnp.int32, (rows, rows), 1
    )
    column = jnp.sum(jnp.where(diagonal, noise, 0.0), axis=1, keepdims=True)
    scale_ref[...] = jnp.broadcast_to(column, (rows, width))


def count_planes(class_weight, inv_noise, orientations, width, slabs):
    rows, classes, each = orientations.shape
    vmem = pl.BlockSpec(memory_space=pltpu.VMEM)
    return pl.pallas_call(
        functools.partial(count_kernel, slabs),
        in_specs=[vmem] * 3,
        out_specs=[vmem, vmem],
        out_shape=[
            jax.ShapeDtypeStruct((classes, rows, width), F32),
            jax.ShapeDtypeStruct((rows, width), F32),
        ],
        compiler_params=params(4),
        name="count",
    )(
        class_weight.reshape(1, classes),
        inv_noise.reshape(1, rows),
        orientations.reshape(rows, classes * each),
    )


def weigh_kernel(base_ref, scale_ref, *refs):
    table_refs, (own_ref, both_ref) = refs[:-2], refs[-2:]
    classes = base_ref.shape[0]
    planes = own_ref.shape[0]
    local = planes // classes
    scores = []
    for one in range(classes):
        parts = [
            ref[:, start + one * local : start + (one + 1) * local]
            for ref in table_refs
            for start in range(0, ref.shape[1], planes)
        ]
        scores.append(base_ref[one] + scale_ref[...] * jnp.concatenate(parts, axis=1))
    peak = functools.reduce(jnp.maximum, [jnp.max(score, axis=1, keepdims=True) for score in scores])
    raw = [jnp.exp(score - peak) for score in scores]
    total = functools.reduce(jnp.add, [jnp.sum(part, axis=1, keepdims=True) for part in raw])
    slabs = [
        jnp.concatenate([part[:, place * local : (place + 1) * local] for part in raw], axis=1) / total
        for place in range(2)
    ]
    own_ref[...] = slabs[0].T
    both_ref[...] = jnp.concatenate(slabs, axis=1)


def weigh(base, scale, tables, planes):
    rows = base.shape[1]
    return pl.pallas_call(
        weigh_kernel,
        out_shape=[
            jax.ShapeDtypeStruct((planes, rows), F32),
            jax.ShapeDtypeStruct((rows, 2 * planes), F32),
        ],
        compiler_params=params(4),
        name="weigh",
    )(base, scale, *tables)


def gather_kernel(items, keep_hbm, got_hbm, out_ref, got, in_sem):
    number, rows2, wide = out_ref.shape
    rows = rows2 // 2
    incoming = []
    for place, (side, k) in enumerate(items):
        cut = slice((2 * k + side) * wide, (2 * k + side + 1) * wide)
        incoming.append([
            pltpu.make_async_copy(keep_hbm.at[:, cut], out_ref.at[place, :rows], in_sem.at[place, 0]),
            pltpu.make_async_copy(got_hbm.at[:, cut], got.at[place], in_sem.at[place, 1]),
        ])
        for copy in incoming[-1]:
            copy.start()
    for place in range(number):
        for copy in incoming[place]:
            copy.wait()
        out_ref[place, rows:] = got[place].astype(BF16)


def gather_images(items, keep, got, wide):
    rows = keep.shape[0]
    number = len(items)
    held = pl.BlockSpec(memory_space=pl.ANY)
    return pl.pallas_call(
        functools.partial(gather_kernel, items),
        in_specs=[held] * 2,
        out_specs=pl.BlockSpec(memory_space=pltpu.VMEM),
        out_shape=jax.ShapeDtypeStruct((number, 2 * rows, wide), BF16),
        scratch_shapes=[
            pltpu.VMEM((number, rows, wide), F32),
            pltpu.SemaphoreType.DMA((number, 2)),
        ],
        compiler_params=params(8),
        name="gather",
    )(keep, got)


def first_sums_kernel(items, own_w_ref, sib_w_ref, both_w_ref, image_ref, *outs):
    wide = image_ref.shape[2]
    weights = jnp.concatenate([own_w_ref[...], sib_w_ref[...]], axis=1).astype(BF16)
    slots = [0] * len(outs)
    for place, (side, _) in enumerate(items):
        out_ref, slot = outs[side], slots[side]
        slots[side] += 1
        out_ref[slot, :, :wide] = jnp.dot(weights, image_ref[place], preferred_element_type=F32)
        out_ref[slot, :, wide:] = both_w_ref[...]


def first_sums(items, own_w, sib_w, both_w, images):
    planes = own_w.shape[0]
    wide = images.shape[2]
    vmem = pl.BlockSpec(memory_space=pltpu.VMEM)
    return pl.pallas_call(
        functools.partial(first_sums_kernel, items),
        in_specs=[vmem] * 4,
        out_specs=[vmem] * 2,
        out_shape=[
            jax.ShapeDtypeStruct(
                (sum(side == one for side, _ in items), planes, wide + both_w.shape[1]), F32
            )
            for one in (0, 1)
        ],
        compiler_params=params(8),
        name="first_sums",
    )(own_w, sib_w, both_w, images)


def sums_kernel(items, own_w_ref, sib_w_ref, keep_hbm, got_hbm, *refs):
    outs = refs[: len(items)]
    keep, got, in_sem = refs[len(items) :]
    number, _, wide = keep.shape
    places = [(slot, k, side) for side, ks in enumerate(items) for slot, k in enumerate(ks)]
    incoming = []
    for place, (slot, k, side) in enumerate(places):
        source = slice((2 * k + side) * wide, (2 * k + side + 1) * wide)
        incoming.append([
            pltpu.make_async_copy(keep_hbm.at[:, source], keep.at[place], in_sem.at[place, 0]),
            pltpu.make_async_copy(got_hbm.at[:, source], got.at[place], in_sem.at[place, 1]),
        ])
        for copy in incoming[-1]:
            copy.start()
    weights = jnp.concatenate([own_w_ref[...], sib_w_ref[...]], axis=1).astype(BF16)
    for place, (slot, k, side) in enumerate(places):
        for copy in incoming[place]:
            copy.wait()
        images = jnp.concatenate([keep[place], got[place].astype(BF16)], axis=0)
        outs[side][slot] = jnp.dot(weights, images, preferred_element_type=F32)


def partial_sums(items, own_w, sib_w, keep, got, wide):
    rows = keep.shape[0]
    planes = own_w.shape[0]
    number = sum(len(ks) for ks in items)
    held = pl.BlockSpec(memory_space=pl.ANY)
    vmem = pl.BlockSpec(memory_space=pltpu.VMEM)
    return pl.pallas_call(
        functools.partial(sums_kernel, items),
        in_specs=[vmem] * 2 + [held] * 2,
        out_specs=[vmem] * 2,
        out_shape=[jax.ShapeDtypeStruct((len(ks), planes, wide), F32) for ks in items],
        scratch_shapes=[
            pltpu.VMEM((number, rows, wide), BF16),
            pltpu.VMEM((number, rows, wide), F32),
            pltpu.SemaphoreType.DMA((number, 2)),
        ],
        compiler_params=params(12),
        name="sums",
    )(own_w, sib_w, keep, got)


def meet_kernel(chips, ctf_ref, *refs):
    weight_refs, image_refs, outs = refs[:chips], refs[chips : 2 * chips], refs[2 * chips :]
    planes, width = outs[0].shape
    met = width - LANES
    weights, ctf = [], []
    for ref in weight_refs:
        wide = ref.shape[-1]
        part = ref[:, wide - planes :] if len(ref.shape) == 2 else ref[0, :, wide - planes :]
        weights.append(part.astype(BF16))
    weights = jnp.concatenate(weights, axis=0)

    def sums(parts):
        return lax.dot_general(
            weights,
            jnp.concatenate(parts, axis=0),
            (((0,), (0,)), ((), ())),
            preferred_element_type=F32,
        )

    ctf = [lanes_wide(ctf_ref[...])] + [ref[:, 2 * met :] for ref in image_refs[1:]]
    shells = sums([(part * part).astype(BF16) for part in ctf])
    for other, out_ref in enumerate(outs):
        cut = slice(other * met, (other + 1) * met)
        out_ref[:, :met] = sums([ref[:, cut].astype(BF16) for ref in image_refs])
        out_ref[:, met:] = shells


def meet(ctf_table, weights, images):
    met = images[0].shape[1] // 2
    planes = weights[0].shape[1]
    return pl.pallas_call(
        functools.partial(meet_kernel, len(weights)),
        out_shape=[jax.ShapeDtypeStruct((planes, met + LANES), F32)] * 2,
        compiler_params=params(16),
        name="meet",
    )(ctf_table, *weights, *images)


def prepare_kernel(places, index_hbm, met_ref, sib_met_ref, *refs):
    total = sum(map(len, places))
    parts, (base_ref, scale_ref, index, in_sem) = refs[:total], refs[total:]
    planes, share = base_ref.shape
    wide, met = split_share(share)
    mine = pl.ds(pl.multiple_of(lax.axis_index("img") * share, share), share)
    fetch = pltpu.make_async_copy(index_hbm.at[:, mine], index, in_sem)
    fetch.start()
    start = 0
    for side, numbers in enumerate(places):
        refs = list(zip(parts[start : start + len(numbers)], numbers))
        start += len(numbers)
        base_ref[:, side * wide : (side + 1) * wide] = functools.reduce(
            jnp.add, [ref[place] for ref, place in refs]
        )
    half = lax.rem(lax.axis_index("slab"), 2)
    own = pl.ds(pl.multiple_of(2 * wide + half * met, LANES), met)
    other = pl.ds(pl.multiple_of(2 * wide + (1 - half) * met, LANES), met)
    base_ref[:, own] = met_ref[:planes, :met] + sib_met_ref[:planes, :met]
    base_ref[:, other] = jnp.zeros((planes, met), F32)
    shells = met_ref[:planes, met:] + sib_met_ref[:planes, met:]
    fetch.wait()
    for start in range(0, share, LANES):
        cut = slice(start, start + LANES)
        scale_ref[:, cut] = 1.0 / (spread(shells, index[:, cut]) + 1.0)


def prepare(index, met, sib_met, sides, share):
    planes = met.shape[0] // 2
    held = pl.BlockSpec(memory_space=pl.ANY)
    vmem = pl.BlockSpec(memory_space=pltpu.VMEM)
    places = [[place for _, place in side] for side in sides]
    parts = [part for side in sides for part, _ in side]
    return pl.pallas_call(
        functools.partial(prepare_kernel, places),
        in_specs=[held] + [vmem] * (2 + len(parts)),
        out_specs=[vmem, vmem],
        out_shape=[jax.ShapeDtypeStruct((planes, share), F32)] * 2,
        scratch_shapes=[pltpu.VMEM((1, share), jnp.int32), pltpu.SemaphoreType.DMA(())],
        compiler_params=params(8),
        name="prepare",
    )(index, met, sib_met, *parts)


def finish_kernel(base_ref, scale_ref, left_ref, right_ref, partner_ref, out_hbm, out, out_sem):
    planes, share = out.shape
    wide, met = split_share(share)
    half = lax.rem(lax.axis_index("slab"), 2)
    own = pl.multiple_of(2 * wide + half * met, LANES)
    other = pl.multiple_of(2 * wide + (1 - half) * met, LANES)

    def scaled(place, size, last=None):
        for start in range(0, size, LANES):
            at = pl.ds(pl.multiple_of(place + start, LANES), LANES)
            value = base_ref[:, at]
            if last is not None:
                value += last(slice(start, start + LANES))
            out[:, at] = value * scale_ref[:, at]

    stores = []

    def store(start, stop):
        cut = slice(start, stop)
        stores.append(
            pltpu.make_async_copy(out.at[:, cut], out_hbm.at[:, cut], out_sem.at[len(stores)])
        )
        stores[-1].start()

    scaled(own, met)
    scaled(other, met, lambda cut: partner_ref[:, cut])
    store(2 * wide, share)
    scaled(0, wide, lambda cut: left_ref[0, :, cut])
    store(0, wide)
    scaled(wide, wide, lambda cut: right_ref[0, :, cut])
    store(wide, 2 * wide)
    for copy in stores:
        copy.wait()


def finish(base, scale, left, right, partner):
    vmem = pl.BlockSpec(memory_space=pltpu.VMEM)
    return pl.pallas_call(
        finish_kernel,
        in_specs=[vmem] * 5,
        out_specs=pl.BlockSpec(memory_space=pl.ANY),
        out_shape=jax.ShapeDtypeStruct(base.shape, F32),
        scratch_shapes=[pltpu.VMEM(base.shape, F32), pltpu.SemaphoreType.DMA((3,))],
        compiler_params=params(8),
        name="finish",
    )(base, scale, left, right, partner)


def swap(array, bit, size):
    return lax.ppermute(array, "img", [(one, one ^ bit) for one in range(size)])


def shards(images, references, orientations, ctf_table, inv_noise, class_weight):
    rows, width = images.shape
    classes, local_planes, _ = references.shape
    size = lax.axis_size("img")
    slabs = lax.axis_size("slab")
    chips = size // 2
    share = width // size
    wide, met_wide = split_share(share)
    index = entry_shells(width, ctf_table.shape[1])
    top_index = jnp.asarray(index[:, : width // 2 + 2 * math.isqrt(width // 2)])
    index = jnp.asarray(index)
    planes = references.reshape(classes * local_planes, width)

    beyond = tuple(k for k in range(chips) if k & (k - 1))
    near = tuple(k for k in range(chips) if k not in beyond)
    met_images = {}
    if beyond:
        early = early_images(index, images, ctf_table, share, beyond)
        images, *early = lax.optimization_barrier((images, *early))
        met_images = {k: swap(part, 2 * k, size) for k, part in zip(beyond, early)}
    give, keep, table, *parts_near = estep(
        top_index, images, planes, ctf_table, share, near
    )
    if beyond:
        give, keep, met_images[beyond[-1]], *parts_near = lax.optimization_barrier(
            (give, keep, met_images[beyond[-1]], *parts_near)
        )
    for k, part in zip(near, parts_near):
        met_images[k] = swap(part, 2 * k, size) if k else part
    keep, *met_images = far(keep, *[met_images[k] for k in range(chips)])
    base, scale = count_planes(
        class_weight, inv_noise, orientations, slabs * local_planes, slabs
    )
    tables, bit = [table], 1
    while bit < slabs:
        held = tables[0]
        if len(tables) > 1:
            held = jnp.concatenate(tables, axis=1)
        pairs = [(one, one ^ bit) for one in range(slabs)]
        tables = [held, lax.ppermute(held, "slab", pairs)]
        bit *= 2
    got = swap(give, 1, size)
    own_w, both_w = weigh(base, scale, tables, classes * local_planes)
    sib_w = swap(own_w, 1, size)

    sums = functools.partial(
        partial_sums, own_w=own_w, sib_w=sib_w, keep=keep, got=got, wide=wide,
    )
    low = [1 << place for place in range(chips.bit_length() - 1)]
    orders = (low, low[::-1])
    first = [[k for k in range(chips) if k & order[0]] for order in orders]
    onward = [[k for k in ks if k & order[1]] for ks, order in zip(first, orders)]
    direct = [[k for k in ks if not k & order[1]] for ks, order in zip(first, orders)]
    stay = [[k for k in range(chips) if not k & order[0]] for order in orders]
    parts = [{k: [] for k in ks} for ks in stay]

    def deliver(side, ks, array, bit):
        arrived = swap(array, 2 * bit, size)
        for place, k in enumerate(ks):
            parts[side][k ^ bit].append((arrived, place))
        return arrived

    def compute(groups):
        return sums(tuple(tuple(ks) for ks in groups))

    items = tuple((side, k) for side, ks in enumerate(onward) for k in ks)
    sent = first_sums(items, own_w, sib_w, both_w, gather_images(items, keep, got, wide))
    arrived = [swap(sent[side], 2 * orders[side][0], size) for side in (0, 1)]
    both_w, _ = lax.optimization_barrier((both_w, sent[1]))
    others = [k for k in range(1, chips) if k not in (orders[0][0], orders[1][0])]
    far_w = [swap(both_w, 2 * k, size) for k in others]
    sums.keywords["keep"], *met_images = lax.optimization_barrier((keep, *met_images))
    sent = compute(direct)
    for side in (0, 1):
        deliver(side, direct[side], sent[side], orders[side][0])
    kept = compute(stay)
    for side in (0, 1):
        for place, k in enumerate(stay[side]):
            parts[side][k].append((kept[side], place))

    met_images[0], _, *arrived = lax.optimization_barrier(
        (met_images[0], sent[0], *arrived, *far_w)
    )
    far_w = dict(zip(others, arrived[2:]))
    far_w[0] = both_w
    for side in (0, 1):
        bit = orders[side][0]
        far_w[bit] = arrived[side]
        for place, k in enumerate(onward[side]):
            parts[side][k ^ bit].append((arrived[side], place))
    met, for_sib = meet(ctf_table, [far_w[k] for k in range(chips)], met_images)
    sib_met = swap(for_sib, 1, size)
    own_planes = classes * local_planes
    partner = lax.ppermute(
        met[own_planes:, :met_wide] + sib_met[own_planes:, :met_wide], "slab", [(one, one ^ 1) for one in range(slabs)]
    )

    for turn in range(1, len(low)):
        for side in (0, 1):
            bit = orders[side][turn]
            ks = [k for k in parts[side] if k & bit]
            sent = jnp.stack(
                [sum(part[place, :, :wide] for part, place in parts[side].pop(k)) for k in ks]
            )
            deliver(side, ks, sent, bit)
    base, scale = prepare(
        index, met, sib_met, [parts[side][0][:-1] for side in (0, 1)], share
    )
    out = finish(base, scale, parts[0][0][-1][0], parts[1][0][-1][0], partner)
    return out.reshape(classes, local_planes, share)


def solution(mesh):
    return jax.shard_map(
        shards,
        mesh=mesh,
        in_specs=(
            P("img", None),
            P(None, "slab", None),
            P("img", None, None),
            P("img", None),
            P("img"),
            P(),
        ),
        out_specs=P(None, "slab", "img"),
        check_vma=False,
    )
```

```python
import functools
import math

import jax
import jax.numpy as jnp
import numpy as np
from jax import lax
from jax.experimental import pallas as pl
from jax.experimental.pallas import tpu as pltpu
from jax.sharding import PartitionSpec as P

F32 = jnp.float32
BF16 = jnp.bfloat16
LANES = 128
MIB = 1024 * 1024


def entry_shells(width, shells):
    pixels = width // 2
    box = math.isqrt(pixels)
    place = np.arange(pixels)
    column = place % box - box // 2
    row = place // box - box // 2
    radius = column * column + row * row
    levels = np.arange(1, shells)
    shell = np.sum(2 * levels[None, :] ** 2 <= radius[:, None], axis=1)
    return np.repeat(shell, 2).astype(np.int32)[None, :]


def split_share(share):
    met = max(LANES, 6 * share // 32 // LANES * LANES)
    return share // 2 - met, met


def met_column(share, owner, slab):
    wide, met = split_share(share)
    return pl.multiple_of(owner * share + 2 * wide + lax.rem(slab, 2) * met, LANES)


def params(mib):
    return pltpu.CompilerParams(vmem_limit_bytes=mib * MIB)


def lanes_wide(table):
    rows, shells = table.shape
    if shells == LANES:
        return table
    return jnp.concatenate([table, jnp.zeros((rows, LANES - shells), table.dtype)], axis=1)


def spread(table, index):
    return jnp.take_along_axis(table, jnp.broadcast_to(index, table.shape), axis=1)


def contract_last(left, right):
    return lax.dot_general(left, right, (((1,), (1,)), ((), ())), preferred_element_type=F32)


def estep_kernel(
    blocks, share, near, index_hbm, image_hbm, plane_hbm, ctf_hbm, *refs,
):
    give_hbm, keep_hbm, score_ref = refs[:3]
    near_refs = refs[3 : 3 + len(near)]
    index, image, plane, ctf_held, weighted, give, squared, energy_of = refs[-11:-3]
    small_sem, in_sem, out_sem = refs[-3:]
    rows, width = image.shape
    wide, met = split_share(share)
    chips, summed = width // share // 2, 2 * wide
    box = math.isqrt(width // 2)
    line = 2 * box
    deep = box // (2 * blocks)
    span = deep * line

    small = [
        pltpu.make_async_copy(index_hbm, index, small_sem.at[0]),
        pltpu.make_async_copy(ctf_hbm, ctf_held, small_sem.at[1]),
    ]
    incoming = []
    for block in range(blocks):
        copies = []
        for side, start in enumerate((block * span, width - (block + 1) * span)):
            cut = pl.ds(start, span)
            copies += [
                pltpu.make_async_copy(
                    image_hbm.at[:, cut], image.at[:, cut], in_sem.at[block, side, 0]
                ),
                pltpu.make_async_copy(
                    plane_hbm.at[:, cut], plane.at[:, cut], in_sem.at[block, side, 1]
                ),
            ]
        incoming.append(copies)
    for copy in small + [copy for copies in incoming for copy in copies]:
        copy.start()
    for copy in small:
        copy.wait()
    table = lanes_wide(ctf_held[...])

    def weigh_image(cut, ctf):
        weighted[:, cut] = (image[:, cut].astype(F32) * ctf).astype(BF16)

    def square(cut):
        part = plane[:, cut].astype(F32)
        return part * part

    def expand(row, slot, place):
        mirror = box - row if 0 < row < box // 2 else None
        for start in range(0, line, LANES):
            cut = slice(row * line + start, row * line + start + LANES)
            ctf = spread(table, index[:, cut])
            weigh_image(cut, ctf)
            power = square(cut)
            if mirror is not None:
                other = slice(mirror * line + start, mirror * line + start + LANES)
                weigh_image(other, ctf)
                power += square(other)
            held = slice(place + start, place + start + LANES)
            squared[slot, :, held] = (ctf * ctf).astype(BF16)
            energy_of[slot, :, held] = power.astype(BF16)

    def fit(start, stop):
        return contract_last(weighted[:, start:stop], plane[:, start:stop])

    def energy(slot, size):
        return contract_last(squared[slot, :, :size], energy_of[slot, :, :size])

    def block_table(block):
        low, high = fit(block * span, (block + 1) * span), width - block * span
        stop = high + line if block else high
        low += fit(high - span + line, stop)
        return 2.0 * low - energy(block % 2, span)

    chip, core = lax.axis_index("img") // 2, lax.rem(lax.axis_index("img"), 2)
    outgoing = []

    def hand_over(done):
        for pair in range(chips):
            first, last = 2 * pair * share // line, -(-2 * (pair + 1) * share // line)
            if pair in handed or not all(row in done for row in range(first, last)):
                continue
            handed.add(pair)
            place = pair ^ chip
            given = pl.ds(pl.multiple_of((2 * pair + 1 - core) * share, share), summed)
            kept = pl.ds(pl.multiple_of((2 * pair + core) * share, share), summed)
            at = pl.ds(pl.multiple_of(place * summed, LANES), summed)
            give[:, at] = weighted[:, given].astype(F32)
            outgoing.extend([
                pltpu.make_async_copy(give.at[:, at], give_hbm.at[:, at], out_sem.at[pair, 0]),
                pltpu.make_async_copy(weighted.at[:, kept], keep_hbm.at[:, at], out_sem.at[pair, 1]),
            ])
            outgoing[-2].start()
            outgoing[-1].start()

    handed, done = set(), set()
    total = jnp.zeros(score_ref.shape, F32)
    for block in range(blocks):
        for copy in incoming[block]:
            copy.wait()
        for row in range(block * deep, (block + 1) * deep):
            expand(row, block % 2, (row - block * deep) * line)
            done |= {row, box - row}
        if block == blocks - 1:
            expand(box // 2, 2, 0)
            done.add(box // 2)
        if block:
            total += block_table(block - 1)
        hand_over(done)
    total += block_table(blocks - 1)
    middle = width // 2
    total += 2.0 * fit(middle, middle + line) - energy(2, line)
    score_ref[...] = total
    for k, near_ref in zip(near, near_refs):
        for other in range(2):
            owner = (k ^ chip) * 2 + lax.rem(core + other, 2)
            part = weighted[:, pl.ds(met_column(share, owner, lax.axis_index("slab")), met)]
            near_ref[:, other * met : (other + 1) * met] = part.astype(near_ref.dtype)
        if k:
            near_ref[:, 2 * met :] = table
    for copy in outgoing:
        copy.wait()


def far(*operands):
    return [pltpu.with_memory_space_constraint(operand, pltpu.HBM) for operand in operands]


def estep(index, images, planes, ctf_table, share, near):
    rows, width = images.shape
    chips = width // share // 2
    wide, met = split_share(share)
    summed = 2 * wide
    count = planes.shape[0]
    blocks = 4
    span = width // (2 * blocks)
    held = pl.BlockSpec(memory_space=pl.ANY)
    vmem = pl.BlockSpec(memory_space=pltpu.VMEM)
    hbm = pl.BlockSpec(memory_space=pltpu.HBM)
    return pl.pallas_call(
        functools.partial(estep_kernel, blocks, share, near),
        in_specs=[hbm] * 4,
        out_specs=[held, held] + [vmem] * (1 + len(near)),
        out_shape=[
            jax.ShapeDtypeStruct((rows, chips * summed), F32),
            pltpu.HBM((rows, chips * summed), BF16),
            jax.ShapeDtypeStruct((rows, count), F32),
        ]
        + [
            jax.ShapeDtypeStruct((rows, 2 * met + LANES), F32)
            if k
            else pltpu.HBM((rows, 2 * met), BF16)
            for k in near
        ],
        scratch_shapes=[
            pltpu.VMEM(index.shape, jnp.int32),
            pltpu.VMEM((rows, width), BF16),
            pltpu.VMEM((count, width), BF16),
            pltpu.VMEM(ctf_table.shape, F32),
            pltpu.VMEM((rows, width), BF16),
            pltpu.VMEM((rows, chips * summed), F32),
            pltpu.VMEM((3, rows, span), BF16),
            pltpu.VMEM((3, count, span), BF16),
            pltpu.SemaphoreType.DMA((2,)),
            pltpu.SemaphoreType.DMA((blocks, 2, 2)),
            pltpu.SemaphoreType.DMA((chips, 2)),
        ],
        compiler_params=params(28),
        name="estep",
    )(*far(index, images, planes, ctf_table))


def early_kernel(share, beyond, index_hbm, image_hbm, ctf_hbm, *refs):
    outs = refs[: len(beyond)]
    index, image, ctf_held, index_sem, image_sem, ctf_sem = refs[len(beyond) :]
    met = split_share(share)[1]
    chip, core = lax.axis_index("img") // 2, lax.rem(lax.axis_index("img"), 2)
    fetch = pltpu.make_async_copy(ctf_hbm, ctf_held, ctf_sem)
    fetch.start()
    copies = []
    for place, k in enumerate(beyond):
        for other in range(2):
            owner = (k ^ chip) * 2 + lax.rem(core + other, 2)
            cut = pl.ds(met_column(share, owner, lax.axis_index("slab")), met)
            copies.append([
                pltpu.make_async_copy(
                    index_hbm.at[:, cut], index.at[place, other], index_sem.at[place, other]
                ),
                pltpu.make_async_copy(
                    image_hbm.at[:, cut], image.at[place, other], image_sem.at[place, other]
                ),
            ])
            for copy in copies[-1]:
                copy.start()
    fetch.wait()
    table = lanes_wide(ctf_held[...])
    for place, out_ref in enumerate(outs):
        for other in range(2):
            for copy in copies[2 * place + other]:
                copy.wait()
            for start in range(0, met, LANES):
                cut = slice(start, start + LANES)
                ctf = spread(table, index[place, other, :, cut])
                part = (image[place, other, :, cut].astype(F32) * ctf).astype(BF16)
                out_ref[:, other * met + start : other * met + start + LANES] = part.astype(F32)
        if out_ref.shape[1] > 2 * met:
            out_ref[:, 2 * met :] = table


def early_images(index, images, ctf_table, share, beyond, relayed):
    rows = images.shape[0]
    met = split_share(share)[1]
    number = len(beyond)
    vmem = pl.BlockSpec(memory_space=pltpu.VMEM)
    hbm = pl.BlockSpec(memory_space=pltpu.HBM)
    return pl.pallas_call(
        functools.partial(early_kernel, share, beyond),
        in_specs=[hbm, hbm, hbm],
        out_specs=[vmem] * number,
        out_shape=[
            jax.ShapeDtypeStruct((rows, 2 * met + LANES * (k != relayed)), F32) for k in beyond
        ],
        scratch_shapes=[
            pltpu.VMEM((number, 2, 1, met), jnp.int32),
            pltpu.VMEM((number, 2, rows, met), BF16),
            pltpu.VMEM(ctf_table.shape, F32),
            pltpu.SemaphoreType.DMA((number, 2)),
            pltpu.SemaphoreType.DMA((number, 2)),
            pltpu.SemaphoreType.DMA(()),
        ],
        compiler_params=params(12),
        name="early",
    )(*far(index, images, ctf_table))


def count_kernel(slabs, prior_ref, noise_ref, list_ref, base_ref, scale_ref):
    rows, listed = list_ref.shape
    classes, _, width = base_ref.shape
    each = listed // classes
    local = width // slabs
    lane = lax.broadcasted_iota(jnp.int32, (rows, width), 1)
    home = lax.axis_index("slab") ^ (lane // local)
    plane = home * local + lax.rem(lane, local)
    for one in range(classes):
        sums = jnp.zeros((rows, width), F32)
        for entry in range(each):
            place = one * each + entry
            sums += jnp.where(list_ref[:, place : place + 1] == plane, 1.0, 0.0)
        base_ref[one] = jnp.where(sums > 0.0, jnp.log(sums) + jnp.log(prior_ref[:, one : one + 1]), -jnp.inf)
    noise = jnp.broadcast_to(noise_ref[...], (rows, rows))
    diagonal = lax.broadcasted_iota(jnp.int32, (rows, rows), 0) == lax.broadcasted_iota(
        jnp.int32, (rows, rows), 1
    )
    column = jnp.sum(jnp.where(diagonal, noise, 0.0), axis=1, keepdims=True)
    scale_ref[...] = jnp.broadcast_to(column, (rows, width))


def count_planes(class_weight, inv_noise, orientations, width, slabs):
    rows, classes, each = orientations.shape
    vmem = pl.BlockSpec(memory_space=pltpu.VMEM)
    return pl.pallas_call(
        functools.partial(count_kernel, slabs),
        in_specs=[vmem] * 3,
        out_specs=[vmem, vmem],
        out_shape=[
            jax.ShapeDtypeStruct((classes, rows, width), F32),
            jax.ShapeDtypeStruct((rows, width), F32),
        ],
        compiler_params=params(4),
        name="count",
    )(
        class_weight.reshape(1, classes),
        inv_noise.reshape(1, rows),
        orientations.reshape(rows, classes * each),
    )


def weigh_kernel(base_ref, scale_ref, *refs):
    table_refs, (own_ref, both_ref) = refs[:-2], refs[-2:]
    classes = base_ref.shape[0]
    planes = own_ref.shape[0]
    local = planes // classes
    scores = []
    for one in range(classes):
        parts = [
            ref[:, start + one * local : start + (one + 1) * local]
            for ref in table_refs
            for start in range(0, ref.shape[1], planes)
        ]
        scores.append(base_ref[one] + scale_ref[...] * jnp.concatenate(parts, axis=1))
    peak = functools.reduce(jnp.maximum, [jnp.max(score, axis=1, keepdims=True) for score in scores])
    raw = [jnp.exp(score - peak) for score in scores]
    total = functools.reduce(jnp.add, [jnp.sum(part, axis=1, keepdims=True) for part in raw])
    slabs = [
        jnp.concatenate([part[:, place * local : (place + 1) * local] for part in raw], axis=1) / total
        for place in range(2)
    ]
    own_ref[...] = slabs[0].T
    both_ref[...] = jnp.concatenate(slabs, axis=1)


def weigh(base, scale, tables, planes):
    rows = base.shape[1]
    return pl.pallas_call(
        weigh_kernel,
        out_shape=[
            jax.ShapeDtypeStruct((planes, rows), F32),
            jax.ShapeDtypeStruct((rows, 2 * planes), F32),
        ],
        compiler_params=params(4),
        name="weigh",
    )(base, scale, *tables)


def gather_kernel(items, keep_hbm, got_hbm, out_ref, got, in_sem):
    number, rows2, wide = out_ref.shape
    rows = rows2 // 2
    incoming = []
    for place, (side, k) in enumerate(items):
        cut = slice((2 * k + side) * wide, (2 * k + side + 1) * wide)
        incoming.append([
            pltpu.make_async_copy(keep_hbm.at[:, cut], out_ref.at[place, :rows], in_sem.at[place, 0]),
            pltpu.make_async_copy(got_hbm.at[:, cut], got.at[place], in_sem.at[place, 1]),
        ])
        for copy in incoming[-1]:
            copy.start()
    for place in range(number):
        for copy in incoming[place]:
            copy.wait()
        out_ref[place, rows:] = got[place].astype(BF16)


def gather_images(items, keep, got, wide):
    rows = keep.shape[0]
    number = len(items)
    held = pl.BlockSpec(memory_space=pl.ANY)
    return pl.pallas_call(
        functools.partial(gather_kernel, items),
        in_specs=[held] * 2,
        out_specs=pl.BlockSpec(memory_space=pltpu.VMEM),
        out_shape=jax.ShapeDtypeStruct((number, 2 * rows, wide), BF16),
        scratch_shapes=[
            pltpu.VMEM((number, rows, wide), F32),
            pltpu.SemaphoreType.DMA((number, 2)),
        ],
        compiler_params=params(8),
        name="gather",
    )(keep, got)


def first_sums_kernel(items, own_w_ref, sib_w_ref, both_w_ref, image_ref, *outs):
    wide = image_ref.shape[2]
    weights = jnp.concatenate([own_w_ref[...], sib_w_ref[...]], axis=1).astype(BF16)
    slots = [0] * len(outs)
    for place, (side, _) in enumerate(items):
        out_ref, slot = outs[side], slots[side]
        slots[side] += 1
        out_ref[slot, :, :wide] = jnp.dot(weights, image_ref[place], preferred_element_type=F32)
        out_ref[slot, :, wide:] = both_w_ref[...]


def first_sums(items, own_w, sib_w, both_w, images):
    planes = own_w.shape[0]
    wide = images.shape[2]
    vmem = pl.BlockSpec(memory_space=pltpu.VMEM)
    return pl.pallas_call(
        functools.partial(first_sums_kernel, items),
        in_specs=[vmem] * 4,
        out_specs=[vmem] * 2,
        out_shape=[
            jax.ShapeDtypeStruct(
                (sum(side == one for side, _ in items), planes, wide + both_w.shape[1]), F32
            )
            for one in (0, 1)
        ],
        compiler_params=params(8),
        name="first_sums",
    )(own_w, sib_w, both_w, images)


def sums_kernel(items, relay, own_w_ref, sib_w_ref, keep_hbm, got_hbm, *refs):
    if relay:
        ctf_hbm, refs = refs[0], refs[1:]
    outs = refs[: len(items)]
    keep, got, in_sem = refs[len(items) : len(items) + 3]
    number, _, wide = keep.shape
    places = [(slot, k, side) for side, ks in enumerate(items) for slot, k in enumerate(ks)]
    incoming = []
    for place, (slot, k, side) in enumerate(places):
        source = slice((2 * k + side) * wide, (2 * k + side + 1) * wide)
        incoming.append([
            pltpu.make_async_copy(keep_hbm.at[:, source], keep.at[place], in_sem.at[place, 0]),
            pltpu.make_async_copy(got_hbm.at[:, source], got.at[place], in_sem.at[place, 1]),
        ])
        for copy in incoming[-1]:
            copy.start()
    if relay:
        ctf, ctf_sem = refs[-2:]
        fetch = pltpu.make_async_copy(ctf_hbm.at[:, ctf_hbm.shape[1] - LANES :], ctf, ctf_sem)
        fetch.start()
    weights = jnp.concatenate([own_w_ref[...], sib_w_ref[...]], axis=1).astype(BF16)
    for place, (slot, k, side) in enumerate(places):
        for copy in incoming[place]:
            copy.wait()
        images = jnp.concatenate([keep[place], got[place].astype(BF16)], axis=0)
        outs[side][slot, :, :wide] = jnp.dot(weights, images, preferred_element_type=F32)
    if relay:
        fetch.wait()
        for slot in range(outs[0].shape[0]):
            outs[0][slot, :, wide:] = ctf[...]


def partial_sums(items, own_w, sib_w, keep, got, wide, relay=()):
    rows = keep.shape[0]
    planes = own_w.shape[0]
    number = sum(len(ks) for ks in items)
    held = pl.BlockSpec(memory_space=pl.ANY)
    vmem = pl.BlockSpec(memory_space=pltpu.VMEM)
    return pl.pallas_call(
        functools.partial(sums_kernel, items, bool(relay)),
        in_specs=[vmem] * 2 + [held] * (2 + len(relay)),
        out_specs=[vmem] * 2,
        out_shape=[
            jax.ShapeDtypeStruct((len(ks), planes, wide + extra), F32)
            for ks, extra in zip(items, (LANES * len(relay), 0))
        ],
        scratch_shapes=[
            pltpu.VMEM((number, rows, wide), BF16),
            pltpu.VMEM((number, rows, wide), F32),
            pltpu.SemaphoreType.DMA((number, 2)),
        ]
        + [pltpu.VMEM((rows, LANES), F32), pltpu.SemaphoreType.DMA(())] * len(relay),
        compiler_params=params(12),
        name="sums",
    )(own_w, sib_w, keep, got, *relay)


def meet_kernel(chips, *refs):
    weight_refs, image_refs, outs = refs[:chips], refs[chips : 2 * chips], refs[2 * chips :]
    planes, met = outs[0].shape
    weights = []
    for ref in weight_refs:
        wide = ref.shape[-1]
        part = ref[:, wide - planes :] if len(ref.shape) == 2 else ref[0, :, wide - planes :]
        weights.append(part.astype(BF16))
    weights = jnp.concatenate(weights, axis=0)
    for other, out_ref in enumerate(outs):
        cut = slice(other * met, (other + 1) * met)
        images = jnp.concatenate([ref[:, cut].astype(BF16) for ref in image_refs], axis=0)
        out_ref[...] = lax.dot_general(
            weights, images, (((0,), (0,)), ((), ())), preferred_element_type=F32
        )


def meet(weights, images):
    met = images[0].shape[1] // 2
    planes = weights[0].shape[1]
    return pl.pallas_call(
        functools.partial(meet_kernel, len(weights)),
        out_shape=[jax.ShapeDtypeStruct((planes, met), F32)] * 2,
        compiler_params=params(16),
        name="meet",
    )(*weights, *images)


def shells_kernel(chips, ctf_ref, *refs):
    weight_refs, tail_refs, out_ref = refs[:chips], refs[chips:-1], refs[-1]
    planes = out_ref.shape[0]
    weights = []
    for ref in weight_refs:
        cut = slice(ref.shape[-1] - 2 * planes, ref.shape[-1] - planes)
        weights.append((ref[:, cut] if len(ref.shape) == 2 else ref[0, :, cut]).astype(BF16))
    ctf = [lanes_wide(ctf_ref[...])]
    ctf += [ref[...] if len(ref.shape) == 2 else ref[0] for ref in tail_refs]
    squares = jnp.concatenate([(part * part).astype(BF16) for part in ctf], axis=0)
    out_ref[...] = lax.dot_general(
        jnp.concatenate(weights, axis=0), squares, (((0,), (0,)), ((), ())), preferred_element_type=F32
    )


def shell_sums(ctf_table, weights, tails):
    rows = ctf_table.shape[0]
    planes = weights[0].shape[1] // 2

    def whole(array):
        return pl.BlockSpec(array.shape, lambda step: (0,) * len(array.shape))

    def last(array):
        place = array.shape[-1] // LANES - 1
        if len(array.shape) == 2:
            return pl.BlockSpec((rows, LANES), lambda step: (0, place))
        return pl.BlockSpec((1, rows, LANES), lambda step: (0, 0, place))

    return pl.pallas_call(
        functools.partial(shells_kernel, len(weights)),
        grid=(1,),
        in_specs=[whole(ctf_table)] + [whole(part) for part in weights] + [last(part) for part in tails],
        out_specs=pl.BlockSpec((planes, LANES), lambda step: (0, 0)),
        out_shape=jax.ShapeDtypeStruct((planes, LANES), F32),
        compiler_params=params(8),
        name="shells",
    )(ctf_table, *weights, *tails)


def prepare_kernel(places, index_hbm, met_ref, sib_met_ref, shell_ref, sib_shell_ref, *refs):
    total = sum(map(len, places))
    parts, (base_ref, scale_ref, index, in_sem) = refs[:total], refs[total:]
    planes, share = base_ref.shape
    wide, met = split_share(share)
    mine = pl.ds(pl.multiple_of(lax.axis_index("img") * share, share), share)
    fetch = pltpu.make_async_copy(index_hbm.at[:, mine], index, in_sem)
    fetch.start()
    start = 0
    for side, numbers in enumerate(places):
        refs = list(zip(parts[start : start + len(numbers)], numbers))
        start += len(numbers)
        base_ref[:, side * wide : (side + 1) * wide] = functools.reduce(
            jnp.add, [ref[place, :, :wide] for ref, place in refs]
        )
    half = lax.rem(lax.axis_index("slab"), 2)
    own = pl.ds(pl.multiple_of(2 * wide + half * met, LANES), met)
    other = pl.ds(pl.multiple_of(2 * wide + (1 - half) * met, LANES), met)
    base_ref[:, own] = met_ref[:planes, :met] + sib_met_ref[:planes, :met]
    base_ref[:, other] = jnp.zeros((planes, met), F32)
    shells = shell_ref[...] + sib_shell_ref[...]
    fetch.wait()
    for start in range(0, share, LANES):
        cut = slice(start, start + LANES)
        scale_ref[:, cut] = 1.0 / (spread(shells, index[:, cut]) + 1.0)


def prepare(index, met, sib_met, shells, sib_shells, sides, share):
    planes = met.shape[0] // 2
    held = pl.BlockSpec(memory_space=pl.ANY)
    vmem = pl.BlockSpec(memory_space=pltpu.VMEM)
    places = [[place for _, place in side] for side in sides]
    parts = [part for side in sides for part, _ in side]
    return pl.pallas_call(
        functools.partial(prepare_kernel, places),
        in_specs=[held] + [vmem] * (4 + len(parts)),
        out_specs=[vmem, vmem],
        out_shape=[jax.ShapeDtypeStruct((planes, share), F32)] * 2,
        scratch_shapes=[pltpu.VMEM((1, share), jnp.int32), pltpu.SemaphoreType.DMA(())],
        compiler_params=params(8),
        name="prepare",
    )(index, met, sib_met, shells, sib_shells, *parts)


def finish_kernel(base_ref, scale_ref, left_ref, right_ref, partner_ref, out_hbm, out, out_sem):
    planes, share = out.shape
    wide, met = split_share(share)
    half = lax.rem(lax.axis_index("slab"), 2)
    own = pl.multiple_of(2 * wide + half * met, LANES)
    other = pl.multiple_of(2 * wide + (1 - half) * met, LANES)

    def scaled(place, size, last=None):
        for start in range(0, size, LANES):
            at = pl.ds(pl.multiple_of(place + start, LANES), LANES)
            value = base_ref[:, at]
            if last is not None:
                value += last(slice(start, start + LANES))
            out[:, at] = value * scale_ref[:, at]

    stores = []

    def store(start, stop):
        cut = slice(start, stop)
        stores.append(
            pltpu.make_async_copy(out.at[:, cut], out_hbm.at[:, cut], out_sem.at[len(stores)])
        )
        stores[-1].start()

    scaled(own, met)
    scaled(other, met, lambda cut: partner_ref[:, cut])
    store(2 * wide, share)
    scaled(0, wide, lambda cut: left_ref[0, :, cut])
    store(0, wide)
    scaled(wide, wide, lambda cut: right_ref[0, :, cut])
    store(wide, 2 * wide)
    for copy in stores:
        copy.wait()


def finish(base, scale, left, right, partner):
    vmem = pl.BlockSpec(memory_space=pltpu.VMEM)
    return pl.pallas_call(
        finish_kernel,
        in_specs=[vmem] * 5,
        out_specs=pl.BlockSpec(memory_space=pl.ANY),
        out_shape=jax.ShapeDtypeStruct(base.shape, F32),
        scratch_shapes=[pltpu.VMEM(base.shape, F32), pltpu.SemaphoreType.DMA((3,))],
        compiler_params=params(8),
        name="finish",
    )(base, scale, left, right, partner)


def swap(array, bit, size):
    return lax.ppermute(array, "img", [(one, one ^ bit) for one in range(size)])


def shards(images, references, orientations, ctf_table, inv_noise, class_weight):
    rows, width = images.shape
    classes, local_planes, _ = references.shape
    size = lax.axis_size("img")
    slabs = lax.axis_size("slab")
    chips = size // 2
    share = width // size
    wide, met_wide = split_share(share)
    index = entry_shells(width, ctf_table.shape[1])
    top_index = jnp.asarray(index[:, : width // 2 + 2 * math.isqrt(width // 2)])
    index = jnp.asarray(index)
    planes = references.reshape(classes * local_planes, width)

    beyond = tuple(k for k in range(chips) if k & (k - 1))
    near = tuple(k for k in range(chips) if k not in beyond)
    relayed = 1 | chips // 2
    met_images = {}
    if beyond:
        early = early_images(index, images, ctf_table, share, beyond, relayed)
        images, *early = lax.optimization_barrier((images, *early))
        met_images = {k: swap(part, 2 * k, size) for k, part in zip(beyond, early)}
    give, keep, table, *parts_near = estep(
        top_index, images, planes, ctf_table, share, near
    )
    if beyond:
        give, keep, met_images[beyond[-1]], *parts_near = lax.optimization_barrier(
            (give, keep, met_images[beyond[-1]], *parts_near)
        )
    for k, part in zip(near, parts_near):
        met_images[k] = swap(part, 2 * k, size) if k else part
    keep, *met_images = far(keep, *[met_images[k] for k in range(chips)])
    base, scale = count_planes(
        class_weight, inv_noise, orientations, slabs * local_planes, slabs
    )
    tables, bit = [table], 1
    while bit < slabs:
        held = tables[0]
        if len(tables) > 1:
            held = jnp.concatenate(tables, axis=1)
        pairs = [(one, one ^ bit) for one in range(slabs)]
        tables = [held, lax.ppermute(held, "slab", pairs)]
        bit *= 2
    got = swap(give, 1, size)
    own_w, both_w = weigh(base, scale, tables, classes * local_planes)
    sib_w = swap(own_w, 1, size)

    sums = functools.partial(
        partial_sums, own_w=own_w, sib_w=sib_w, keep=keep, got=got, wide=wide,
    )
    low = [1 << place for place in range(chips.bit_length() - 1)]
    orders = (low, low[::-1])
    first = [[k for k in range(chips) if k & order[0]] for order in orders]
    onward = [[k for k in ks if k & order[1]] for ks, order in zip(first, orders)]
    direct = [[k for k in ks if not k & order[1]] for ks, order in zip(first, orders)]
    stay = [[k for k in range(chips) if not k & order[0]] for order in orders]
    parts = [{k: [] for k in ks} for ks in stay]

    def deliver(side, ks, array, bit):
        arrived = swap(array, 2 * bit, size)
        for place, k in enumerate(ks):
            parts[side][k ^ bit].append((arrived, place))
        return arrived

    def compute(groups, relay=()):
        return sums(tuple(tuple(ks) for ks in groups), relay=relay)

    items = tuple((side, k) for side, ks in enumerate(onward) for k in ks)
    sent = first_sums(items, own_w, sib_w, both_w, gather_images(items, keep, got, wide))
    arrived = [swap(sent[side], 2 * orders[side][0], size) for side in (0, 1)]
    both_w, _ = lax.optimization_barrier((both_w, sent[1]))
    others = [k for k in range(1, chips) if k not in (orders[0][0], orders[1][0])]
    far_w = [swap(both_w, 2 * k, size) for k in others]
    sums.keywords["keep"], *met_images = lax.optimization_barrier((keep, *met_images))
    sent = compute(direct, (met_images[chips // 2],))
    relays = [deliver(side, direct[side], sent[side], orders[side][0]) for side in (0, 1)]
    kept = compute(stay)
    for side in (0, 1):
        for place, k in enumerate(stay[side]):
            parts[side][k].append((kept[side], place))

    met_images[0], _, *arrived = lax.optimization_barrier(
        (met_images[0], sent[0], *arrived, *far_w)
    )
    far_w = dict(zip(others, arrived[2:]))
    far_w[0] = both_w
    for side in (0, 1):
        bit = orders[side][0]
        far_w[bit] = arrived[side]
        for place, k in enumerate(onward[side]):
            parts[side][k ^ bit].append((arrived[side], place))
    weights = [far_w[k] for k in range(chips)]
    met, for_sib = meet(weights, met_images)
    tails = [relays[0] if k == relayed else met_images[k] for k in range(1, chips)]
    shells = shell_sums(ctf_table, weights, tails)
    sib_shells = swap(shells, 1, size)
    sib_met = swap(for_sib, 1, size)
    own_planes = classes * local_planes
    partner = lax.ppermute(
        met[own_planes:, :met_wide] + sib_met[own_planes:, :met_wide], "slab", [(one, one ^ 1) for one in range(slabs)]
    )

    for turn in range(1, len(low)):
        for side in (0, 1):
            bit = orders[side][turn]
            ks = [k for k in parts[side] if k & bit]
            sent = jnp.stack(
                [sum(part[place, :, :wide] for part, place in parts[side].pop(k)) for k in ks]
            )
            deliver(side, ks, sent, bit)
    base, scale = prepare(
        index, met, sib_met, shells, sib_shells, [parts[side][0][:-1] for side in (0, 1)], share
    )
    out = finish(base, scale, parts[0][0][-1][0], parts[1][0][-1][0], partner)
    return out.reshape(classes, local_planes, share)


def solution(mesh):
    return jax.shard_map(
        shards,
        mesh=mesh,
        in_specs=(
            P("img", None),
            P(None, "slab", None),
            P("img", None, None),
            P("img", None),
            P("img"),
            P(),
        ),
        out_specs=P(None, "slab", "img"),
        check_vma=False,
    )
```

```python
import functools
import math

import jax
import jax.numpy as jnp
import numpy as np
from jax import lax
from jax.experimental import pallas as pl
from jax.experimental.pallas import tpu as pltpu
from jax.sharding import PartitionSpec as P

F32 = jnp.float32
BF16 = jnp.bfloat16
LANES = 128
PIECE = 5 * LANES
MIB = 1024 * 1024


def entry_shells(width, shells):
    pixels = width // 2
    box = math.isqrt(pixels)
    place = np.arange(pixels)
    column = place % box - box // 2
    row = place // box - box // 2
    radius = column * column + row * row
    levels = np.arange(1, shells)
    shell = np.sum(2 * levels[None, :] ** 2 <= radius[:, None], axis=1)
    return np.repeat(shell, 2).astype(np.int32)[None, :]


def split_share(share):
    met = max(LANES, 6 * share // 32 // LANES * LANES)
    return share // 2 - met, met


def met_column(share, owner, slab):
    wide, met = split_share(share)
    return pl.multiple_of(owner * share + 2 * wide + lax.rem(slab, 2) * met, LANES)


def params(mib):
    return pltpu.CompilerParams(vmem_limit_bytes=mib * MIB)


def lanes_wide(table):
    rows, shells = table.shape
    if shells == LANES:
        return table
    return jnp.concatenate([table, jnp.zeros((rows, LANES - shells), table.dtype)], axis=1)


def spread(table, index):
    return jnp.take_along_axis(table, jnp.broadcast_to(index, table.shape), axis=1)


def contract_last(left, right):
    return lax.dot_general(left, right, (((1,), (1,)), ((), ())), preferred_element_type=F32)


def estep_kernel(
    blocks, share, near, index_hbm, image_hbm, plane_hbm, ctf_hbm, *refs,
):
    give_hbm, keep_hbm, score_ref = refs[:3]
    near_refs = refs[3 : 3 + len(near)]
    index, image, plane, ctf_held, weighted, give, squared, energy_of = refs[-11:-3]
    small_sem, in_sem, out_sem = refs[-3:]
    rows, width = image.shape
    wide, met = split_share(share)
    chips, summed = width // share // 2, 2 * wide
    box = math.isqrt(width // 2)
    line = 2 * box
    deep = box // (2 * blocks)
    span = deep * line

    small = [
        pltpu.make_async_copy(index_hbm, index, small_sem.at[0]),
        pltpu.make_async_copy(ctf_hbm, ctf_held, small_sem.at[1]),
    ]
    incoming = []
    for block in range(blocks):
        copies = []
        for side, start in enumerate((block * span, width - (block + 1) * span)):
            cut = pl.ds(start, span)
            copies += [
                pltpu.make_async_copy(
                    image_hbm.at[:, cut], image.at[:, cut], in_sem.at[block, side, 0]
                ),
                pltpu.make_async_copy(
                    plane_hbm.at[:, cut], plane.at[:, cut], in_sem.at[block, side, 1]
                ),
            ]
        incoming.append(copies)
    for copy in small + [copy for copies in incoming for copy in copies]:
        copy.start()
    for copy in small:
        copy.wait()
    table = lanes_wide(ctf_held[...])

    def weigh_image(cut, ctf):
        weighted[:, cut] = (image[:, cut].astype(F32) * ctf).astype(BF16)

    def square(cut):
        part = plane[:, cut].astype(F32)
        return part * part

    def expand(row, slot, place):
        mirror = box - row if 0 < row < box // 2 else None
        for start in range(0, line, LANES):
            cut = slice(row * line + start, row * line + start + LANES)
            ctf = spread(table, index[:, cut])
            weigh_image(cut, ctf)
            power = square(cut)
            if mirror is not None:
                other = slice(mirror * line + start, mirror * line + start + LANES)
                weigh_image(other, ctf)
                power += square(other)
            held = slice(place + start, place + start + LANES)
            squared[slot, :, held] = (ctf * ctf).astype(BF16)
            energy_of[slot, :, held] = power.astype(BF16)

    def fit(start, stop):
        return contract_last(weighted[:, start:stop], plane[:, start:stop])

    def energy(slot, size):
        return contract_last(squared[slot, :, :size], energy_of[slot, :, :size])

    def block_table(block):
        low, high = fit(block * span, (block + 1) * span), width - block * span
        stop = high + line if block else high
        low += fit(high - span + line, stop)
        return 2.0 * low - energy(block % 2, span)

    chip, core = lax.axis_index("img") // 2, lax.rem(lax.axis_index("img"), 2)
    outgoing = []

    def hand_over(done):
        for pair in range(chips):
            first, last = 2 * pair * share // line, -(-2 * (pair + 1) * share // line)
            if pair in handed or not all(row in done for row in range(first, last)):
                continue
            handed.add(pair)
            place = pair ^ chip
            given = pl.ds(pl.multiple_of((2 * pair + 1 - core) * share, share), summed)
            kept = pl.ds(pl.multiple_of((2 * pair + core) * share, share), summed)
            at = pl.ds(pl.multiple_of(place * summed, LANES), summed)
            give[:, at] = weighted[:, given].astype(F32)
            outgoing.extend([
                pltpu.make_async_copy(give.at[:, at], give_hbm.at[:, at], out_sem.at[pair, 0]),
                pltpu.make_async_copy(weighted.at[:, kept], keep_hbm.at[:, at], out_sem.at[pair, 1]),
            ])
            outgoing[-2].start()
            outgoing[-1].start()

    handed, done = set(), set()
    total = jnp.zeros(score_ref.shape, F32)
    for block in range(blocks):
        for copy in incoming[block]:
            copy.wait()
        for row in range(block * deep, (block + 1) * deep):
            expand(row, block % 2, (row - block * deep) * line)
            done |= {row, box - row}
        if block == blocks - 1:
            expand(box // 2, 2, 0)
            done.add(box // 2)
        if block:
            total += block_table(block - 1)
        hand_over(done)
    total += block_table(blocks - 1)
    middle = width // 2
    total += 2.0 * fit(middle, middle + line) - energy(2, line)
    score_ref[...] = total
    for k, near_ref in zip(near, near_refs):
        for other in range(2):
            owner = (k ^ chip) * 2 + lax.rem(core + other, 2)
            part = weighted[:, pl.ds(met_column(share, owner, lax.axis_index("slab")), met)]
            near_ref[:, other * met : (other + 1) * met] = part.astype(near_ref.dtype)
        if k:
            near_ref[:, 2 * met :] = table
    for copy in outgoing:
        copy.wait()


def far(*operands):
    return [pltpu.with_memory_space_constraint(operand, pltpu.HBM) for operand in operands]


def estep(index, images, planes, ctf_table, share, near):
    rows, width = images.shape
    chips = width // share // 2
    wide, met = split_share(share)
    summed = 2 * wide
    count = planes.shape[0]
    blocks = 4
    span = width // (2 * blocks)
    held = pl.BlockSpec(memory_space=pl.ANY)
    vmem = pl.BlockSpec(memory_space=pltpu.VMEM)
    hbm = pl.BlockSpec(memory_space=pltpu.HBM)
    return pl.pallas_call(
        functools.partial(estep_kernel, blocks, share, near),
        in_specs=[hbm] * 4,
        out_specs=[held, held] + [vmem] * (1 + len(near)),
        out_shape=[
            jax.ShapeDtypeStruct((rows, chips * summed), F32),
            pltpu.HBM((rows, chips * summed), BF16),
            jax.ShapeDtypeStruct((rows, count), F32),
        ]
        + [
            jax.ShapeDtypeStruct((rows, 2 * met + LANES), F32)
            if k
            else pltpu.HBM((rows, 2 * met), BF16)
            for k in near
        ],
        scratch_shapes=[
            pltpu.VMEM(index.shape, jnp.int32),
            pltpu.VMEM((rows, width), BF16),
            pltpu.VMEM((count, width), BF16),
            pltpu.VMEM(ctf_table.shape, F32),
            pltpu.VMEM((rows, width), BF16),
            pltpu.VMEM((rows, chips * summed), F32),
            pltpu.VMEM((3, rows, span), BF16),
            pltpu.VMEM((3, count, span), BF16),
            pltpu.SemaphoreType.DMA((2,)),
            pltpu.SemaphoreType.DMA((blocks, 2, 2)),
            pltpu.SemaphoreType.DMA((chips, 2)),
        ],
        compiler_params=params(28),
        name="estep",
    )(*far(index, images, planes, ctf_table))


def early_kernel(share, beyond, index_hbm, image_hbm, ctf_hbm, *refs):
    outs = refs[: len(beyond)]
    index, image, ctf_held, index_sem, image_sem, ctf_sem = refs[len(beyond) :]
    met = split_share(share)[1]
    chip, core = lax.axis_index("img") // 2, lax.rem(lax.axis_index("img"), 2)
    fetch = pltpu.make_async_copy(ctf_hbm, ctf_held, ctf_sem)
    fetch.start()
    copies = []
    for place, k in enumerate(beyond):
        for other in range(2):
            owner = (k ^ chip) * 2 + lax.rem(core + other, 2)
            cut = pl.ds(met_column(share, owner, lax.axis_index("slab")), met)
            copies.append([
                pltpu.make_async_copy(
                    index_hbm.at[:, cut], index.at[place, other], index_sem.at[place, other]
                ),
                pltpu.make_async_copy(
                    image_hbm.at[:, cut], image.at[place, other], image_sem.at[place, other]
                ),
            ])
            for copy in copies[-1]:
                copy.start()
    fetch.wait()
    table = lanes_wide(ctf_held[...])
    for place, out_ref in enumerate(outs):
        for other in range(2):
            for copy in copies[2 * place + other]:
                copy.wait()
            for start in range(0, met, LANES):
                cut = slice(start, start + LANES)
                ctf = spread(table, index[place, other, :, cut])
                part = (image[place, other, :, cut].astype(F32) * ctf).astype(BF16)
                out_ref[:, other * met + start : other * met + start + LANES] = part.astype(F32)
        if out_ref.shape[1] > 2 * met:
            out_ref[:, 2 * met :] = table


def early_images(index, images, ctf_table, share, beyond, relayed):
    rows = images.shape[0]
    met = split_share(share)[1]
    number = len(beyond)
    vmem = pl.BlockSpec(memory_space=pltpu.VMEM)
    hbm = pl.BlockSpec(memory_space=pltpu.HBM)
    return pl.pallas_call(
        functools.partial(early_kernel, share, beyond),
        in_specs=[hbm, hbm, hbm],
        out_specs=[vmem] * number,
        out_shape=[
            jax.ShapeDtypeStruct((rows, 2 * met + LANES * (k != relayed)), F32) for k in beyond
        ],
        scratch_shapes=[
            pltpu.VMEM((number, 2, 1, met), jnp.int32),
            pltpu.VMEM((number, 2, rows, met), BF16),
            pltpu.VMEM(ctf_table.shape, F32),
            pltpu.SemaphoreType.DMA((number, 2)),
            pltpu.SemaphoreType.DMA((number, 2)),
            pltpu.SemaphoreType.DMA(()),
        ],
        compiler_params=params(12),
        name="early",
    )(*far(index, images, ctf_table))


def count_kernel(slabs, prior_ref, noise_ref, list_ref, base_ref, scale_ref):
    rows, listed = list_ref.shape
    classes, _, width = base_ref.shape
    each = listed // classes
    local = width // slabs
    lane = lax.broadcasted_iota(jnp.int32, (rows, width), 1)
    home = lax.axis_index("slab") ^ (lane // local)
    plane = home * local + lax.rem(lane, local)
    for one in range(classes):
        sums = jnp.zeros((rows, width), F32)
        for entry in range(each):
            place = one * each + entry
            sums += jnp.where(list_ref[:, place : place + 1] == plane, 1.0, 0.0)
        base_ref[one] = jnp.where(sums > 0.0, jnp.log(sums) + jnp.log(prior_ref[:, one : one + 1]), -jnp.inf)
    noise = jnp.broadcast_to(noise_ref[...], (rows, rows))
    diagonal = lax.broadcasted_iota(jnp.int32, (rows, rows), 0) == lax.broadcasted_iota(
        jnp.int32, (rows, rows), 1
    )
    column = jnp.sum(jnp.where(diagonal, noise, 0.0), axis=1, keepdims=True)
    scale_ref[...] = jnp.broadcast_to(column, (rows, width))


def count_planes(class_weight, inv_noise, orientations, width, slabs):
    rows, classes, each = orientations.shape
    vmem = pl.BlockSpec(memory_space=pltpu.VMEM)
    return pl.pallas_call(
        functools.partial(count_kernel, slabs),
        in_specs=[vmem] * 3,
        out_specs=[vmem, vmem],
        out_shape=[
            jax.ShapeDtypeStruct((classes, rows, width), F32),
            jax.ShapeDtypeStruct((rows, width), F32),
        ],
        compiler_params=params(4),
        name="count",
    )(
        class_weight.reshape(1, classes),
        inv_noise.reshape(1, rows),
        orientations.reshape(rows, classes * each),
    )


def weigh_kernel(base_ref, scale_ref, *refs):
    table_refs, (own_ref, both_ref) = refs[:-2], refs[-2:]
    classes = base_ref.shape[0]
    planes = own_ref.shape[0]
    local = planes // classes
    scores = []
    for one in range(classes):
        parts = [
            ref[:, start + one * local : start + (one + 1) * local]
            for ref in table_refs
            for start in range(0, ref.shape[1], planes)
        ]
        scores.append(base_ref[one] + scale_ref[...] * jnp.concatenate(parts, axis=1))
    peak = functools.reduce(jnp.maximum, [jnp.max(score, axis=1, keepdims=True) for score in scores])
    raw = [jnp.exp(score - peak) for score in scores]
    total = functools.reduce(jnp.add, [jnp.sum(part, axis=1, keepdims=True) for part in raw])
    slabs = [
        jnp.concatenate([part[:, place * local : (place + 1) * local] for part in raw], axis=1) / total
        for place in range(2)
    ]
    own_ref[...] = slabs[0].T
    both_ref[...] = jnp.concatenate(slabs, axis=1)


def weigh(base, scale, tables, planes):
    rows = base.shape[1]
    return pl.pallas_call(
        weigh_kernel,
        out_shape=[
            jax.ShapeDtypeStruct((planes, rows), F32),
            jax.ShapeDtypeStruct((rows, 2 * planes), F32),
        ],
        compiler_params=params(4),
        name="weigh",
    )(base, scale, *tables)


def gather_kernel(items, keep_hbm, got_hbm, out_ref, got, in_sem):
    number, rows2, wide = out_ref.shape
    rows = rows2 // 2
    incoming = []
    for place, (side, k) in enumerate(items):
        cut = slice((2 * k + side) * wide, (2 * k + side + 1) * wide)
        incoming.append([
            pltpu.make_async_copy(keep_hbm.at[:, cut], out_ref.at[place, :rows], in_sem.at[place, 0]),
            pltpu.make_async_copy(got_hbm.at[:, cut], got.at[place], in_sem.at[place, 1]),
        ])
        for copy in incoming[-1]:
            copy.start()
    for place in range(number):
        for copy in incoming[place]:
            copy.wait()
        out_ref[place, rows:] = got[place].astype(BF16)


def gather_images(items, keep, got, wide):
    rows = keep.shape[0]
    number = len(items)
    held = pl.BlockSpec(memory_space=pl.ANY)
    return pl.pallas_call(
        functools.partial(gather_kernel, items),
        in_specs=[held] * 2,
        out_specs=pl.BlockSpec(memory_space=pltpu.VMEM),
        out_shape=jax.ShapeDtypeStruct((number, 2 * rows, wide), BF16),
        scratch_shapes=[
            pltpu.VMEM((number, rows, wide), F32),
            pltpu.SemaphoreType.DMA((number, 2)),
        ],
        compiler_params=params(8),
        name="gather",
    )(keep, got)


def first_sums_kernel(items, own_w_ref, sib_w_ref, both_w_ref, image_ref, *outs):
    wide = image_ref.shape[2]
    weights = jnp.concatenate([own_w_ref[...], sib_w_ref[...]], axis=1).astype(BF16)
    slots = [0] * len(outs)
    for place, (side, _) in enumerate(items):
        out_ref, slot = outs[side], slots[side]
        slots[side] += 1
        out_ref[slot, :, :wide] = jnp.dot(weights, image_ref[place], preferred_element_type=F32)
        out_ref[slot, :, wide:] = both_w_ref[...]


def first_sums(items, own_w, sib_w, both_w, images):
    planes = own_w.shape[0]
    wide = images.shape[2]
    vmem = pl.BlockSpec(memory_space=pltpu.VMEM)
    return pl.pallas_call(
        functools.partial(first_sums_kernel, items),
        in_specs=[vmem] * 4,
        out_specs=[vmem] * 2,
        out_shape=[
            jax.ShapeDtypeStruct(
                (sum(side == one for side, _ in items), planes, wide + both_w.shape[1]), F32
            )
            for one in (0, 1)
        ],
        compiler_params=params(8),
        name="first_sums",
    )(own_w, sib_w, both_w, images)


def sums_kernel(items, relay, own_w_ref, sib_w_ref, keep_hbm, got_hbm, *refs):
    if relay:
        ctf_hbm, refs = refs[0], refs[1:]
    outs = refs[: len(items)]
    keep, got, in_sem = refs[len(items) : len(items) + 3]
    number, _, wide = keep.shape
    places = [(slot, k, side) for side, ks in enumerate(items) for slot, k in enumerate(ks)]
    incoming = []
    for place, (slot, k, side) in enumerate(places):
        source = slice((2 * k + side) * wide, (2 * k + side + 1) * wide)
        incoming.append([
            pltpu.make_async_copy(keep_hbm.at[:, source], keep.at[place], in_sem.at[place, 0]),
            pltpu.make_async_copy(got_hbm.at[:, source], got.at[place], in_sem.at[place, 1]),
        ])
        for copy in incoming[-1]:
            copy.start()
    if relay:
        ctf, ctf_sem = refs[-2:]
        fetch = pltpu.make_async_copy(ctf_hbm.at[:, ctf_hbm.shape[1] - LANES :], ctf, ctf_sem)
        fetch.start()
    weights = jnp.concatenate([own_w_ref[...], sib_w_ref[...]], axis=1).astype(BF16)
    for place, (slot, k, side) in enumerate(places):
        for copy in incoming[place]:
            copy.wait()
        images = jnp.concatenate([keep[place], got[place].astype(BF16)], axis=0)
        outs[side][slot, :, :wide] = jnp.dot(weights, images, preferred_element_type=F32)
    if relay:
        fetch.wait()
        for slot in range(outs[0].shape[0]):
            outs[0][slot, :, wide:] = ctf[...]


def partial_sums(items, own_w, sib_w, keep, got, wide, relay=()):
    rows = keep.shape[0]
    planes = own_w.shape[0]
    number = sum(len(ks) for ks in items)
    held = pl.BlockSpec(memory_space=pl.ANY)
    vmem = pl.BlockSpec(memory_space=pltpu.VMEM)
    return pl.pallas_call(
        functools.partial(sums_kernel, items, bool(relay)),
        in_specs=[vmem] * 2 + [held] * (2 + len(relay)),
        out_specs=[vmem] * 2,
        out_shape=[
            jax.ShapeDtypeStruct((len(ks), planes, wide + extra), F32)
            for ks, extra in zip(items, (LANES * len(relay), 0))
        ],
        scratch_shapes=[
            pltpu.VMEM((number, rows, wide), BF16),
            pltpu.VMEM((number, rows, wide), F32),
            pltpu.SemaphoreType.DMA((number, 2)),
        ]
        + [pltpu.VMEM((rows, LANES), F32), pltpu.SemaphoreType.DMA(())] * len(relay),
        compiler_params=params(12),
        name="sums",
    )(own_w, sib_w, keep, got, *relay)


def meet_kernel(chips, *refs):
    weight_refs, image_refs, outs = refs[:chips], refs[chips : 2 * chips], refs[2 * chips :]
    planes, met = outs[0].shape
    weights = []
    for ref in weight_refs:
        wide = ref.shape[-1]
        part = ref[:, wide - planes :] if len(ref.shape) == 2 else ref[0, :, wide - planes :]
        weights.append(part.astype(BF16))
    weights = jnp.concatenate(weights, axis=0)
    for other, out_ref in enumerate(outs):
        cut = slice(other * met, (other + 1) * met)
        images = jnp.concatenate([ref[:, cut].astype(BF16) for ref in image_refs], axis=0)
        out_ref[...] = lax.dot_general(
            weights, images, (((0,), (0,)), ((), ())), preferred_element_type=F32
        )


def meet(weights, images):
    met = images[0].shape[1] // 2
    planes = weights[0].shape[1]
    return pl.pallas_call(
        functools.partial(meet_kernel, len(weights)),
        out_shape=[jax.ShapeDtypeStruct((planes, met), F32)] * 2,
        compiler_params=params(16),
        name="meet",
    )(*weights, *images)


def shells_kernel(chips, ctf_ref, *refs):
    weight_refs, tail_refs, out_ref = refs[:chips], refs[chips:-1], refs[-1]
    planes = out_ref.shape[0]
    weights = []
    for ref in weight_refs:
        cut = slice(ref.shape[-1] - 2 * planes, ref.shape[-1] - planes)
        weights.append((ref[:, cut] if len(ref.shape) == 2 else ref[0, :, cut]).astype(BF16))
    ctf = [lanes_wide(ctf_ref[...])]
    ctf += [ref[...] if len(ref.shape) == 2 else ref[0] for ref in tail_refs]
    squares = jnp.concatenate([(part * part).astype(BF16) for part in ctf], axis=0)
    out_ref[...] = lax.dot_general(
        jnp.concatenate(weights, axis=0), squares, (((0,), (0,)), ((), ())), preferred_element_type=F32
    )


def shell_sums(ctf_table, weights, tails):
    rows = ctf_table.shape[0]
    planes = weights[0].shape[1] // 2

    def whole(array):
        return pl.BlockSpec(array.shape, lambda step: (0,) * len(array.shape))

    def last(array):
        place = array.shape[-1] // LANES - 1
        if len(array.shape) == 2:
            return pl.BlockSpec((rows, LANES), lambda step: (0, place))
        return pl.BlockSpec((1, rows, LANES), lambda step: (0, 0, place))

    return pl.pallas_call(
        functools.partial(shells_kernel, len(weights)),
        grid=(1,),
        in_specs=[whole(ctf_table)] + [whole(part) for part in weights] + [last(part) for part in tails],
        out_specs=pl.BlockSpec((planes, LANES), lambda step: (0, 0)),
        out_shape=jax.ShapeDtypeStruct((planes, LANES), F32),
        compiler_params=params(8),
        name="shells",
    )(ctf_table, *weights, *tails)


def prepare_kernel(places, index_hbm, met_ref, sib_met_ref, shell_ref, sib_shell_ref, *refs):
    total = sum(map(len, places))
    parts, (base_ref, scale_ref, index, in_sem) = refs[:total], refs[total:]
    planes, share = base_ref.shape
    wide, met = split_share(share)
    mine = pl.ds(pl.multiple_of(lax.axis_index("img") * share, share), share)
    fetch = pltpu.make_async_copy(index_hbm.at[:, mine], index, in_sem)
    fetch.start()
    start = 0
    for side, numbers in enumerate(places):
        refs = list(zip(parts[start : start + len(numbers)], numbers))
        start += len(numbers)
        base_ref[:, side * wide : (side + 1) * wide] = functools.reduce(
            jnp.add, [ref[place, :, :wide] for ref, place in refs]
        )
    half = lax.rem(lax.axis_index("slab"), 2)
    own = pl.ds(pl.multiple_of(2 * wide + half * met, LANES), met)
    other = pl.ds(pl.multiple_of(2 * wide + (1 - half) * met, LANES), met)
    base_ref[:, own] = met_ref[:planes, :met] + sib_met_ref[:planes, :met]
    base_ref[:, other] = jnp.zeros((planes, met), F32)
    shells = shell_ref[...] + sib_shell_ref[...]
    fetch.wait()
    for start in range(0, share, LANES):
        cut = slice(start, start + LANES)
        scale_ref[:, cut] = 1.0 / (spread(shells, index[:, cut]) + 1.0)


def prepare(index, met, sib_met, shells, sib_shells, sides, share):
    planes = met.shape[0] // 2
    held = pl.BlockSpec(memory_space=pl.ANY)
    vmem = pl.BlockSpec(memory_space=pltpu.VMEM)
    places = [[place for _, place in side] for side in sides]
    parts = [part for side in sides for part, _ in side]
    return pl.pallas_call(
        functools.partial(prepare_kernel, places),
        in_specs=[held] + [vmem] * (4 + len(parts)),
        out_specs=[vmem, vmem],
        out_shape=[jax.ShapeDtypeStruct((planes, share), F32)] * 2,
        scratch_shapes=[pltpu.VMEM((1, share), jnp.int32), pltpu.SemaphoreType.DMA(())],
        compiler_params=params(8),
        name="prepare",
    )(index, met, sib_met, shells, sib_shells, *parts)


def finish_kernel(base_ref, scale_ref, left_ref, right_ref, partner_ref, out_hbm, out, out_sem):
    planes, share = out.shape
    wide, met = split_share(share)
    half = lax.rem(lax.axis_index("slab"), 2)
    own = pl.multiple_of(2 * wide + half * met, LANES)
    other = pl.multiple_of(2 * wide + (1 - half) * met, LANES)

    def scaled(place, size, last=None):
        for start in range(0, size, LANES):
            at = pl.ds(pl.multiple_of(place + start, LANES), LANES)
            value = base_ref[:, at]
            if last is not None:
                value += last(slice(start, start + LANES))
            out[:, at] = value * scale_ref[:, at]

    stores = []

    def scale_and_store(place, size, last=None):
        for first in range(0, size, PIECE):
            piece = min(PIECE, size - first)
            from_here = None if last is None else lambda cut: last(slice(cut.start + first, cut.stop + first))
            scaled(place + first, piece, from_here)
            cut = pl.ds(pl.multiple_of(place + first, LANES), piece)
            stores.append(
                pltpu.make_async_copy(out.at[:, cut], out_hbm.at[:, cut], out_sem.at[len(stores)])
            )
            stores[-1].start()

    scale_and_store(own, met)
    scale_and_store(other, met, lambda cut: partner_ref[:, cut])
    scale_and_store(0, wide, lambda cut: left_ref[0, :, cut])
    scale_and_store(wide, wide, lambda cut: right_ref[0, :, cut])
    for copy in stores:
        copy.wait()


def finish(base, scale, left, right, partner):
    wide, met = split_share(base.shape[1])
    pieces = 2 * (pl.cdiv(wide, PIECE) + pl.cdiv(met, PIECE))
    vmem = pl.BlockSpec(memory_space=pltpu.VMEM)
    return pl.pallas_call(
        finish_kernel,
        in_specs=[vmem] * 5,
        out_specs=pl.BlockSpec(memory_space=pl.ANY),
        out_shape=jax.ShapeDtypeStruct(base.shape, F32),
        scratch_shapes=[pltpu.VMEM(base.shape, F32), pltpu.SemaphoreType.DMA((pieces,))],
        compiler_params=params(8),
        name="finish",
    )(base, scale, left, right, partner)


def swap(array, bit, size):
    return lax.ppermute(array, "img", [(one, one ^ bit) for one in range(size)])


def shards(images, references, orientations, ctf_table, inv_noise, class_weight):
    rows, width = images.shape
    classes, local_planes, _ = references.shape
    size = lax.axis_size("img")
    slabs = lax.axis_size("slab")
    chips = size // 2
    share = width // size
    wide, met_wide = split_share(share)
    index = entry_shells(width, ctf_table.shape[1])
    top_index = jnp.asarray(index[:, : width // 2 + 2 * math.isqrt(width // 2)])
    index = jnp.asarray(index)
    planes = references.reshape(classes * local_planes, width)

    beyond = tuple(k for k in range(chips) if k & (k - 1))
    near = tuple(k for k in range(chips) if k not in beyond)
    relayed = 1 | chips // 2
    met_images = {}
    if beyond:
        early = early_images(index, images, ctf_table, share, beyond, relayed)
        images, *early = lax.optimization_barrier((images, *early))
        met_images = {k: swap(part, 2 * k, size) for k, part in zip(beyond, early)}
    give, keep, table, *parts_near = estep(
        top_index, images, planes, ctf_table, share, near
    )
    if beyond:
        give, keep, met_images[beyond[-1]], *parts_near = lax.optimization_barrier(
            (give, keep, met_images[beyond[-1]], *parts_near)
        )
    for k, part in zip(near, parts_near):
        met_images[k] = swap(part, 2 * k, size) if k else part
    keep, *met_images = far(keep, *[met_images[k] for k in range(chips)])
    base, scale = count_planes(
        class_weight, inv_noise, orientations, slabs * local_planes, slabs
    )
    tables, bit = [table], 1
    while bit < slabs:
        held = tables[0]
        if len(tables) > 1:
            held = jnp.concatenate(tables, axis=1)
        pairs = [(one, one ^ bit) for one in range(slabs)]
        tables = [held, lax.ppermute(held, "slab", pairs)]
        bit *= 2
    got = swap(give, 1, size)
    own_w, both_w = weigh(base, scale, tables, classes * local_planes)
    sib_w = swap(own_w, 1, size)

    sums = functools.partial(
        partial_sums, own_w=own_w, sib_w=sib_w, keep=keep, got=got, wide=wide,
    )
    low = [1 << place for place in range(chips.bit_length() - 1)]
    orders = (low, low[::-1])
    first = [[k for k in range(chips) if k & order[0]] for order in orders]
    onward = [[k for k in ks if k & order[1]] for ks, order in zip(first, orders)]
    direct = [[k for k in ks if not k & order[1]] for ks, order in zip(first, orders)]
    stay = [[k for k in range(chips) if not k & order[0]] for order in orders]
    parts = [{k: [] for k in ks} for ks in stay]

    def deliver(side, ks, array, bit):
        arrived = swap(array, 2 * bit, size)
        for place, k in enumerate(ks):
            parts[side][k ^ bit].append((arrived, place))
        return arrived

    def compute(groups, relay=()):
        return sums(tuple(tuple(ks) for ks in groups), relay=relay)

    items = tuple((side, k) for side, ks in enumerate(onward) for k in ks)
    sent = first_sums(items, own_w, sib_w, both_w, gather_images(items, keep, got, wide))
    arrived = [swap(sent[side], 2 * orders[side][0], size) for side in (0, 1)]
    both_w, _ = lax.optimization_barrier((both_w, sent[1]))
    others = [k for k in range(1, chips) if k not in (orders[0][0], orders[1][0])]
    far_w = [swap(both_w, 2 * k, size) for k in others]
    sums.keywords["keep"], *met_images = lax.optimization_barrier((keep, *met_images))
    sent = compute(direct, (met_images[chips // 2],))
    relays = [deliver(side, direct[side], sent[side], orders[side][0]) for side in (0, 1)]
    kept = compute(stay)
    for side in (0, 1):
        for place, k in enumerate(stay[side]):
            parts[side][k].append((kept[side], place))

    met_images[0], _, *arrived = lax.optimization_barrier(
        (met_images[0], sent[0], *arrived, *far_w)
    )
    far_w = dict(zip(others, arrived[2:]))
    far_w[0] = both_w
    for side in (0, 1):
        bit = orders[side][0]
        far_w[bit] = arrived[side]
        for place, k in enumerate(onward[side]):
            parts[side][k ^ bit].append((arrived[side], place))
    weights = [far_w[k] for k in range(chips)]
    met, for_sib = meet(weights, met_images)
    tails = [relays[0] if k == relayed else met_images[k] for k in range(1, chips)]
    shells = shell_sums(ctf_table, weights, tails)
    sib_shells = swap(shells, 1, size)
    sib_met = swap(for_sib, 1, size)
    own_planes = classes * local_planes
    partner = lax.ppermute(
        met[own_planes:, :met_wide] + sib_met[own_planes:, :met_wide], "slab", [(one, one ^ 1) for one in range(slabs)]
    )

    for turn in range(1, len(low)):
        for side in (0, 1):
            bit = orders[side][turn]
            ks = [k for k in parts[side] if k & bit]
            sent = jnp.stack(
                [sum(part[place, :, :wide] for part, place in parts[side].pop(k)) for k in ks]
            )
            deliver(side, ks, sent, bit)
    base, scale = prepare(
        index, met, sib_met, shells, sib_shells, [parts[side][0][:-1] for side in (0, 1)], share
    )
    out = finish(base, scale, parts[0][0][-1][0], parts[1][0][-1][0], partner)
    return out.reshape(classes, local_planes, share)


def solution(mesh):
    return jax.shard_map(
        shards,
        mesh=mesh,
        in_specs=(
            P("img", None),
            P(None, "slab", None),
            P("img", None, None),
            P("img", None),
            P("img"),
            P(),
        ),
        out_specs=P(None, "slab", "img"),
        check_vma=False,
    )
```

```python
import functools
import math

import jax
import jax.numpy as jnp
import numpy as np
from jax import lax
from jax.experimental import pallas as pl
from jax.experimental.pallas import tpu as pltpu
from jax.sharding import PartitionSpec as P

F32 = jnp.float32
BF16 = jnp.bfloat16
LANES = 128
PIECE = 5 * LANES
MIB = 1024 * 1024


def entry_shells(width, shells):
    pixels = width // 2
    box = math.isqrt(pixels)
    place = np.arange(pixels)
    column = place % box - box // 2
    row = place // box - box // 2
    radius = column * column + row * row
    levels = np.arange(1, shells)
    shell = np.sum(2 * levels[None, :] ** 2 <= radius[:, None], axis=1)
    return np.repeat(shell, 2).astype(np.int32)[None, :]


def split_share(share):
    met = max(LANES, 6 * share // 32 // LANES * LANES)
    return share // 2 - met, met


def met_column(share, owner, slab):
    wide, met = split_share(share)
    return pl.multiple_of(owner * share + 2 * wide + lax.rem(slab, 2) * met, LANES)


def params(mib):
    return pltpu.CompilerParams(vmem_limit_bytes=mib * MIB)


def lanes_wide(table):
    rows, shells = table.shape
    if shells == LANES:
        return table
    return jnp.concatenate([table, jnp.zeros((rows, LANES - shells), table.dtype)], axis=1)


def spread(table, index):
    return jnp.take_along_axis(table, jnp.broadcast_to(index, table.shape), axis=1)


def contract_last(left, right):
    return lax.dot_general(left, right, (((1,), (1,)), ((), ())), preferred_element_type=F32)


def estep_kernel(
    blocks, share, near, index_hbm, image_hbm, plane_hbm, ctf_hbm, *refs,
):
    give_hbm, keep_hbm, score_ref = refs[:3]
    near_refs = refs[3 : 3 + len(near)]
    index, image, plane, ctf_held, weighted, give, squared, energy_of = refs[-11:-3]
    small_sem, in_sem, out_sem = refs[-3:]
    rows, width = image.shape
    wide, met = split_share(share)
    chips, summed = width // share // 2, 2 * wide
    box = math.isqrt(width // 2)
    line = 2 * box
    deep = box // (2 * blocks)
    span = deep * line

    small = [
        pltpu.make_async_copy(index_hbm, index, small_sem.at[0]),
        pltpu.make_async_copy(ctf_hbm, ctf_held, small_sem.at[1]),
    ]
    incoming = []
    for block in range(blocks):
        copies = []
        for side, start in enumerate((block * span, width - (block + 1) * span)):
            cut = pl.ds(start, span)
            copies += [
                pltpu.make_async_copy(
                    image_hbm.at[:, cut], image.at[:, cut], in_sem.at[block, side, 0]
                ),
                pltpu.make_async_copy(
                    plane_hbm.at[:, cut], plane.at[:, cut], in_sem.at[block, side, 1]
                ),
            ]
        incoming.append(copies)
    for copy in small + [copy for copies in incoming for copy in copies]:
        copy.start()
    for copy in small:
        copy.wait()
    table = lanes_wide(ctf_held[...])

    def weigh_image(cut, ctf):
        weighted[:, cut] = (image[:, cut].astype(F32) * ctf).astype(BF16)

    def square(cut):
        part = plane[:, cut].astype(F32)
        return part * part

    def expand(row, slot, place):
        mirror = box - row if 0 < row < box // 2 else None
        for start in range(0, line, LANES):
            cut = slice(row * line + start, row * line + start + LANES)
            ctf = spread(table, index[:, cut])
            weigh_image(cut, ctf)
            power = square(cut)
            if mirror is not None:
                other = slice(mirror * line + start, mirror * line + start + LANES)
                weigh_image(other, ctf)
                power += square(other)
            held = slice(place + start, place + start + LANES)
            squared[slot, :, held] = (ctf * ctf).astype(BF16)
            energy_of[slot, :, held] = power.astype(BF16)

    def fit(start, stop):
        return contract_last(weighted[:, start:stop], plane[:, start:stop])

    def energy(slot, size):
        return contract_last(squared[slot, :, :size], energy_of[slot, :, :size])

    def block_table(block):
        low, high = fit(block * span, (block + 1) * span), width - block * span
        stop = high + line if block else high
        low += fit(high - span + line, stop)
        return 2.0 * low - energy(block % 2, span)

    chip, core = lax.axis_index("img") // 2, lax.rem(lax.axis_index("img"), 2)
    outgoing = []

    def hand_over(done):
        for pair in range(chips):
            first, last = 2 * pair * share // line, -(-2 * (pair + 1) * share // line)
            if pair in handed or not all(row in done for row in range(first, last)):
                continue
            handed.add(pair)
            place = pair ^ chip
            given = pl.ds(pl.multiple_of((2 * pair + 1 - core) * share, share), summed)
            kept = pl.ds(pl.multiple_of((2 * pair + core) * share, share), summed)
            at = pl.ds(pl.multiple_of(place * summed, LANES), summed)
            give[:, at] = weighted[:, given].astype(F32)
            outgoing.extend([
                pltpu.make_async_copy(give.at[:, at], give_hbm.at[:, at], out_sem.at[pair, 0]),
                pltpu.make_async_copy(weighted.at[:, kept], keep_hbm.at[:, at], out_sem.at[pair, 1]),
            ])
            outgoing[-2].start()
            outgoing[-1].start()

    handed, done = set(), set()
    total = jnp.zeros(score_ref.shape, F32)
    for block in range(blocks):
        for copy in incoming[block]:
            copy.wait()
        for row in range(block * deep, (block + 1) * deep):
            expand(row, block % 2, (row - block * deep) * line)
            done |= {row, box - row}
        if block == blocks - 1:
            expand(box // 2, 2, 0)
            done.add(box // 2)
        if block:
            total += block_table(block - 1)
        hand_over(done)
    total += block_table(blocks - 1)
    middle = width // 2
    total += 2.0 * fit(middle, middle + line) - energy(2, line)
    score_ref[...] = total
    for k, near_ref in zip(near, near_refs):
        for other in range(2):
            owner = (k ^ chip) * 2 + lax.rem(core + other, 2)
            part = weighted[:, pl.ds(met_column(share, owner, lax.axis_index("slab")), met)]
            near_ref[:, other * met : (other + 1) * met] = part.astype(near_ref.dtype)
        if k:
            near_ref[:, 2 * met :] = table
    for copy in outgoing:
        copy.wait()


def far(*operands):
    return [pltpu.with_memory_space_constraint(operand, pltpu.HBM) for operand in operands]


def estep(index, images, planes, ctf_table, share, near):
    rows, width = images.shape
    chips = width // share // 2
    wide, met = split_share(share)
    summed = 2 * wide
    count = planes.shape[0]
    blocks = 4
    span = width // (2 * blocks)
    held = pl.BlockSpec(memory_space=pl.ANY)
    vmem = pl.BlockSpec(memory_space=pltpu.VMEM)
    hbm = pl.BlockSpec(memory_space=pltpu.HBM)
    return pl.pallas_call(
        functools.partial(estep_kernel, blocks, share, near),
        in_specs=[hbm] * 4,
        out_specs=[held, held] + [vmem] * (1 + len(near)),
        out_shape=[
            jax.ShapeDtypeStruct((rows, chips * summed), F32),
            pltpu.HBM((rows, chips * summed), BF16),
            jax.ShapeDtypeStruct((rows, count), F32),
        ]
        + [
            jax.ShapeDtypeStruct((rows, 2 * met + LANES), F32)
            if k
            else pltpu.HBM((rows, 2 * met), BF16)
            for k in near
        ],
        scratch_shapes=[
            pltpu.VMEM(index.shape, jnp.int32),
            pltpu.VMEM((rows, width), BF16),
            pltpu.VMEM((count, width), BF16),
            pltpu.VMEM(ctf_table.shape, F32),
            pltpu.VMEM((rows, width), BF16),
            pltpu.VMEM((rows, chips * summed), F32),
            pltpu.VMEM((3, rows, span), BF16),
            pltpu.VMEM((3, count, span), BF16),
            pltpu.SemaphoreType.DMA((2,)),
            pltpu.SemaphoreType.DMA((blocks, 2, 2)),
            pltpu.SemaphoreType.DMA((chips, 2)),
        ],
        compiler_params=params(28),
        name="estep",
    )(*far(index, images, planes, ctf_table))


def early_kernel(share, beyond, index_hbm, image_hbm, ctf_hbm, *refs):
    outs = refs[: len(beyond)]
    index, image, ctf_held, index_sem, image_sem, ctf_sem = refs[len(beyond) :]
    met = split_share(share)[1]
    chip, core = lax.axis_index("img") // 2, lax.rem(lax.axis_index("img"), 2)
    fetch = pltpu.make_async_copy(ctf_hbm, ctf_held, ctf_sem)
    fetch.start()
    copies = []
    for place, k in enumerate(beyond):
        for other in range(2):
            owner = (k ^ chip) * 2 + lax.rem(core + other, 2)
            cut = pl.ds(met_column(share, owner, lax.axis_index("slab")), met)
            copies.append([
                pltpu.make_async_copy(
                    index_hbm.at[:, cut], index.at[place, other], index_sem.at[place, other]
                ),
                pltpu.make_async_copy(
                    image_hbm.at[:, cut], image.at[place, other], image_sem.at[place, other]
                ),
            ])
            for copy in copies[-1]:
                copy.start()
    fetch.wait()
    table = lanes_wide(ctf_held[...])
    for place, out_ref in enumerate(outs):
        for other in range(2):
            for copy in copies[2 * place + other]:
                copy.wait()
            for start in range(0, met, LANES):
                cut = slice(start, start + LANES)
                ctf = spread(table, index[place, other, :, cut])
                part = (image[place, other, :, cut].astype(F32) * ctf).astype(BF16)
                out_ref[:, other * met + start : other * met + start + LANES] = part.astype(F32)
        if out_ref.shape[1] > 2 * met:
            out_ref[:, 2 * met :] = table


def early_images(index, images, ctf_table, share, beyond, relayed):
    rows = images.shape[0]
    met = split_share(share)[1]
    number = len(beyond)
    vmem = pl.BlockSpec(memory_space=pltpu.VMEM)
    hbm = pl.BlockSpec(memory_space=pltpu.HBM)
    return pl.pallas_call(
        functools.partial(early_kernel, share, beyond),
        in_specs=[hbm, hbm, hbm],
        out_specs=[vmem] * number,
        out_shape=[
            jax.ShapeDtypeStruct((rows, 2 * met + LANES * (k != relayed)), F32) for k in beyond
        ],
        scratch_shapes=[
            pltpu.VMEM((number, 2, 1, met), jnp.int32),
            pltpu.VMEM((number, 2, rows, met), BF16),
            pltpu.VMEM(ctf_table.shape, F32),
            pltpu.SemaphoreType.DMA((number, 2)),
            pltpu.SemaphoreType.DMA((number, 2)),
            pltpu.SemaphoreType.DMA(()),
        ],
        compiler_params=params(12),
        name="early",
    )(*far(index, images, ctf_table))


def count_kernel(slabs, prior_ref, noise_ref, list_ref, base_ref, scale_ref):
    rows, listed = list_ref.shape
    classes, _, width = base_ref.shape
    each = listed // classes
    local = width // slabs
    lane = lax.broadcasted_iota(jnp.int32, (rows, width), 1)
    home = lax.axis_index("slab") ^ (lane // local)
    plane = home * local + lax.rem(lane, local)
    for one in range(classes):
        sums = jnp.zeros((rows, width), F32)
        for entry in range(each):
            place = one * each + entry
            sums += jnp.where(list_ref[:, place : place + 1] == plane, 1.0, 0.0)
        base_ref[one] = jnp.where(sums > 0.0, jnp.log(sums) + jnp.log(prior_ref[:, one : one + 1]), -jnp.inf)
    noise = jnp.broadcast_to(noise_ref[...], (rows, rows))
    diagonal = lax.broadcasted_iota(jnp.int32, (rows, rows), 0) == lax.broadcasted_iota(
        jnp.int32, (rows, rows), 1
    )
    column = jnp.sum(jnp.where(diagonal, noise, 0.0), axis=1, keepdims=True)
    scale_ref[...] = jnp.broadcast_to(column, (rows, width))


def count_planes(class_weight, inv_noise, orientations, width, slabs):
    rows, classes, each = orientations.shape
    vmem = pl.BlockSpec(memory_space=pltpu.VMEM)
    return pl.pallas_call(
        functools.partial(count_kernel, slabs),
        in_specs=[vmem] * 3,
        out_specs=[vmem, vmem],
        out_shape=[
            jax.ShapeDtypeStruct((classes, rows, width), F32),
            jax.ShapeDtypeStruct((rows, width), F32),
        ],
        compiler_params=params(4),
        name="count",
    )(
        class_weight.reshape(1, classes),
        inv_noise.reshape(1, rows),
        orientations.reshape(rows, classes * each),
    )


def weigh_kernel(base_ref, scale_ref, *refs):
    table_refs, (own_ref, both_ref) = refs[:-2], refs[-2:]
    classes = base_ref.shape[0]
    planes = own_ref.shape[0]
    local = planes // classes
    scores = []
    for one in range(classes):
        parts = [
            ref[:, start + one * local : start + (one + 1) * local]
            for ref in table_refs
            for start in range(0, ref.shape[1], planes)
        ]
        scores.append(base_ref[one] + scale_ref[...] * jnp.concatenate(parts, axis=1))
    peak = functools.reduce(jnp.maximum, [jnp.max(score, axis=1, keepdims=True) for score in scores])
    raw = [jnp.exp(score - peak) for score in scores]
    total = functools.reduce(jnp.add, [jnp.sum(part, axis=1, keepdims=True) for part in raw])
    slabs = [
        jnp.concatenate([part[:, place * local : (place + 1) * local] for part in raw], axis=1) / total
        for place in range(2)
    ]
    own_ref[...] = slabs[0].T
    both_ref[...] = jnp.concatenate(slabs, axis=1)


def weigh(base, scale, tables, planes):
    rows = base.shape[1]
    return pl.pallas_call(
        weigh_kernel,
        out_shape=[
            jax.ShapeDtypeStruct((planes, rows), F32),
            jax.ShapeDtypeStruct((rows, 2 * planes), F32),
        ],
        compiler_params=params(4),
        name="weigh",
    )(base, scale, *tables)


def gather_kernel(items, keep_hbm, got_hbm, out_ref, got, in_sem):
    number, rows2, wide = out_ref.shape
    rows = rows2 // 2
    incoming = []
    for place, (side, k) in enumerate(items):
        cut = slice((2 * k + side) * wide, (2 * k + side + 1) * wide)
        incoming.append([
            pltpu.make_async_copy(keep_hbm.at[:, cut], out_ref.at[place, :rows], in_sem.at[place, 0]),
            pltpu.make_async_copy(got_hbm.at[:, cut], got.at[place], in_sem.at[place, 1]),
        ])
        for copy in incoming[-1]:
            copy.start()
    for place in range(number):
        for copy in incoming[place]:
            copy.wait()
        out_ref[place, rows:] = got[place].astype(BF16)


def gather_images(items, keep, got, wide):
    rows = keep.shape[0]
    number = len(items)
    held = pl.BlockSpec(memory_space=pl.ANY)
    return pl.pallas_call(
        functools.partial(gather_kernel, items),
        in_specs=[held] * 2,
        out_specs=pl.BlockSpec(memory_space=pltpu.VMEM),
        out_shape=jax.ShapeDtypeStruct((number, 2 * rows, wide), BF16),
        scratch_shapes=[
            pltpu.VMEM((number, rows, wide), F32),
            pltpu.SemaphoreType.DMA((number, 2)),
        ],
        compiler_params=params(8),
        name="gather",
    )(keep, got)


def first_sums_kernel(items, own_w_ref, sib_w_ref, both_w_ref, image_ref, *outs):
    wide = image_ref.shape[2]
    weights = jnp.concatenate([own_w_ref[...], sib_w_ref[...]], axis=1).astype(BF16)
    slots = [0] * len(outs)
    for place, (side, _) in enumerate(items):
        out_ref, slot = outs[side], slots[side]
        slots[side] += 1
        out_ref[slot, :, :wide] = jnp.dot(weights, image_ref[place], preferred_element_type=F32)
        out_ref[slot, :, wide:] = both_w_ref[...]


def first_sums(items, own_w, sib_w, both_w, images):
    planes = own_w.shape[0]
    wide = images.shape[2]
    vmem = pl.BlockSpec(memory_space=pltpu.VMEM)
    return pl.pallas_call(
        functools.partial(first_sums_kernel, items),
        in_specs=[vmem] * 4,
        out_specs=[vmem] * 2,
        out_shape=[
            jax.ShapeDtypeStruct(
                (sum(side == one for side, _ in items), planes, wide + both_w.shape[1]), F32
            )
            for one in (0, 1)
        ],
        compiler_params=params(8),
        name="first_sums",
    )(own_w, sib_w, both_w, images)


def sums_kernel(items, relay, own_w_ref, sib_w_ref, keep_hbm, got_hbm, *refs):
    if relay:
        ctf_hbm, refs = refs[0], refs[1:]
    outs = refs[: len(items)]
    keep, got, in_sem = refs[len(items) : len(items) + 3]
    number, _, wide = keep.shape
    places = [(slot, k, side) for side, ks in enumerate(items) for slot, k in enumerate(ks)]
    incoming = []
    for place, (slot, k, side) in enumerate(places):
        source = slice((2 * k + side) * wide, (2 * k + side + 1) * wide)
        incoming.append([
            pltpu.make_async_copy(keep_hbm.at[:, source], keep.at[place], in_sem.at[place, 0]),
            pltpu.make_async_copy(got_hbm.at[:, source], got.at[place], in_sem.at[place, 1]),
        ])
        for copy in incoming[-1]:
            copy.start()
    if relay:
        ctf, ctf_sem = refs[-2:]
        fetch = pltpu.make_async_copy(ctf_hbm.at[:, ctf_hbm.shape[1] - LANES :], ctf, ctf_sem)
        fetch.start()
    weights = jnp.concatenate([own_w_ref[...], sib_w_ref[...]], axis=1).astype(BF16)
    for place, (slot, k, side) in enumerate(places):
        for copy in incoming[place]:
            copy.wait()
        images = jnp.concatenate([keep[place], got[place].astype(BF16)], axis=0)
        outs[side][slot, :, :wide] = jnp.dot(weights, images, preferred_element_type=F32)
    if relay:
        fetch.wait()
        for slot in range(outs[0].shape[0]):
            outs[0][slot, :, wide:] = ctf[...]


def partial_sums(items, own_w, sib_w, keep, got, wide, relay=()):
    rows = keep.shape[0]
    planes = own_w.shape[0]
    number = sum(len(ks) for ks in items)
    held = pl.BlockSpec(memory_space=pl.ANY)
    vmem = pl.BlockSpec(memory_space=pltpu.VMEM)
    return pl.pallas_call(
        functools.partial(sums_kernel, items, bool(relay)),
        in_specs=[vmem] * 2 + [held] * (2 + len(relay)),
        out_specs=[vmem] * 2,
        out_shape=[
            jax.ShapeDtypeStruct((len(ks), planes, wide + extra), F32)
            for ks, extra in zip(items, (LANES * len(relay), 0))
        ],
        scratch_shapes=[
            pltpu.VMEM((number, rows, wide), BF16),
            pltpu.VMEM((number, rows, wide), F32),
            pltpu.SemaphoreType.DMA((number, 2)),
        ]
        + [pltpu.VMEM((rows, LANES), F32), pltpu.SemaphoreType.DMA(())] * len(relay),
        compiler_params=params(12),
        name="sums",
    )(own_w, sib_w, keep, got, *relay)


def meet_kernel(chips, *refs):
    weight_refs, image_refs, outs = refs[:chips], refs[chips : 2 * chips], refs[2 * chips :]
    planes, met = outs[0].shape
    weights = []
    for ref in weight_refs:
        wide = ref.shape[-1]
        part = ref[:, wide - planes :] if len(ref.shape) == 2 else ref[0, :, wide - planes :]
        weights.append(part.astype(BF16))
    weights = jnp.concatenate(weights, axis=0)
    for other, out_ref in enumerate(outs):
        cut = slice(other * met, (other + 1) * met)
        images = jnp.concatenate([ref[:, cut].astype(BF16) for ref in image_refs], axis=0)
        out_ref[...] = lax.dot_general(
            weights, images, (((0,), (0,)), ((), ())), preferred_element_type=F32
        )


def meet(weights, images):
    met = images[0].shape[1] // 2
    planes = weights[0].shape[1]
    return pl.pallas_call(
        functools.partial(meet_kernel, len(weights)),
        out_shape=[jax.ShapeDtypeStruct((planes, met), F32)] * 2,
        compiler_params=params(16),
        name="meet",
    )(*weights, *images)


def shells_kernel(chips, ctf_ref, *refs):
    weight_refs, tail_refs, out_ref = refs[:chips], refs[chips:-1], refs[-1]
    planes = out_ref.shape[0]
    weights = []
    for ref in weight_refs:
        cut = slice(ref.shape[-1] - 2 * planes, ref.shape[-1] - planes)
        weights.append((ref[:, cut] if len(ref.shape) == 2 else ref[0, :, cut]).astype(BF16))
    ctf = [lanes_wide(ctf_ref[...])]
    ctf += [ref[...] if len(ref.shape) == 2 else ref[0] for ref in tail_refs]
    squares = jnp.concatenate([(part * part).astype(BF16) for part in ctf], axis=0)
    out_ref[...] = lax.dot_general(
        jnp.concatenate(weights, axis=0), squares, (((0,), (0,)), ((), ())), preferred_element_type=F32
    )


def shell_sums(ctf_table, weights, tails):
    rows = ctf_table.shape[0]
    planes = weights[0].shape[1] // 2

    def whole(array):
        return pl.BlockSpec(array.shape, lambda step: (0,) * len(array.shape))

    def last(array):
        place = array.shape[-1] // LANES - 1
        if len(array.shape) == 2:
            return pl.BlockSpec((rows, LANES), lambda step: (0, place))
        return pl.BlockSpec((1, rows, LANES), lambda step: (0, 0, place))

    return pl.pallas_call(
        functools.partial(shells_kernel, len(weights)),
        grid=(1,),
        in_specs=[whole(ctf_table)] + [whole(part) for part in weights] + [last(part) for part in tails],
        out_specs=pl.BlockSpec((planes, LANES), lambda step: (0, 0)),
        out_shape=jax.ShapeDtypeStruct((planes, LANES), F32),
        compiler_params=params(8),
        name="shells",
    )(ctf_table, *weights, *tails)


def prepare_kernel(places, index_hbm, met_ref, sib_met_ref, shell_ref, sib_shell_ref, *refs):
    total = sum(map(len, places))
    parts, (base_ref, scale_ref, index, in_sem) = refs[:total], refs[total:]
    planes, share = base_ref.shape
    wide, met = split_share(share)
    mine = pl.ds(pl.multiple_of(lax.axis_index("img") * share, share), share)
    fetch = pltpu.make_async_copy(index_hbm.at[:, mine], index, in_sem)
    fetch.start()
    start = 0
    for side, numbers in enumerate(places):
        refs = list(zip(parts[start : start + len(numbers)], numbers))
        start += len(numbers)
        base_ref[:, side * wide : (side + 1) * wide] = functools.reduce(
            jnp.add, [ref[place, :, :wide] for ref, place in refs]
        )
    half = lax.rem(lax.axis_index("slab"), 2)
    own = pl.ds(pl.multiple_of(2 * wide + half * met, LANES), met)
    other = pl.ds(pl.multiple_of(2 * wide + (1 - half) * met, LANES), met)
    base_ref[:, own] = met_ref[:planes, :met] + sib_met_ref[:planes, :met]
    base_ref[:, other] = jnp.zeros((planes, met), F32)
    shells = shell_ref[...] + sib_shell_ref[...]
    fetch.wait()
    for start in range(0, share, LANES):
        cut = slice(start, start + LANES)
        scale = 1.0 / (spread(shells, index[:, cut]) + 1.0)
        scale_ref[:, cut] = scale
        base_ref[:, cut] = base_ref[:, cut] * scale


def prepare(index, met, sib_met, shells, sib_shells, sides, share):
    planes = met.shape[0] // 2
    held = pl.BlockSpec(memory_space=pl.ANY)
    vmem = pl.BlockSpec(memory_space=pltpu.VMEM)
    places = [[place for _, place in side] for side in sides]
    parts = [part for side in sides for part, _ in side]
    return pl.pallas_call(
        functools.partial(prepare_kernel, places),
        in_specs=[held] + [vmem] * (4 + len(parts)),
        out_specs=[vmem, vmem],
        out_shape=[jax.ShapeDtypeStruct((planes, share), F32)] * 2,
        scratch_shapes=[pltpu.VMEM((1, share), jnp.int32), pltpu.SemaphoreType.DMA(())],
        compiler_params=params(8),
        name="prepare",
    )(index, met, sib_met, shells, sib_shells, *parts)


def finish_kernel(base_ref, scale_ref, left_ref, right_ref, partner_ref, out_hbm, out, out_sem):
    planes, share = out.shape
    wide, met = split_share(share)
    half = lax.rem(lax.axis_index("slab"), 2)
    own = pl.multiple_of(2 * wide + half * met, LANES)
    other = pl.multiple_of(2 * wide + (1 - half) * met, LANES)

    def scaled(place, size, last):
        for start in range(0, size, LANES):
            at = pl.ds(pl.multiple_of(place + start, LANES), LANES)
            out[:, at] = base_ref[:, at] + last(slice(start, start + LANES)) * scale_ref[:, at]

    stores = []

    def scale_and_store(place, size, last):
        for first in range(0, size, PIECE):
            piece = min(PIECE, size - first)
            scaled(place + first, piece, lambda cut: last(slice(cut.start + first, cut.stop + first)))
            cut = pl.ds(pl.multiple_of(place + first, LANES), piece)
            stores.append(
                pltpu.make_async_copy(out.at[:, cut], out_hbm.at[:, cut], out_sem.at[len(stores)])
            )
            stores[-1].start()

    cut = pl.ds(own, met)
    stores.append(
        pltpu.make_async_copy(base_ref.at[:, cut], out_hbm.at[:, cut], out_sem.at[len(stores)])
    )
    stores[-1].start()
    scale_and_store(other, met, lambda cut: partner_ref[:, cut])
    scale_and_store(0, wide, lambda cut: left_ref[0, :, cut])
    scale_and_store(wide, wide, lambda cut: right_ref[0, :, cut])
    for copy in stores:
        copy.wait()


def finish(base, scale, left, right, partner):
    wide, met = split_share(base.shape[1])
    pieces = 2 * (pl.cdiv(wide, PIECE) + pl.cdiv(met, PIECE))
    vmem = pl.BlockSpec(memory_space=pltpu.VMEM)
    return pl.pallas_call(
        finish_kernel,
        in_specs=[vmem] * 5,
        out_specs=pl.BlockSpec(memory_space=pl.ANY),
        out_shape=jax.ShapeDtypeStruct(base.shape, F32),
        scratch_shapes=[pltpu.VMEM(base.shape, F32), pltpu.SemaphoreType.DMA((pieces,))],
        compiler_params=params(8),
        name="finish",
    )(base, scale, left, right, partner)


def swap(array, bit, size):
    return lax.ppermute(array, "img", [(one, one ^ bit) for one in range(size)])


def shards(images, references, orientations, ctf_table, inv_noise, class_weight):
    rows, width = images.shape
    classes, local_planes, _ = references.shape
    size = lax.axis_size("img")
    slabs = lax.axis_size("slab")
    chips = size // 2
    share = width // size
    wide, met_wide = split_share(share)
    index = entry_shells(width, ctf_table.shape[1])
    top_index = jnp.asarray(index[:, : width // 2 + 2 * math.isqrt(width // 2)])
    index = jnp.asarray(index)
    planes = references.reshape(classes * local_planes, width)

    beyond = tuple(k for k in range(chips) if k & (k - 1))
    near = tuple(k for k in range(chips) if k not in beyond)
    relayed = 1 | chips // 2
    met_images = {}
    if beyond:
        early = early_images(index, images, ctf_table, share, beyond, relayed)
        images, *early = lax.optimization_barrier((images, *early))
        met_images = {k: swap(part, 2 * k, size) for k, part in zip(beyond, early)}
    give, keep, table, *parts_near = estep(
        top_index, images, planes, ctf_table, share, near
    )
    if beyond:
        give, keep, met_images[beyond[-1]], *parts_near = lax.optimization_barrier(
            (give, keep, met_images[beyond[-1]], *parts_near)
        )
    for k, part in zip(near, parts_near):
        met_images[k] = swap(part, 2 * k, size) if k else part
    keep, *met_images = far(keep, *[met_images[k] for k in range(chips)])
    base, scale = count_planes(
        class_weight, inv_noise, orientations, slabs * local_planes, slabs
    )
    tables, bit = [table], 1
    while bit < slabs:
        held = tables[0]
        if len(tables) > 1:
            held = jnp.concatenate(tables, axis=1)
        pairs = [(one, one ^ bit) for one in range(slabs)]
        tables = [held, lax.ppermute(held, "slab", pairs)]
        bit *= 2
    got = swap(give, 1, size)
    own_w, both_w = weigh(base, scale, tables, classes * local_planes)
    sib_w = swap(own_w, 1, size)

    sums = functools.partial(
        partial_sums, own_w=own_w, sib_w=sib_w, keep=keep, got=got, wide=wide,
    )
    low = [1 << place for place in range(chips.bit_length() - 1)]
    orders = (low, low[::-1])
    first = [[k for k in range(chips) if k & order[0]] for order in orders]
    onward = [[k for k in ks if k & order[1]] for ks, order in zip(first, orders)]
    direct = [[k for k in ks if not k & order[1]] for ks, order in zip(first, orders)]
    stay = [[k for k in range(chips) if not k & order[0]] for order in orders]
    parts = [{k: [] for k in ks} for ks in stay]

    def deliver(side, ks, array, bit):
        arrived = swap(array, 2 * bit, size)
        for place, k in enumerate(ks):
            parts[side][k ^ bit].append((arrived, place))
        return arrived

    def compute(groups, relay=()):
        return sums(tuple(tuple(ks) for ks in groups), relay=relay)

    items = tuple((side, k) for side, ks in enumerate(onward) for k in ks)
    sent = first_sums(items, own_w, sib_w, both_w, gather_images(items, keep, got, wide))
    arrived = [swap(sent[side], 2 * orders[side][0], size) for side in (0, 1)]
    both_w, _ = lax.optimization_barrier((both_w, sent[1]))
    others = [k for k in range(1, chips) if k not in (orders[0][0], orders[1][0])]
    far_w = [swap(both_w, 2 * k, size) for k in others]
    sums.keywords["keep"], *met_images = lax.optimization_barrier((keep, *met_images))
    sent = compute(direct, (met_images[chips // 2],))
    relays = [deliver(side, direct[side], sent[side], orders[side][0]) for side in (0, 1)]
    kept = compute(stay)
    for side in (0, 1):
        for place, k in enumerate(stay[side]):
            parts[side][k].append((kept[side], place))

    met_images[0], _, *arrived = lax.optimization_barrier(
        (met_images[0], sent[0], *arrived, *far_w)
    )
    far_w = dict(zip(others, arrived[2:]))
    far_w[0] = both_w
    for side in (0, 1):
        bit = orders[side][0]
        far_w[bit] = arrived[side]
        for place, k in enumerate(onward[side]):
            parts[side][k ^ bit].append((arrived[side], place))
    weights = [far_w[k] for k in range(chips)]
    met, for_sib = meet(weights, met_images)
    tails = [relays[0] if k == relayed else met_images[k] for k in range(1, chips)]
    shells = shell_sums(ctf_table, weights, tails)
    sib_shells = swap(shells, 1, size)
    sib_met = swap(for_sib, 1, size)
    own_planes = classes * local_planes
    partner = lax.ppermute(
        met[own_planes:, :met_wide] + sib_met[own_planes:, :met_wide], "slab", [(one, one ^ 1) for one in range(slabs)]
    )

    for turn in range(1, len(low)):
        for side in (0, 1):
            bit = orders[side][turn]
            ks = [k for k in parts[side] if k & bit]
            sent = jnp.stack(
                [sum(part[place, :, :wide] for part, place in parts[side].pop(k)) for k in ks]
            )
            deliver(side, ks, sent, bit)
    base, scale = prepare(
        index, met, sib_met, shells, sib_shells, [parts[side][0][:-1] for side in (0, 1)], share
    )
    out = finish(base, scale, parts[0][0][-1][0], parts[1][0][-1][0], partner)
    return out.reshape(classes, local_planes, share)


def solution(mesh):
    return jax.shard_map(
        shards,
        mesh=mesh,
        in_specs=(
            P("img", None),
            P(None, "slab", None),
            P("img", None, None),
            P("img", None),
            P("img"),
            P(),
        ),
        out_specs=P(None, "slab", "img"),
        check_vma=False,
    )
```

```python
import functools
import math

import jax
import jax.numpy as jnp
import numpy as np
from jax import lax
from jax.experimental import pallas as pl
from jax.experimental.pallas import tpu as pltpu
from jax.sharding import PartitionSpec as P

F32 = jnp.float32
BF16 = jnp.bfloat16
LANES = 128
PIECE = 3 * LANES
MIB = 1024 * 1024


def entry_shells(width, shells):
    pixels = width // 2
    box = math.isqrt(pixels)
    place = np.arange(pixels)
    column = place % box - box // 2
    row = place // box - box // 2
    radius = column * column + row * row
    levels = np.arange(1, shells)
    shell = np.sum(2 * levels[None, :] ** 2 <= radius[:, None], axis=1)
    return np.repeat(shell, 2).astype(np.int32)[None, :]


def split_share(share):
    met = max(LANES, 6 * share // 32 // LANES * LANES)
    return share // 2 - met, met


def met_column(share, owner, slab):
    wide, met = split_share(share)
    return pl.multiple_of(owner * share + 2 * wide + lax.rem(slab, 2) * met, LANES)


def params(mib):
    return pltpu.CompilerParams(vmem_limit_bytes=mib * MIB)


def lanes_wide(table):
    rows, shells = table.shape
    if shells == LANES:
        return table
    return jnp.concatenate([table, jnp.zeros((rows, LANES - shells), table.dtype)], axis=1)


def spread(table, index):
    return jnp.take_along_axis(table, jnp.broadcast_to(index, table.shape), axis=1)


def contract_last(left, right):
    return lax.dot_general(left, right, (((1,), (1,)), ((), ())), preferred_element_type=F32)


def estep_kernel(
    blocks, share, near, index_hbm, image_hbm, plane_hbm, ctf_hbm, *refs,
):
    give_hbm, keep_hbm, score_ref = refs[:3]
    near_refs = refs[3 : 3 + len(near)]
    index, image, plane, ctf_held, weighted, give, squared, energy_of = refs[-11:-3]
    small_sem, in_sem, out_sem = refs[-3:]
    rows, width = image.shape
    wide, met = split_share(share)
    chips, summed = width // share // 2, 2 * wide
    box = math.isqrt(width // 2)
    line = 2 * box
    deep = box // (2 * blocks)
    span = deep * line

    small = [
        pltpu.make_async_copy(index_hbm, index, small_sem.at[0]),
        pltpu.make_async_copy(ctf_hbm, ctf_held, small_sem.at[1]),
    ]
    incoming = []
    for block in range(blocks):
        copies = []
        for side, start in enumerate((block * span, width - (block + 1) * span)):
            cut = pl.ds(start, span)
            copies += [
                pltpu.make_async_copy(
                    image_hbm.at[:, cut], image.at[:, cut], in_sem.at[block, side, 0]
                ),
                pltpu.make_async_copy(
                    plane_hbm.at[:, cut], plane.at[:, cut], in_sem.at[block, side, 1]
                ),
            ]
        incoming.append(copies)
    for copy in small + [copy for copies in incoming for copy in copies]:
        copy.start()
    for copy in small:
        copy.wait()
    table = lanes_wide(ctf_held[...])

    def weigh_image(cut, ctf):
        weighted[:, cut] = (image[:, cut].astype(F32) * ctf).astype(BF16)

    def square(cut):
        part = plane[:, cut].astype(F32)
        return part * part

    def expand(row, slot, place):
        mirror = box - row if 0 < row < box // 2 else None
        for start in range(0, line, LANES):
            cut = slice(row * line + start, row * line + start + LANES)
            ctf = spread(table, index[:, cut])
            weigh_image(cut, ctf)
            power = square(cut)
            if mirror is not None:
                other = slice(mirror * line + start, mirror * line + start + LANES)
                weigh_image(other, ctf)
                power += square(other)
            held = slice(place + start, place + start + LANES)
            squared[slot, :, held] = (ctf * ctf).astype(BF16)
            energy_of[slot, :, held] = power.astype(BF16)

    def fit(start, stop):
        return contract_last(weighted[:, start:stop], plane[:, start:stop])

    def energy(slot, size):
        return contract_last(squared[slot, :, :size], energy_of[slot, :, :size])

    def block_table(block):
        low, high = fit(block * span, (block + 1) * span), width - block * span
        stop = high + line if block else high
        low += fit(high - span + line, stop)
        return 2.0 * low - energy(block % 2, span)

    chip, core = lax.axis_index("img") // 2, lax.rem(lax.axis_index("img"), 2)
    outgoing = []

    def hand_over(done):
        for pair in range(chips):
            first, last = 2 * pair * share // line, -(-2 * (pair + 1) * share // line)
            if pair in handed or not all(row in done for row in range(first, last)):
                continue
            handed.add(pair)
            place = pair ^ chip
            given = pl.ds(pl.multiple_of((2 * pair + 1 - core) * share, share), summed)
            kept = pl.ds(pl.multiple_of((2 * pair + core) * share, share), summed)
            at = pl.ds(pl.multiple_of(place * summed, LANES), summed)
            give[:, at] = weighted[:, given].astype(F32)
            outgoing.extend([
                pltpu.make_async_copy(give.at[:, at], give_hbm.at[:, at], out_sem.at[pair, 0]),
                pltpu.make_async_copy(weighted.at[:, kept], keep_hbm.at[:, at], out_sem.at[pair, 1]),
            ])
            outgoing[-2].start()
            outgoing[-1].start()

    handed, done = set(), set()
    total = jnp.zeros(score_ref.shape, F32)
    for block in range(blocks):
        for copy in incoming[block]:
            copy.wait()
        for row in range(block * deep, (block + 1) * deep):
            expand(row, block % 2, (row - block * deep) * line)
            done |= {row, box - row}
        if block == blocks - 1:
            expand(box // 2, 2, 0)
            done.add(box // 2)
        if block:
            total += block_table(block - 1)
        hand_over(done)
    total += block_table(blocks - 1)
    middle = width // 2
    total += 2.0 * fit(middle, middle + line) - energy(2, line)
    score_ref[...] = total
    for k, near_ref in zip(near, near_refs):
        for other in range(2):
            owner = (k ^ chip) * 2 + lax.rem(core + other, 2)
            part = weighted[:, pl.ds(met_column(share, owner, lax.axis_index("slab")), met)]
            near_ref[:, other * met : (other + 1) * met] = part.astype(near_ref.dtype)
        if k:
            near_ref[:, 2 * met :] = table
    for copy in outgoing:
        copy.wait()


def far(*operands):
    return [pltpu.with_memory_space_constraint(operand, pltpu.HBM) for operand in operands]


def estep(index, images, planes, ctf_table, share, near):
    rows, width = images.shape
    chips = width // share // 2
    wide, met = split_share(share)
    summed = 2 * wide
    count = planes.shape[0]
    blocks = 4
    span = width // (2 * blocks)
    held = pl.BlockSpec(memory_space=pl.ANY)
    vmem = pl.BlockSpec(memory_space=pltpu.VMEM)
    hbm = pl.BlockSpec(memory_space=pltpu.HBM)
    return pl.pallas_call(
        functools.partial(estep_kernel, blocks, share, near),
        in_specs=[hbm] * 4,
        out_specs=[held, held] + [vmem] * (1 + len(near)),
        out_shape=[
            jax.ShapeDtypeStruct((rows, chips * summed), F32),
            pltpu.HBM((rows, chips * summed), BF16),
            jax.ShapeDtypeStruct((rows, count), F32),
        ]
        + [
            jax.ShapeDtypeStruct((rows, 2 * met + LANES), F32)
            if k
            else pltpu.HBM((rows, 2 * met), BF16)
            for k in near
        ],
        scratch_shapes=[
            pltpu.VMEM(index.shape, jnp.int32),
            pltpu.VMEM((rows, width), BF16),
            pltpu.VMEM((count, width), BF16),
            pltpu.VMEM(ctf_table.shape, F32),
            pltpu.VMEM((rows, width), BF16),
            pltpu.VMEM((rows, chips * summed), F32),
            pltpu.VMEM((3, rows, span), BF16),
            pltpu.VMEM((3, count, span), BF16),
            pltpu.SemaphoreType.DMA((2,)),
            pltpu.SemaphoreType.DMA((blocks, 2, 2)),
            pltpu.SemaphoreType.DMA((chips, 2)),
        ],
        compiler_params=params(28),
        name="estep",
    )(*far(index, images, planes, ctf_table))


def early_kernel(share, beyond, index_hbm, image_hbm, ctf_hbm, *refs):
    outs = refs[: len(beyond)]
    index, image, ctf_held, index_sem, image_sem, ctf_sem = refs[len(beyond) :]
    met = split_share(share)[1]
    chip, core = lax.axis_index("img") // 2, lax.rem(lax.axis_index("img"), 2)
    fetch = pltpu.make_async_copy(ctf_hbm, ctf_held, ctf_sem)
    fetch.start()
    copies = []
    for place, k in enumerate(beyond):
        for other in range(2):
            owner = (k ^ chip) * 2 + lax.rem(core + other, 2)
            cut = pl.ds(met_column(share, owner, lax.axis_index("slab")), met)
            copies.append([
                pltpu.make_async_copy(
                    index_hbm.at[:, cut], index.at[place, other], index_sem.at[place, other]
                ),
                pltpu.make_async_copy(
                    image_hbm.at[:, cut], image.at[place, other], image_sem.at[place, other]
                ),
            ])
            for copy in copies[-1]:
                copy.start()
    fetch.wait()
    table = lanes_wide(ctf_held[...])
    for place, out_ref in enumerate(outs):
        for other in range(2):
            for copy in copies[2 * place + other]:
                copy.wait()
            for start in range(0, met, LANES):
                cut = slice(start, start + LANES)
                ctf = spread(table, index[place, other, :, cut])
                part = (image[place, other, :, cut].astype(F32) * ctf).astype(BF16)
                out_ref[:, other * met + start : other * met + start + LANES] = part.astype(F32)
        if out_ref.shape[1] > 2 * met:
            out_ref[:, 2 * met :] = table


def early_images(index, images, ctf_table, share, beyond, relayed):
    rows = images.shape[0]
    met = split_share(share)[1]
    number = len(beyond)
    vmem = pl.BlockSpec(memory_space=pltpu.VMEM)
    hbm = pl.BlockSpec(memory_space=pltpu.HBM)
    return pl.pallas_call(
        functools.partial(early_kernel, share, beyond),
        in_specs=[hbm, hbm, hbm],
        out_specs=[vmem] * number,
        out_shape=[
            jax.ShapeDtypeStruct((rows, 2 * met + LANES * (k != relayed)), F32) for k in beyond
        ],
        scratch_shapes=[
            pltpu.VMEM((number, 2, 1, met), jnp.int32),
            pltpu.VMEM((number, 2, rows, met), BF16),
            pltpu.VMEM(ctf_table.shape, F32),
            pltpu.SemaphoreType.DMA((number, 2)),
            pltpu.SemaphoreType.DMA((number, 2)),
            pltpu.SemaphoreType.DMA(()),
        ],
        compiler_params=params(12),
        name="early",
    )(*far(index, images, ctf_table))


def count_kernel(slabs, prior_ref, noise_ref, list_ref, base_ref, scale_ref):
    rows, listed = list_ref.shape
    classes, _, width = base_ref.shape
    each = listed // classes
    local = width // slabs
    lane = lax.broadcasted_iota(jnp.int32, (rows, width), 1)
    home = lax.axis_index("slab") ^ (lane // local)
    plane = home * local + lax.rem(lane, local)
    for one in range(classes):
        sums = jnp.zeros((rows, width), F32)
        for entry in range(each):
            place = one * each + entry
            sums += jnp.where(list_ref[:, place : place + 1] == plane, 1.0, 0.0)
        base_ref[one] = jnp.where(sums > 0.0, jnp.log(sums) + jnp.log(prior_ref[:, one : one + 1]), -jnp.inf)
    noise = jnp.broadcast_to(noise_ref[...], (rows, rows))
    diagonal = lax.broadcasted_iota(jnp.int32, (rows, rows), 0) == lax.broadcasted_iota(
        jnp.int32, (rows, rows), 1
    )
    column = jnp.sum(jnp.where(diagonal, noise, 0.0), axis=1, keepdims=True)
    scale_ref[...] = jnp.broadcast_to(column, (rows, width))


def count_planes(class_weight, inv_noise, orientations, width, slabs):
    rows, classes, each = orientations.shape
    vmem = pl.BlockSpec(memory_space=pltpu.VMEM)
    return pl.pallas_call(
        functools.partial(count_kernel, slabs),
        in_specs=[vmem] * 3,
        out_specs=[vmem, vmem],
        out_shape=[
            jax.ShapeDtypeStruct((classes, rows, width), F32),
            jax.ShapeDtypeStruct((rows, width), F32),
        ],
        compiler_params=params(4),
        name="count",
    )(
        class_weight.reshape(1, classes),
        inv_noise.reshape(1, rows),
        orientations.reshape(rows, classes * each),
    )


def weigh_kernel(base_ref, scale_ref, *refs):
    table_refs, (own_ref, both_ref) = refs[:-2], refs[-2:]
    classes = base_ref.shape[0]
    planes = own_ref.shape[0]
    local = planes // classes
    scores = []
    for one in range(classes):
        parts = [
            ref[:, start + one * local : start + (one + 1) * local]
            for ref in table_refs
            for start in range(0, ref.shape[1], planes)
        ]
        scores.append(base_ref[one] + scale_ref[...] * jnp.concatenate(parts, axis=1))
    peak = functools.reduce(jnp.maximum, [jnp.max(score, axis=1, keepdims=True) for score in scores])
    raw = [jnp.exp(score - peak) for score in scores]
    total = functools.reduce(jnp.add, [jnp.sum(part, axis=1, keepdims=True) for part in raw])
    slabs = [
        jnp.concatenate([part[:, place * local : (place + 1) * local] for part in raw], axis=1) / total
        for place in range(2)
    ]
    own_ref[...] = slabs[0].T
    both_ref[...] = jnp.concatenate(slabs, axis=1)


def weigh(base, scale, tables, planes):
    rows = base.shape[1]
    return pl.pallas_call(
        weigh_kernel,
        out_shape=[
            jax.ShapeDtypeStruct((planes, rows), F32),
            jax.ShapeDtypeStruct((rows, 2 * planes), F32),
        ],
        compiler_params=params(4),
        name="weigh",
    )(base, scale, *tables)


def gather_kernel(items, keep_hbm, got_hbm, out_ref, got, in_sem):
    number, rows2, wide = out_ref.shape
    rows = rows2 // 2
    incoming = []
    for place, (side, k) in enumerate(items):
        cut = slice((2 * k + side) * wide, (2 * k + side + 1) * wide)
        incoming.append([
            pltpu.make_async_copy(keep_hbm.at[:, cut], out_ref.at[place, :rows], in_sem.at[place, 0]),
            pltpu.make_async_copy(got_hbm.at[:, cut], got.at[place], in_sem.at[place, 1]),
        ])
        for copy in incoming[-1]:
            copy.start()
    for place in range(number):
        for copy in incoming[place]:
            copy.wait()
        out_ref[place, rows:] = got[place].astype(BF16)


def gather_images(items, keep, got, wide):
    rows = keep.shape[0]
    number = len(items)
    held = pl.BlockSpec(memory_space=pl.ANY)
    return pl.pallas_call(
        functools.partial(gather_kernel, items),
        in_specs=[held] * 2,
        out_specs=pl.BlockSpec(memory_space=pltpu.VMEM),
        out_shape=jax.ShapeDtypeStruct((number, 2 * rows, wide), BF16),
        scratch_shapes=[
            pltpu.VMEM((number, rows, wide), F32),
            pltpu.SemaphoreType.DMA((number, 2)),
        ],
        compiler_params=params(8),
        name="gather",
    )(keep, got)


def first_sums_kernel(items, own_w_ref, sib_w_ref, both_w_ref, image_ref, *outs):
    wide = image_ref.shape[2]
    weights = jnp.concatenate([own_w_ref[...], sib_w_ref[...]], axis=1).astype(BF16)
    slots = [0] * len(outs)
    for place, (side, _) in enumerate(items):
        out_ref, slot = outs[side], slots[side]
        slots[side] += 1
        out_ref[slot, :, :wide] = jnp.dot(weights, image_ref[place], preferred_element_type=F32)
        out_ref[slot, :, wide:] = both_w_ref[...]


def first_sums(items, own_w, sib_w, both_w, images):
    planes = own_w.shape[0]
    wide = images.shape[2]
    vmem = pl.BlockSpec(memory_space=pltpu.VMEM)
    return pl.pallas_call(
        functools.partial(first_sums_kernel, items),
        in_specs=[vmem] * 4,
        out_specs=[vmem] * 2,
        out_shape=[
            jax.ShapeDtypeStruct(
                (sum(side == one for side, _ in items), planes, wide + both_w.shape[1]), F32
            )
            for one in (0, 1)
        ],
        compiler_params=params(8),
        name="first_sums",
    )(own_w, sib_w, both_w, images)


def sums_kernel(items, relay, own_w_ref, sib_w_ref, keep_hbm, got_hbm, *refs):
    if relay:
        ctf_hbm, refs = refs[0], refs[1:]
    outs = refs[: len(items)]
    keep, got, in_sem = refs[len(items) : len(items) + 3]
    number, _, wide = keep.shape
    places = [(slot, k, side) for side, ks in enumerate(items) for slot, k in enumerate(ks)]
    incoming = []
    for place, (slot, k, side) in enumerate(places):
        source = slice((2 * k + side) * wide, (2 * k + side + 1) * wide)
        incoming.append([
            pltpu.make_async_copy(keep_hbm.at[:, source], keep.at[place], in_sem.at[place, 0]),
            pltpu.make_async_copy(got_hbm.at[:, source], got.at[place], in_sem.at[place, 1]),
        ])
        for copy in incoming[-1]:
            copy.start()
    if relay:
        ctf, ctf_sem = refs[-2:]
        fetch = pltpu.make_async_copy(ctf_hbm.at[:, ctf_hbm.shape[1] - LANES :], ctf, ctf_sem)
        fetch.start()
    weights = jnp.concatenate([own_w_ref[...], sib_w_ref[...]], axis=1).astype(BF16)
    for place, (slot, k, side) in enumerate(places):
        for copy in incoming[place]:
            copy.wait()
        images = jnp.concatenate([keep[place], got[place].astype(BF16)], axis=0)
        outs[side][slot, :, :wide] = jnp.dot(weights, images, preferred_element_type=F32)
    if relay:
        fetch.wait()
        for slot in range(outs[0].shape[0]):
            outs[0][slot, :, wide:] = ctf[...]


def partial_sums(items, own_w, sib_w, keep, got, wide, relay=()):
    rows = keep.shape[0]
    planes = own_w.shape[0]
    number = sum(len(ks) for ks in items)
    held = pl.BlockSpec(memory_space=pl.ANY)
    vmem = pl.BlockSpec(memory_space=pltpu.VMEM)
    return pl.pallas_call(
        functools.partial(sums_kernel, items, bool(relay)),
        in_specs=[vmem] * 2 + [held] * (2 + len(relay)),
        out_specs=[vmem] * 2,
        out_shape=[
            jax.ShapeDtypeStruct((len(ks), planes, wide + extra), F32)
            for ks, extra in zip(items, (LANES * len(relay), 0))
        ],
        scratch_shapes=[
            pltpu.VMEM((number, rows, wide), BF16),
            pltpu.VMEM((number, rows, wide), F32),
            pltpu.SemaphoreType.DMA((number, 2)),
        ]
        + [pltpu.VMEM((rows, LANES), F32), pltpu.SemaphoreType.DMA(())] * len(relay),
        compiler_params=params(12),
        name="sums",
    )(own_w, sib_w, keep, got, *relay)


def meet_kernel(chips, *refs):
    weight_refs, image_refs, outs = refs[:chips], refs[chips : 2 * chips], refs[2 * chips :]
    planes, met = outs[0].shape
    weights = []
    for ref in weight_refs:
        wide = ref.shape[-1]
        part = ref[:, wide - planes :] if len(ref.shape) == 2 else ref[0, :, wide - planes :]
        weights.append(part.astype(BF16))
    weights = jnp.concatenate(weights, axis=0)
    for other, out_ref in enumerate(outs):
        cut = slice(other * met, (other + 1) * met)
        images = jnp.concatenate([ref[:, cut].astype(BF16) for ref in image_refs], axis=0)
        out_ref[...] = lax.dot_general(
            weights, images, (((0,), (0,)), ((), ())), preferred_element_type=F32
        )


def meet(weights, images):
    met = images[0].shape[1] // 2
    planes = weights[0].shape[1]
    return pl.pallas_call(
        functools.partial(meet_kernel, len(weights)),
        out_shape=[jax.ShapeDtypeStruct((planes, met), F32)] * 2,
        compiler_params=params(16),
        name="meet",
    )(*weights, *images)


def shells_kernel(chips, ctf_ref, *refs):
    weight_refs, tail_refs, out_ref = refs[:chips], refs[chips:-1], refs[-1]
    planes = out_ref.shape[0]
    weights = []
    for ref in weight_refs:
        cut = slice(ref.shape[-1] - 2 * planes, ref.shape[-1] - planes)
        weights.append((ref[:, cut] if len(ref.shape) == 2 else ref[0, :, cut]).astype(BF16))
    ctf = [lanes_wide(ctf_ref[...])]
    ctf += [ref[...] if len(ref.shape) == 2 else ref[0] for ref in tail_refs]
    squares = jnp.concatenate([(part * part).astype(BF16) for part in ctf], axis=0)
    out_ref[...] = lax.dot_general(
        jnp.concatenate(weights, axis=0), squares, (((0,), (0,)), ((), ())), preferred_element_type=F32
    )


def shell_sums(ctf_table, weights, tails):
    rows = ctf_table.shape[0]
    planes = weights[0].shape[1] // 2

    def whole(array):
        return pl.BlockSpec(array.shape, lambda step: (0,) * len(array.shape))

    def last(array):
        place = array.shape[-1] // LANES - 1
        if len(array.shape) == 2:
            return pl.BlockSpec((rows, LANES), lambda step: (0, place))
        return pl.BlockSpec((1, rows, LANES), lambda step: (0, 0, place))

    return pl.pallas_call(
        functools.partial(shells_kernel, len(weights)),
        grid=(1,),
        in_specs=[whole(ctf_table)] + [whole(part) for part in weights] + [last(part) for part in tails],
        out_specs=pl.BlockSpec((planes, LANES), lambda step: (0, 0)),
        out_shape=jax.ShapeDtypeStruct((planes, LANES), F32),
        compiler_params=params(8),
        name="shells",
    )(ctf_table, *weights, *tails)


def prepare_kernel(places, index_hbm, met_ref, sib_met_ref, shell_ref, sib_shell_ref, *refs):
    total = sum(map(len, places))
    parts, (base_ref, scale_ref, index, in_sem) = refs[:total], refs[total:]
    planes, share = base_ref.shape
    wide, met = split_share(share)
    mine = pl.ds(pl.multiple_of(lax.axis_index("img") * share, share), share)
    fetch = pltpu.make_async_copy(index_hbm.at[:, mine], index, in_sem)
    fetch.start()
    start = 0
    for side, numbers in enumerate(places):
        refs = list(zip(parts[start : start + len(numbers)], numbers))
        start += len(numbers)
        base_ref[:, side * wide : (side + 1) * wide] = functools.reduce(
            jnp.add, [ref[place, :, :wide] for ref, place in refs]
        )
    half = lax.rem(lax.axis_index("slab"), 2)
    own = pl.ds(pl.multiple_of(2 * wide + half * met, LANES), met)
    other = pl.ds(pl.multiple_of(2 * wide + (1 - half) * met, LANES), met)
    base_ref[:, own] = met_ref[:planes, :met] + sib_met_ref[:planes, :met]
    base_ref[:, other] = jnp.zeros((planes, met), F32)
    shells = shell_ref[...] + sib_shell_ref[...]
    fetch.wait()
    for start in range(0, share, LANES):
        cut = slice(start, start + LANES)
        scale_ref[:, cut] = 1.0 / (spread(shells, index[:, cut]) + 1.0)


def prepare(index, met, sib_met, shells, sib_shells, sides, share):
    planes = met.shape[0] // 2
    held = pl.BlockSpec(memory_space=pl.ANY)
    vmem = pl.BlockSpec(memory_space=pltpu.VMEM)
    places = [[place for _, place in side] for side in sides]
    parts = [part for side in sides for part, _ in side]
    return pl.pallas_call(
        functools.partial(prepare_kernel, places),
        in_specs=[held] + [vmem] * (4 + len(parts)),
        out_specs=[vmem, vmem],
        out_shape=[jax.ShapeDtypeStruct((planes, share), F32)] * 2,
        scratch_shapes=[pltpu.VMEM((1, share), jnp.int32), pltpu.SemaphoreType.DMA(())],
        compiler_params=params(8),
        name="prepare",
    )(index, met, sib_met, shells, sib_shells, *parts)


def finish_kernel(base_ref, scale_ref, left_ref, right_ref, partner_ref, out_hbm, out, out_sem):
    planes, share = out.shape
    wide, met = split_share(share)
    half = lax.rem(lax.axis_index("slab"), 2)
    own = pl.multiple_of(2 * wide + half * met, LANES)
    other = pl.multiple_of(2 * wide + (1 - half) * met, LANES)

    def scaled(place, size, last=None):
        for start in range(0, size, LANES):
            at = pl.ds(pl.multiple_of(place + start, LANES), LANES)
            value = base_ref[:, at]
            if last is not None:
                value += last(slice(start, start + LANES))
            out[:, at] = value * scale_ref[:, at]

    stores = []

    def scale_and_store(place, size, last=None):
        for first in range(0, size, PIECE):
            piece = min(PIECE, size - first)
            from_here = None if last is None else lambda cut: last(slice(cut.start + first, cut.stop + first))
            scaled(place + first, piece, from_here)
            cut = pl.ds(pl.multiple_of(place + first, LANES), piece)
            stores.append(
                pltpu.make_async_copy(out.at[:, cut], out_hbm.at[:, cut], out_sem.at[len(stores)])
            )
            stores[-1].start()

    scale_and_store(own, met)
    scale_and_store(other, met, lambda cut: partner_ref[:, cut])
    scale_and_store(0, wide, lambda cut: left_ref[0, :, cut])
    scale_and_store(wide, wide, lambda cut: right_ref[0, :, cut])
    for copy in stores:
        copy.wait()


def finish(base, scale, left, right, partner):
    wide, met = split_share(base.shape[1])
    pieces = 2 * (pl.cdiv(wide, PIECE) + pl.cdiv(met, PIECE))
    vmem = pl.BlockSpec(memory_space=pltpu.VMEM)
    return pl.pallas_call(
        finish_kernel,
        in_specs=[vmem] * 5,
        out_specs=pl.BlockSpec(memory_space=pl.ANY),
        out_shape=jax.ShapeDtypeStruct(base.shape, F32),
        scratch_shapes=[pltpu.VMEM(base.shape, F32), pltpu.SemaphoreType.DMA((pieces,))],
        compiler_params=params(8),
        name="finish",
    )(base, scale, left, right, partner)


def swap(array, bit, size):
    return lax.ppermute(array, "img", [(one, one ^ bit) for one in range(size)])


def shards(images, references, orientations, ctf_table, inv_noise, class_weight):
    rows, width = images.shape
    classes, local_planes, _ = references.shape
    size = lax.axis_size("img")
    slabs = lax.axis_size("slab")
    chips = size // 2
    share = width // size
    wide, met_wide = split_share(share)
    index = entry_shells(width, ctf_table.shape[1])
    top_index = jnp.asarray(index[:, : width // 2 + 2 * math.isqrt(width // 2)])
    index = jnp.asarray(index)
    planes = references.reshape(classes * local_planes, width)

    beyond = tuple(k for k in range(chips) if k & (k - 1))
    near = tuple(k for k in range(chips) if k not in beyond)
    relayed = 1 | chips // 2
    met_images = {}
    if beyond:
        early = early_images(index, images, ctf_table, share, beyond, relayed)
        images, *early = lax.optimization_barrier((images, *early))
        met_images = {k: swap(part, 2 * k, size) for k, part in zip(beyond, early)}
    give, keep, table, *parts_near = estep(
        top_index, images, planes, ctf_table, share, near
    )
    if beyond:
        give, keep, met_images[beyond[-1]], *parts_near = lax.optimization_barrier(
            (give, keep, met_images[beyond[-1]], *parts_near)
        )
    for k, part in zip(near, parts_near):
        met_images[k] = swap(part, 2 * k, size) if k else part
    keep, *met_images = far(keep, *[met_images[k] for k in range(chips)])
    base, scale = count_planes(
        class_weight, inv_noise, orientations, slabs * local_planes, slabs
    )
    tables, bit = [table], 1
    while bit < slabs:
        held = tables[0]
        if len(tables) > 1:
            held = jnp.concatenate(tables, axis=1)
        pairs = [(one, one ^ bit) for one in range(slabs)]
        tables = [held, lax.ppermute(held, "slab", pairs)]
        bit *= 2
    got = swap(give, 1, size)
    own_w, both_w = weigh(base, scale, tables, classes * local_planes)
    sib_w = swap(own_w, 1, size)

    sums = functools.partial(
        partial_sums, own_w=own_w, sib_w=sib_w, keep=keep, got=got, wide=wide,
    )
    low = [1 << place for place in range(chips.bit_length() - 1)]
    orders = (low, low[::-1])
    first = [[k for k in range(chips) if k & order[0]] for order in orders]
    onward = [[k for k in ks if k & order[1]] for ks, order in zip(first, orders)]
    direct = [[k for k in ks if not k & order[1]] for ks, order in zip(first, orders)]
    stay = [[k for k in range(chips) if not k & order[0]] for order in orders]
    parts = [{k: [] for k in ks} for ks in stay]

    def deliver(side, ks, array, bit):
        arrived = swap(array, 2 * bit, size)
        for place, k in enumerate(ks):
            parts[side][k ^ bit].append((arrived, place))
        return arrived

    def compute(groups, relay=()):
        return sums(tuple(tuple(ks) for ks in groups), relay=relay)

    items = tuple((side, k) for side, ks in enumerate(onward) for k in ks)
    sent = first_sums(items, own_w, sib_w, both_w, gather_images(items, keep, got, wide))
    arrived = [swap(sent[side], 2 * orders[side][0], size) for side in (0, 1)]
    both_w, _ = lax.optimization_barrier((both_w, sent[1]))
    others = [k for k in range(1, chips) if k not in (orders[0][0], orders[1][0])]
    far_w = [swap(both_w, 2 * k, size) for k in others]
    sums.keywords["keep"], *met_images = lax.optimization_barrier((keep, *met_images))
    sent = compute(direct, (met_images[chips // 2],))
    relays = [deliver(side, direct[side], sent[side], orders[side][0]) for side in (0, 1)]
    kept = compute(stay)
    for side in (0, 1):
        for place, k in enumerate(stay[side]):
            parts[side][k].append((kept[side], place))

    met_images[0], _, *arrived = lax.optimization_barrier(
        (met_images[0], sent[0], *arrived, *far_w)
    )
    far_w = dict(zip(others, arrived[2:]))
    far_w[0] = both_w
    for side in (0, 1):
        bit = orders[side][0]
        far_w[bit] = arrived[side]
        for place, k in enumerate(onward[side]):
            parts[side][k ^ bit].append((arrived[side], place))
    weights = [far_w[k] for k in range(chips)]
    met, for_sib = meet(weights, met_images)
    tails = [relays[0] if k == relayed else met_images[k] for k in range(1, chips)]
    shells = shell_sums(ctf_table, weights, tails)
    sib_shells = swap(shells, 1, size)
    sib_met = swap(for_sib, 1, size)
    own_planes = classes * local_planes
    partner = lax.ppermute(
        met[own_planes:, :met_wide] + sib_met[own_planes:, :met_wide], "slab", [(one, one ^ 1) for one in range(slabs)]
    )

    for turn in range(1, len(low)):
        for side in (0, 1):
            bit = orders[side][turn]
            ks = [k for k in parts[side] if k & bit]
            sent = jnp.stack(
                [sum(part[place, :, :wide] for part, place in parts[side].pop(k)) for k in ks]
            )
            deliver(side, ks, sent, bit)
    base, scale = prepare(
        index, met, sib_met, shells, sib_shells, [parts[side][0][:-1] for side in (0, 1)], share
    )
    out = finish(base, scale, parts[0][0][-1][0], parts[1][0][-1][0], partner)
    return out.reshape(classes, local_planes, share)


def solution(mesh):
    return jax.shard_map(
        shards,
        mesh=mesh,
        in_specs=(
            P("img", None),
            P(None, "slab", None),
            P("img", None, None),
            P("img", None),
            P("img"),
            P(),
        ),
        out_specs=P(None, "slab", "img"),
        check_vma=False,
    )
```
